32 devices in a mesh: req: 16 (over z, y, x), tp: 2 (over core).
Axes of the slice: x: 2, y: 2, z: 4, core: 2. Of those that a mesh axis runs over, the one named last changes fastest.
Arguments:
- hidden_in: bfloat16 [256, 2048], P('req'), may hold values from -6 to 6
- query: bfloat16 [256, 2048], P('req', 'tp'), may hold values from -200 to 200
- new_kv: bfloat16 [256, 4096], P('req', 'tp'), may hold values from -6 to 6
- pool_cache: bfloat16 [1280, 32, 4096], P('req', None, 'tp'), may hold values from -7 to 7
- prompt_table: int32 [32, 24], P('req'), may hold values from 0 to 79, as said below
- prompt_len: int32 [32], P('req'), may hold values from 32 to 768
- req_group: int32 [256], P('req'), may hold values from 0 to 1, as said below
- cont_table: int32 [256, 2], P('req'), may hold values from 0 to 79, as said below
- cont_len: int32 [256], P('req'), may hold values from 1 to 63
- migration: int32 [96, 2], P('req'), may hold values from 0 to 15, as said below
- diff_lambda: float32 [8], P('tp'), may hold values from 0.2 to 0.8
- out_weight: bfloat16 [2048, 2048], P('tp'), may hold values from -0.125 to 0.125
- norm_gain: float32 [2048], replicated, may hold values from 0.1 to 1.9
Outputs:
- hidden_out: bfloat16 [256, 2048], P('req')
- normed_out: bfloat16 [256, 2048], P('req')
- arrived: bfloat16 [128, 64, 4096], P('req', None, 'tp')
The draws below stay inside these ranges and needn't reach their ends.
Inputs may be any that keep to these rules, and one draw needn't show every extreme that they name: `prompt_table`: entries are pages local to the row's index of req; with cont_table, each of a device's 80 pages appears exactly once. `cont_table`: local pages, each page of a device once together with prompt_table. `req_group`: A group index local to the device; every group of a device has a request. `migration`: each device lists 6 rows: a distinct local request slot and a destination offset 1 to 4 along req (with wrap); at most 2 rows of a device share an offset, and that many is reached.
All inputs are finite; a program needn't handle non-finite values.
Results may differ from the reference program's by a relative error of at most 0.012.
Values may be sent and summed in bfloat16 or wider, within the bound.
No kernel may reach another device: no remote copies, remote signals or barrier semaphores. Data moves between devices by JAX's collectives and lax.ppermute only.
A program may use at most 128 MiB of HBM per device.

```python
import jax
import jax.numpy as jnp
from jax import lax

D = 2048
HEADS = 8
HD = 128
VD = 256
REQ_DEV = 16
GROUP_DEV = 2
PAGE = 32
PROMPT_PAGES = 24
CONT_PAGES = 2
MIG_DEV = 6
MIG_REACH = 4
MIG_CAP = 2
POOL = 80
REQS = 256
GROUPS = 32
N_REQ = 16


def layout_tables(key):
    device_keys = jax.random.split(jax.random.fold_in(key, 11), N_REQ)
    page_perm = jax.vmap(lambda device_key: jax.random.permutation(device_key, POOL))(device_keys).astype(jnp.int32)
    prompt_table = page_perm[:, :GROUP_DEV * PROMPT_PAGES].reshape(GROUPS, PROMPT_PAGES)
    cont_table = page_perm[:, GROUP_DEV * PROMPT_PAGES:].reshape(REQS, CONT_PAGES)
    return (prompt_table, cont_table)


def draw_prompt_table(key, part):
    return layout_tables(key)[0]


def draw_cont_table(key, part):
    return layout_tables(key)[1]


def draw_prompt_len(key, part):
    lengths = jax.random.randint(jax.random.fold_in(key, 12), (GROUPS,), PAGE, PROMPT_PAGES * PAGE + 1, dtype=jnp.int32)
    longest = jax.random.randint(jax.random.fold_in(key, 13), (), 0, GROUPS, dtype=jnp.int32)
    return lengths.at[longest].set(PROMPT_PAGES * PAGE)


def draw_cont_len(key, part):
    lengths = jax.random.randint(jax.random.fold_in(key, 14), (REQS,), 1, CONT_PAGES * PAGE, dtype=jnp.int32)
    longest = jax.random.randint(jax.random.fold_in(key, 15), (), 0, REQS, dtype=jnp.int32)
    return lengths.at[longest].set(CONT_PAGES * PAGE - 1)


def draw_req_group(key, part):
    device_keys = jax.random.split(jax.random.fold_in(key, 16), N_REQ)

    def one_device(device_key):
        first_key, second_key = jax.random.split(device_key)
        labels = jnp.concatenate([jnp.arange(GROUP_DEV, dtype=jnp.int32), jax.random.randint(first_key, (REQ_DEV - GROUP_DEV,), 0, GROUP_DEV, dtype=jnp.int32)])
        return jax.random.permutation(second_key, labels)
    return jax.vmap(one_device)(device_keys).reshape(REQS)


def draw_migration(key, part):
    device_keys = jax.random.split(jax.random.fold_in(key, 17), N_REQ)

    def one_device(device_key):
        first_key, second_key = jax.random.split(device_key)
        slots = jax.random.permutation(first_key, REQ_DEV)[:MIG_DEV].astype(jnp.int32)
        offsets = (jax.random.permutation(second_key, MIG_REACH * MIG_CAP)[:MIG_DEV] // MIG_CAP + 1).astype(jnp.int32)
        return jnp.stack([slots, offsets], axis=-1)
    return jax.vmap(one_device)(device_keys).reshape(N_REQ * MIG_DEV, 2)


def anchor_keys(key):
    return jax.random.truncated_normal(jax.random.fold_in(key, 41), -6.0, 6.0, (N_REQ, HEADS * (2 * HD + VD)), jnp.float32)


def anchor_pages(key):
    prompt_table = layout_tables(key)[0]
    return prompt_table.reshape(N_REQ, GROUP_DEV, PROMPT_PAGES)[:, 0, 0] + jnp.arange(N_REQ, dtype=jnp.int32) * POOL


def draw_pool_cache(key, part):
    base = jax.random.truncated_normal(jax.random.fold_in(key, 21), -6.0, 6.0, (N_REQ * POOL, PAGE, HEADS * (2 * HD + VD)), jnp.float32)
    anchors = anchor_keys(key)
    where_page = anchor_pages(key)
    base = base.at[where_page, 0].set(anchors)
    return base.astype(jnp.bfloat16)


def draw_query(key, part):
    base = jax.random.truncated_normal(jax.random.fold_in(key, 31), -6.0, 6.0, (REQS, HEADS * 2 * HD), jnp.float32)
    return base.astype(jnp.bfloat16)


def block_levels(rng, shape, shards, least, top_value):
    def one(dim, shards_of):
        heights = jax.random.uniform(jax.random.fold_in(jax.random.fold_in(rng, 6), dim), (shards_of,), jnp.float32, least / len(shards), top_value / len(shards))
        return jnp.repeat(jnp.exp(heights), shape[dim] // shards_of).reshape((-1,) + (1,) * (len(shape) - dim - 1))

    gain = one(*shards[0])
    for cut in shards[1:]:
        gain = gain * one(*cut)
    return gain


def bell_draw(rng, dims, spread, most, pieces=(), held_as=jnp.bfloat16):
    array = jax.random.normal(rng, dims, jnp.float32) * spread
    if len(pieces) > 0:
        array = block_levels(rng, dims, pieces, -0.22, 0.18) * array
    return jnp.clip(array, min=-most, max=most).astype(held_as)


def setup_inputs(seed: int = 0) -> dict:
    arg_keys = jax.random.split(jax.random.key(seed), 14)
    return {
        "hidden_in": bell_draw(arg_keys[0], (REQS, D), 1.0, 6.0, ((0, 16),)),
        "query": draw_query(jax.random.fold_in(arg_keys[13], 71), 0),
        "new_kv": bell_draw(arg_keys[2], (REQS, HEADS * (2 * HD + VD)), 1.0, 6.0, ((0, 16), (1, 2))),
        "pool_cache": draw_pool_cache(jax.random.fold_in(arg_keys[13], 71), 0),
        "prompt_table": draw_prompt_table(jax.random.fold_in(arg_keys[13], 71), 0),
        "prompt_len": draw_prompt_len(jax.random.fold_in(arg_keys[13], 71), 0),
        "req_group": draw_req_group(jax.random.fold_in(arg_keys[13], 71), 0),
        "cont_table": draw_cont_table(jax.random.fold_in(arg_keys[13], 71), 0),
        "cont_len": draw_cont_len(jax.random.fold_in(arg_keys[13], 71), 0),
        "migration": draw_migration(jax.random.fold_in(arg_keys[13], 71), 0),
        "diff_lambda": jnp.clip(0.2 + 0.6 * jax.random.uniform(arg_keys[10], (HEADS,), jnp.float32) ** block_levels(arg_keys[10], (HEADS,), ((0, 2),), -0.2, 0.2), 0.2, 0.8),
        "out_weight": bell_draw(arg_keys[11], (HEADS * VD, D), (HEADS * VD) ** -0.5, 0.125, ((0, 2),)),
        "norm_gain": jnp.clip(1.0 + 0.18 * jax.random.normal(arg_keys[12], (D,), jnp.float32), 0.1, 1.9),
    }


def head_attention(queries, new_rows, page_pool, prompt_table, prompt_len, req_group, cont_table, cont_len, diff_lambda):
    row_count = queries.shape[0]
    head_count = diff_lambda.shape[0]
    head_width = page_pool.shape[-1] // head_count
    key_width = queries.shape[-1] // head_count // 2
    value_width = head_width - 2 * key_width
    page_len = page_pool.shape[1]
    group_count = prompt_table.shape[0]
    page_of = jnp.take_along_axis(cont_table, (cont_len // page_len)[:, None].astype(jnp.int32), axis=1)[:, 0]
    page_pool = page_pool.at[page_of, cont_len % page_len].set(new_rows)
    prompt_keys = page_pool[prompt_table].reshape(group_count, -1, head_count, head_width).astype(jnp.float32)
    cont_keys = page_pool[cont_table].reshape(row_count, -1, head_count, head_width).astype(jnp.float32)
    split_query = queries.reshape(row_count, head_count, 2, key_width).astype(jnp.float32)
    prompt_pos = jnp.arange(prompt_keys.shape[1], dtype=jnp.int32)
    cont_pos = jnp.arange(cont_keys.shape[1], dtype=jnp.int32)
    group_ids = jnp.arange(group_count, dtype=jnp.int32)
    prompt_mask = (req_group[:, None, None] == group_ids[None, :, None]) & (prompt_pos[None, None, :] < prompt_len[None, :, None])
    prompt_mask = prompt_mask[:, None]
    cont_mask = (cont_pos[None, :] <= cont_len[:, None])[:, None]
    score_scale = key_width ** (-0.5)
    prompt_values = prompt_keys[..., 2 * key_width:]
    cont_values = cont_keys[..., 2 * key_width:]
    outputs = []
    for twin_map in range(2):
        start_col = twin_map * key_width
        prompt_score = jnp.einsum('rhd,gjhd->rhgj', split_query[:, :, twin_map], prompt_keys[..., start_col:start_col + key_width]) * score_scale
        cont_score = jnp.einsum('rhd,rjhd->rhj', split_query[:, :, twin_map], cont_keys[..., start_col:start_col + key_width]) * score_scale
        prompt_score = jnp.where(prompt_mask, prompt_score, -1e+30)
        cont_score = jnp.where(cont_mask, cont_score, -1e+30)
        top_score = jnp.maximum(prompt_score.max(axis=(2, 3)), cont_score.max(axis=2))
        prompt_exp = jnp.exp(prompt_score - top_score[:, :, None, None])
        cont_exp = jnp.exp(cont_score - top_score[:, :, None])
        denominator = prompt_exp.sum(axis=(2, 3)) + cont_exp.sum(axis=2)
        prompt_weight = (prompt_exp / denominator[:, :, None, None]).astype(jnp.bfloat16).astype(jnp.float32)
        cont_weight = (cont_exp / denominator[:, :, None]).astype(jnp.bfloat16).astype(jnp.float32)
        mixture = jnp.einsum('rhgj,gjhe->rhe', prompt_weight, prompt_values) + jnp.einsum('rhj,rjhe->rhe', cont_weight, cont_values)
        outputs.append(mixture)
    difference = outputs[0] - diff_lambda[None, :, None] * outputs[1]
    normed = difference * lax.rsqrt(lax.optimization_barrier(jnp.mean(difference * difference, axis=-1, keepdims=True)) + 1e-05) * 0.8
    return (normed.astype(jnp.bfloat16).reshape(row_count, head_count * value_width), page_pool)

def send_buffer(page_pool, cont_table, cont_len, migration, reach, capacity):
    mig_slot = migration[:, 0]
    mig_off = migration[:, 1]
    entry_count = migration.shape[0]
    entry_order = jnp.arange(entry_count, dtype=jnp.int32)
    earlier = (mig_off[None, :] == mig_off[:, None]) & (entry_order[None, :] < entry_order[:, None])
    slot_place = (mig_off - 1) * capacity + lax.optimization_barrier(jnp.sum(earlier.astype(jnp.int32), axis=1)).astype(jnp.int32)
    page_rows = page_pool[cont_table[mig_slot]]
    page_rows = page_rows.reshape(entry_count, -1, page_pool.shape[-1])
    live_mask = jnp.arange(page_rows.shape[1], dtype=jnp.int32)[None, :] <= cont_len[mig_slot][:, None]
    page_rows = jnp.where(live_mask[:, :, None], page_rows, jnp.zeros_like(page_rows))
    buffer = jnp.zeros((reach * capacity,) + page_rows.shape[1:], page_rows.dtype).at[slot_place].set(page_rows)
    return buffer.reshape(reach, capacity, page_rows.shape[1], page_rows.shape[2])

def reference(hidden_in, query, new_kv, pool_cache, prompt_table, prompt_len, req_group, cont_table, cont_len, migration, diff_lambda, out_weight, norm_gain):

    def one_device(device_parts):
        query_dev, new_dev, pool_dev, prompt_dev, plen_dev, group_dev, cont_dev, clen_dev, mig_dev = device_parts
        attention, pool_new = head_attention(query_dev, new_dev, pool_dev, prompt_dev, plen_dev, group_dev, cont_dev, clen_dev, diff_lambda)
        return (attention, send_buffer(pool_new, cont_dev, clen_dev, mig_dev, MIG_REACH, MIG_CAP))
    stacked = (query.reshape(N_REQ, REQ_DEV, -1), new_kv.reshape(N_REQ, REQ_DEV, -1), pool_cache.reshape(N_REQ, POOL, PAGE, -1), prompt_table.reshape(N_REQ, GROUP_DEV, -1), prompt_len.reshape(N_REQ, GROUP_DEV), req_group.reshape(N_REQ, REQ_DEV), cont_table.reshape(N_REQ, REQ_DEV, -1), cont_len.reshape(N_REQ, REQ_DEV), migration.reshape(N_REQ, MIG_DEV, 2))
    attention, send_all = lax.map(one_device, stacked)
    attention = attention.reshape(REQS, -1)
    projected = jnp.dot(attention, out_weight, preferred_element_type=jnp.float32)
    summed = hidden_in.astype(jnp.float32) + projected
    normed = summed * lax.rsqrt(lax.optimization_barrier(jnp.mean(summed * summed, axis=-1, keepdims=True)) + 1e-05) * norm_gain
    arrived = jnp.stack([jnp.roll(send_all[:, offset - 1], offset, axis=0) for offset in range(1, MIG_REACH + 1)], axis=1)
    arrived = arrived.reshape(N_REQ * MIG_REACH * MIG_CAP, CONT_PAGES * PAGE, -1)
    return (summed.astype(jnp.bfloat16), normed.astype(jnp.bfloat16), arrived)
```

```python
import functools

import jax
import jax.numpy as jnp
from jax import lax
from jax.experimental import pallas as pl
from jax.experimental.pallas import tpu as pltpu
from jax.sharding import PartitionSpec as P

MIG_REACH = 4
MIG_CAP = 2
KEY = 128
ROWS = 16

SMEM = pl.BlockSpec(memory_space=pltpu.SMEM)
VMEM = pl.BlockSpec(memory_space=pltpu.VMEM)
ANY = pl.BlockSpec(memory_space=pl.ANY)
VMEM_BYTES = 40 * 1024 * 1024


def shifted(value, axis, steps):
    count = lax.axis_size(axis)
    pairs = [(source, (source + steps) % count) for source in range(count)]
    return lax.ppermute(value, axis, pairs)


def send_kernel(pieces, table, length, migration, new_ref, pool, *refs):
    outs = refs[: len(pieces)]
    holder, new_rows, sems = refs[len(pieces) :]
    entries = migration.shape[0]
    pages, page = table.shape[1], pool.shape[1]
    where = [(place, outs[n].at[i]) for n, piece in enumerate(pieces) for i, place in enumerate(piece)]
    for place, _ in where:
        holder[place] = -1
    for e in range(entries):
        rank = jnp.int32(0)
        for before in range(e):
            rank += (migration[before, 1] == migration[e, 1]).astype(jnp.int32)
        holder[(migration[e, 1] - 1) * MIG_CAP + rank] = migration[e, 0]

    def page_copy(place, out, j):
        slot = jnp.maximum(holder[place], 0)
        return pltpu.make_async_copy(pool.at[table[slot, j]], out.at[pl.ds(j * page, page)], sems.at[place, j])

    def used(place, j):
        slot = holder[place]
        return (slot >= 0) & (length[jnp.maximum(slot, 0)] >= j * page)

    for place, out in where:
        for j in range(pages):

            @pl.when(used(place, j))
            def _():
                page_copy(place, out, j).start()

    new_rows[...] = new_ref[...].astype(jnp.float32)
    for place, out in where:
        slot = holder[place]
        safe = jnp.maximum(slot, 0)
        last = jnp.where(slot >= 0, length[safe], -1)
        for j in range(pages):

            @pl.when(used(place, j))
            def _():
                page_copy(place, out, j).wait()

            for low in range(j * page, (j + 1) * page, ROWS):

                @pl.when(last < low)
                def _():
                    out[pl.ds(low, ROWS)] = jnp.zeros((ROWS, out.shape[1]), out.dtype)

                @pl.when((last >= low) & (last < low + ROWS))
                def _():
                    held = out[pl.ds(low, ROWS)].astype(jnp.float32)
                    pos = low + lax.broadcasted_iota(jnp.int32, held.shape, 0)
                    new = jnp.where(pos == last, new_rows[pl.ds(safe, 1)], 0.0)
                    out[pl.ds(low, ROWS)] = jnp.where(pos < last, held, new).astype(out.dtype)


def send_slots(pieces, cont_table, cont_len, migration, new_kv, pool):
    span = cont_table.shape[1] * pool.shape[1]
    width = pool.shape[2]
    return pl.pallas_call(
        functools.partial(send_kernel, pieces),
        out_shape=[jax.ShapeDtypeStruct((len(piece), span, width), pool.dtype) for piece in pieces],
        in_specs=[SMEM, SMEM, SMEM, VMEM, ANY],
        out_specs=[VMEM] * len(pieces),
        scratch_shapes=[
            pltpu.SMEM((MIG_REACH * MIG_CAP,), jnp.int32),
            pltpu.VMEM(new_kv.shape, jnp.float32),
            pltpu.SemaphoreType.DMA((MIG_REACH * MIG_CAP, cont_table.shape[1])),
        ],
        compiler_params=pltpu.CompilerParams(vmem_limit_bytes=VMEM_BYTES),
        name="send_slots",
    )(cont_table, cont_len, migration, new_kv, pool)


def column(values, count):
    rows = lax.broadcasted_iota(jnp.int32, (count, 1), 0)
    out = jnp.zeros((count, 1), jnp.int32)
    for r in range(count):
        out = jnp.where(rows == r, values[r], out)
    return out


def attention_kernel(
    prompt_table, prompt_len, req_group, cont_table, cont_len, lam, query, new_ref, weight, pool, out, held, weight_held, sems
):
    groups, prompt_pages = prompt_table.shape
    reqs, cont_pages = cont_table.shape
    heads = lam.shape[0]
    page = pool.shape[1]
    span = prompt_pages * page
    own = cont_pages * page
    start = groups * span
    head_width = pool.shape[2] // heads
    value_width = head_width - 2 * KEY

    for g in range(groups):

        @pl.loop(0, prompt_pages)
        def _(j):
            at = pl.multiple_of(g * span + j * page, page)
            pltpu.make_async_copy(pool.at[prompt_table[g, j]], held.at[pl.ds(at, page)], sems.at[0]).start()

    @pl.loop(0, reqs)
    def _(r):
        for j in range(cont_pages):
            at = pl.multiple_of(start + r * own + j * page, page)
            pltpu.make_async_copy(pool.at[cont_table[r, j]], held.at[pl.ds(at, page)], sems.at[0]).start()

    weight_copy = pltpu.make_async_copy(weight, weight_held, sems.at[1])
    weight_copy.start()

    group_of = column(req_group, reqs)
    length_of = column(cont_len, reqs)
    biases = []
    pos = lax.broadcasted_iota(jnp.int32, (reqs, span), 1)
    for g in range(groups):
        live = (group_of == g) & (pos < prompt_len[g])
        biases.append(jnp.where(live, 0.0, -1e30))
    key = lax.broadcasted_iota(jnp.int32, (reqs, reqs * own), 1)
    pos = key - own * lax.broadcasted_iota(jnp.int32, (reqs, reqs * own), 0)
    biases.append(jnp.where((pos >= 0) & (pos < length_of), 0.0, -1e30))
    live = jnp.concatenate(biases, axis=1) == 0.0

    pltpu.make_async_copy(held, held, sems.at[0]).wait()

    scale = KEY**-0.5
    mixed = []
    for h in range(heads):
        first = h * head_width
        weights, new_weights = [], []
        for i in range(2):
            q = query[:, pl.ds((2 * h + i) * KEY, KEY)]
            cols = pl.ds(first + i * KEY, KEY)
            score = lax.dot_general(
                q, held[:, cols], (((1,), (1,)), ((), ())), preferred_element_type=jnp.float32
            )
            score = jnp.where(live, score * scale, -1e30)
            new = jnp.sum(q.astype(jnp.float32) * new_ref[:, cols].astype(jnp.float32), axis=1, keepdims=True) * scale
            top = jnp.maximum(jnp.max(score, axis=1, keepdims=True), new)
            score = jnp.exp(score - top)
            new = jnp.exp(new - top)
            inverse = 1.0 / (jnp.sum(score, axis=1, keepdims=True) + new)
            weights.append((score * inverse).astype(jnp.bfloat16))
            new_weights.append((new * inverse).astype(jnp.bfloat16).astype(jnp.float32))
        cols = pl.ds(first + 2 * KEY, value_width)
        mixture = jnp.dot(jnp.concatenate(weights, axis=0), held[:, cols], preferred_element_type=jnp.float32)
        new_value = new_ref[:, cols].astype(jnp.float32)
        one = mixture[:reqs] + new_weights[0] * new_value
        two = mixture[reqs:] + new_weights[1] * new_value
        diff = one - lam[h] * two
        norm = lax.rsqrt(jnp.mean(diff * diff, axis=1, keepdims=True) + 1e-05)
        mixed.append((diff * norm * 0.8).astype(jnp.bfloat16))
    weight_copy.wait()
    mixed = jnp.concatenate(mixed, axis=1)
    out[...] = jnp.dot(mixed, weight_held[...], preferred_element_type=jnp.float32).astype(out.dtype)


def attention(query, new_kv, pool, prompt_table, prompt_len, req_group, cont_table, cont_len, lam, weight):
    reqs = query.shape[0]
    page, width = pool.shape[1:]
    keys = (prompt_table.size + cont_table.size) * page
    return pl.pallas_call(
        attention_kernel,
        out_shape=jax.ShapeDtypeStruct((reqs, weight.shape[1]), jnp.bfloat16),
        in_specs=[SMEM] * 6 + [VMEM, VMEM, ANY, ANY],
        out_specs=VMEM,
        scratch_shapes=[
            pltpu.VMEM((keys, width), pool.dtype),
            pltpu.VMEM(weight.shape, weight.dtype),
            pltpu.SemaphoreType.DMA((2,)),
        ],
        compiler_params=pltpu.CompilerParams(vmem_limit_bytes=VMEM_BYTES),
        cost_estimate=pl.CostEstimate(
            flops=4 * reqs * keys * width + 2 * reqs * weight.size,
            bytes_accessed=2 * (keys * width + weight.size),
            transcendentals=reqs * keys * 2 * lam.shape[0],
        ),
        name="attention",
    )(prompt_table, prompt_len, req_group, cont_table, cont_len, lam, query, new_kv, weight, pool)


def finish_kernel(count, hidden, gain, *refs):
    parts = refs[:count]
    hidden_out, normed_out = refs[count:]
    total = parts[0][...].astype(jnp.float32)
    for part in parts[1:]:
        total = total + part[...].astype(jnp.float32)
    summed = hidden[...].astype(jnp.float32) + total
    norm = lax.rsqrt(jnp.mean(summed * summed, axis=1, keepdims=True) + 1e-05)
    hidden_out[...] = summed.astype(hidden_out.dtype)
    normed_out[...] = (summed * norm * gain[...]).astype(normed_out.dtype)


def finish(hidden, gain, parts):
    shape = jax.ShapeDtypeStruct(hidden.shape, jnp.bfloat16)
    return pl.pallas_call(
        functools.partial(finish_kernel, len(parts)),
        out_shape=[shape, shape],
        in_specs=[VMEM] * (2 + len(parts)),
        out_specs=[VMEM, VMEM],
        name="finish",
    )(hidden, gain.reshape(1, -1), *parts)


def gather_kernel(where, *refs):
    parts, out, sems = refs[: len(where)], refs[-2], refs[-1]
    copies = [
        pltpu.make_async_copy(part, out.at[pl.ds(place, part.shape[0])], sems.at[n])
        for n, (part, place) in enumerate(zip(parts, where))
    ]
    for copy in copies:
        copy.start()
    for copy in copies:
        copy.wait()


def arrive(parts, where):
    slots = sum(part.shape[0] for part in parts)
    return pl.pallas_call(
        functools.partial(gather_kernel, where),
        out_shape=jax.ShapeDtypeStruct((slots,) + parts[0].shape[1:], parts[0].dtype),
        in_specs=[ANY] * len(parts),
        out_specs=ANY,
        scratch_shapes=[pltpu.SemaphoreType.DMA((len(parts),))],
        name="arrive",
    )(*parts)


def shards(
    hidden_in,
    query,
    new_kv,
    pool_cache,
    prompt_table,
    prompt_len,
    req_group,
    cont_table,
    cont_len,
    migration,
    diff_lambda,
    out_weight,
    norm_gain,
):
    pieces = tuple(tuple(range(o * MIG_CAP, (o + 1) * MIG_CAP)) for o in range(MIG_REACH))
    outgoing = send_slots(pieces, cont_table, cont_len, migration, new_kv, pool_cache)
    received = [shifted(part, "req", offset + 1) for offset, part in enumerate(outgoing)]
    partial = attention(
        query, new_kv, pool_cache, prompt_table, prompt_len, req_group, cont_table, cont_len, diff_lambda, out_weight
    )
    if lax.axis_size("tp") == 2:
        parts = [partial, shifted(partial, "tp", 1)]
    else:
        parts = [lax.psum(partial, "tp")]
    hidden_out, normed_out = finish(hidden_in, norm_gain, parts)
    arrived = arrive(received, [o * MIG_CAP for o in range(MIG_REACH)])
    return (hidden_out, normed_out, arrived)


def solution(mesh):
    placed = (
        P("req", None),
        P("req", "tp"),
        P("req", "tp"),
        P("req", None, "tp"),
        P("req", None),
        P("req"),
        P("req"),
        P("req", None),
        P("req"),
        P("req", None),
        P("tp"),
        P("tp", None),
        P(),
    )
    return jax.shard_map(
        shards,
        mesh=mesh,
        in_specs=placed,
        out_specs=(P("req", None), P("req", None), P("req", None, "tp")),
        check_vma=False,
    )
```

```python
import functools

import jax
import jax.numpy as jnp
from jax import lax
from jax.experimental import pallas as pl
from jax.experimental.pallas import tpu as pltpu
from jax.sharding import PartitionSpec as P

MIG_REACH = 4
MIG_CAP = 2
KEY = 128
ROWS = 16

SMEM = pl.BlockSpec(memory_space=pltpu.SMEM)
VMEM = pl.BlockSpec(memory_space=pltpu.VMEM)
HBM = pl.BlockSpec(memory_space=pltpu.HBM)
VMEM_BYTES = 40 * 1024 * 1024


def pinned(*arrays):
    return [pltpu.with_memory_space_constraint(array, pltpu.HBM) for array in arrays]


def shifted(value, axis, steps):
    count = lax.axis_size(axis)
    pairs = [(source, (source + steps) % count) for source in range(count)]
    return lax.ppermute(value, axis, pairs)


def send_kernel(pieces, table_in, length_in, migration_in, new_in, pool, *refs):
    outs = refs[: len(pieces)]
    table, length, migration, holder, new_held, new_rows, sems, small_sems = refs[len(pieces) :]
    small = [
        pltpu.make_async_copy(source, target, small_sems.at[n])
        for n, (source, target) in enumerate(
            zip((table_in, length_in, migration_in, new_in), (table, length, migration, new_held))
        )
    ]
    for copy in small:
        copy.start()
    for copy in small[:3]:
        copy.wait()
    entries = migration.shape[1]
    pages, page = table.shape[0], pool.shape[1]
    where = [(place, outs[n].at[i]) for n, piece in enumerate(pieces) for i, place in enumerate(piece)]
    for place, _ in where:
        holder[place] = -1
    for e in range(entries):
        rank = jnp.int32(0)
        for before in range(e):
            rank += (migration[1, before] == migration[1, e]).astype(jnp.int32)
        holder[(migration[1, e] - 1) * MIG_CAP + rank] = migration[0, e]

    def page_copy(place, out, j):
        slot = jnp.maximum(holder[place], 0)
        return pltpu.make_async_copy(pool.at[table[j, slot]], out.at[pl.ds(j * page, page)], sems.at[place, j])

    def used(place, j):
        slot = holder[place]
        return (slot >= 0) & (length[jnp.maximum(slot, 0)] >= j * page)

    for place, out in where:
        for j in range(pages):

            @pl.when(used(place, j))
            def _():
                page_copy(place, out, j).start()

    small[3].wait()
    new_rows[...] = new_held[...].astype(jnp.float32)
    for place, out in where:
        slot = holder[place]
        safe = jnp.maximum(slot, 0)
        last = jnp.where(slot >= 0, length[safe], -1)
        for j in range(pages):

            @pl.when(used(place, j))
            def _():
                page_copy(place, out, j).wait()

            for low in range(j * page, (j + 1) * page, ROWS):

                @pl.when(last < low)
                def _():
                    out[pl.ds(low, ROWS)] = jnp.zeros((ROWS, out.shape[1]), out.dtype)

                @pl.when((last >= low) & (last < low + ROWS))
                def _():
                    held = out[pl.ds(low, ROWS)].astype(jnp.float32)
                    pos = low + lax.broadcasted_iota(jnp.int32, held.shape, 0)
                    new = jnp.where(pos == last, new_rows[pl.ds(safe, 1)], 0.0)
                    out[pl.ds(low, ROWS)] = jnp.where(pos < last, held, new).astype(out.dtype)


def send_slots(pieces, cont_table, cont_len, migration, new_kv, pool):
    span = cont_table.shape[0] * pool.shape[1]
    width = pool.shape[2]
    return pl.pallas_call(
        functools.partial(send_kernel, pieces),
        out_shape=[jax.ShapeDtypeStruct((len(piece), span, width), pool.dtype) for piece in pieces],
        in_specs=[HBM] * 5,
        out_specs=[VMEM] * len(pieces),
        scratch_shapes=[
            pltpu.SMEM(cont_table.shape, jnp.int32),
            pltpu.SMEM(cont_len.shape, jnp.int32),
            pltpu.SMEM(migration.shape, jnp.int32),
            pltpu.SMEM((MIG_REACH * MIG_CAP,), jnp.int32),
            pltpu.VMEM(new_kv.shape, new_kv.dtype),
            pltpu.VMEM(new_kv.shape, jnp.float32),
            pltpu.SemaphoreType.DMA((MIG_REACH * MIG_CAP, cont_table.shape[0])),
            pltpu.SemaphoreType.DMA((4,)),
        ],
        compiler_params=pltpu.CompilerParams(vmem_limit_bytes=VMEM_BYTES),
        name="send_slots",
    )(*pinned(cont_table, cont_len, migration, new_kv, pool))


def column(values, count):
    rows = lax.broadcasted_iota(jnp.int32, (count, 1), 0)
    out = jnp.zeros((count, 1), jnp.int32)
    for r in range(count):
        out = jnp.where(rows == r, values[r], out)
    return out


def attention_kernel(
    prompt_table, prompt_len, req_group, cont_table, cont_len, lam, query, new_ref, weight, pool, out, held, weight_held, sems
):
    groups, prompt_pages = prompt_table.shape
    cont_pages, reqs = cont_table.shape
    heads = lam.shape[0]
    page = pool.shape[1]
    span = prompt_pages * page
    own = cont_pages * page
    start = groups * span
    head_width = pool.shape[2] // heads
    value_width = head_width - 2 * KEY

    for g in range(groups):

        @pl.loop(0, prompt_pages)
        def _(j):
            at = pl.multiple_of(g * span + j * page, page)
            pltpu.make_async_copy(pool.at[prompt_table[g, j]], held.at[pl.ds(at, page)], sems.at[0]).start()

    @pl.loop(0, reqs)
    def _(r):
        for j in range(cont_pages):
            at = pl.multiple_of(start + r * own + j * page, page)
            pltpu.make_async_copy(pool.at[cont_table[j, r]], held.at[pl.ds(at, page)], sems.at[0]).start()

    weight_copy = pltpu.make_async_copy(weight, weight_held, sems.at[1])
    weight_copy.start()

    group_of = column(req_group, reqs)
    length_of = column(cont_len, reqs)
    biases = []
    pos = lax.broadcasted_iota(jnp.int32, (reqs, span), 1)
    for g in range(groups):
        live = (group_of == g) & (pos < prompt_len[g])
        biases.append(jnp.where(live, 0.0, -1e30))
    key = lax.broadcasted_iota(jnp.int32, (reqs, reqs * own), 1)
    pos = key - own * lax.broadcasted_iota(jnp.int32, (reqs, reqs * own), 0)
    biases.append(jnp.where((pos >= 0) & (pos < length_of), 0.0, -1e30))
    live = jnp.concatenate(biases, axis=1) == 0.0

    pltpu.make_async_copy(held, held, sems.at[0]).wait()

    scale = KEY**-0.5
    mixed = []
    for h in range(heads):
        first = h * head_width
        weights, new_weights = [], []
        for i in range(2):
            q = query[:, pl.ds((2 * h + i) * KEY, KEY)]
            cols = pl.ds(first + i * KEY, KEY)
            score = lax.dot_general(
                q, held[:, cols], (((1,), (1,)), ((), ())), preferred_element_type=jnp.float32
            )
            score = jnp.where(live, score * scale, -1e30)
            new = jnp.sum(q.astype(jnp.float32) * new_ref[:, cols].astype(jnp.float32), axis=1, keepdims=True) * scale
            top = jnp.maximum(jnp.max(score, axis=1, keepdims=True), new)
            score = jnp.exp(score - top)
            new = jnp.exp(new - top)
            inverse = 1.0 / (jnp.sum(score, axis=1, keepdims=True) + new)
            weights.append((score * inverse).astype(jnp.bfloat16))
            new_weights.append((new * inverse).astype(jnp.bfloat16).astype(jnp.float32))
        cols = pl.ds(first + 2 * KEY, value_width)
        mixture = jnp.dot(jnp.concatenate(weights, axis=0), held[:, cols], preferred_element_type=jnp.float32)
        new_value = new_ref[:, cols].astype(jnp.float32)
        one = mixture[:reqs] + new_weights[0] * new_value
        two = mixture[reqs:] + new_weights[1] * new_value
        diff = one - lam[h] * two
        norm = lax.rsqrt(jnp.mean(diff * diff, axis=1, keepdims=True) + 1e-05)
        mixed.append((diff * norm * 0.8).astype(jnp.bfloat16))
    weight_copy.wait()
    mixed = jnp.concatenate(mixed, axis=1)
    out[...] = jnp.dot(mixed, weight_held[...], preferred_element_type=jnp.float32).astype(out.dtype)


def attention(query, new_kv, pool, prompt_table, prompt_len, req_group, cont_table, cont_len, lam, weight):
    reqs = query.shape[0]
    page, width = pool.shape[1:]
    keys = (prompt_table.size + cont_table.size) * page
    return pl.pallas_call(
        attention_kernel,
        out_shape=jax.ShapeDtypeStruct((reqs, weight.shape[1]), jnp.bfloat16),
        in_specs=[SMEM] * 6 + [VMEM, VMEM, HBM, HBM],
        out_specs=VMEM,
        scratch_shapes=[
            pltpu.VMEM((keys, width), pool.dtype),
            pltpu.VMEM(weight.shape, weight.dtype),
            pltpu.SemaphoreType.DMA((2,)),
        ],
        compiler_params=pltpu.CompilerParams(vmem_limit_bytes=VMEM_BYTES),
        cost_estimate=pl.CostEstimate(
            flops=4 * reqs * keys * width + 2 * reqs * weight.size,
            bytes_accessed=2 * (keys * width + weight.size),
            transcendentals=reqs * keys * 2 * lam.shape[0],
        ),
        name="attention",
    )(prompt_table, prompt_len, req_group, cont_table, cont_len, lam, query, new_kv, *pinned(weight, pool))


def finish_kernel(count, hidden, gain, *refs):
    parts = refs[:count]
    hidden_out, normed_out = refs[count:]
    total = parts[0][...].astype(jnp.float32)
    for part in parts[1:]:
        total = total + part[...].astype(jnp.float32)
    summed = hidden[...].astype(jnp.float32) + total
    norm = lax.rsqrt(jnp.mean(summed * summed, axis=1, keepdims=True) + 1e-05)
    hidden_out[...] = summed.astype(hidden_out.dtype)
    normed_out[...] = (summed * norm * gain[...]).astype(normed_out.dtype)


def finish(hidden, gain, parts):
    shape = jax.ShapeDtypeStruct(hidden.shape, jnp.bfloat16)
    return pl.pallas_call(
        functools.partial(finish_kernel, len(parts)),
        out_shape=[shape, shape],
        in_specs=[VMEM] * (2 + len(parts)),
        out_specs=[VMEM, VMEM],
        name="finish",
    )(hidden, gain.reshape(1, -1), *parts)


def gather_kernel(where, *refs):
    count = len(refs) - 2
    parts, out, sems = refs[:count], refs[-2], refs[-1]
    col = lax.rem(lax.axis_index("req"), MIG_REACH)
    parts = iter(parts)
    copies = []
    for n, (place, cols) in enumerate(where):
        part = next(parts)
        target = out.at[pl.ds(place, part.shape[0])]
        copy = pltpu.make_async_copy(part, target, sems.at[n])
        if cols:
            second = pltpu.make_async_copy(next(parts), target, sems.at[n])
            relayed = functools.reduce(jnp.logical_or, [col == c for c in cols])
            pl.when(relayed)(second.start)
            pl.when(jnp.logical_not(relayed))(copy.start)
        else:
            copy.start()
        copies.append(copy)
    for copy in copies:
        copy.wait()


def arrive(parts, where):
    slots = MIG_REACH * MIG_CAP
    return pl.pallas_call(
        functools.partial(gather_kernel, where),
        out_shape=jax.ShapeDtypeStruct((slots,) + parts[0].shape[1:], parts[0].dtype),
        in_specs=[VMEM] * len(parts),
        out_specs=HBM,
        scratch_shapes=[pltpu.SemaphoreType.DMA((len(where),))],
        name="arrive",
    )(*parts)


def turned(value, axis, steps):
    count = lax.axis_size(axis)
    pairs = [(s, s - s % MIG_REACH + (s + steps) % MIG_REACH) for s in range(count)]
    return lax.ppermute(value, axis, pairs)


def lifted(value, axis, cols):
    count = lax.axis_size(axis)
    pairs = [(s, (s + MIG_REACH) % count) for s in range(count) if s % MIG_REACH in cols]
    return lax.ppermute(value, axis, pairs)


def migrate(cont_table, cont_len, migration, new_kv, pool):
    count = lax.axis_size("req")
    if count % MIG_REACH or count == MIG_REACH:
        pieces = tuple(tuple(range(o * MIG_CAP, (o + 1) * MIG_CAP)) for o in range(MIG_REACH))
        outgoing = send_slots(pieces, cont_table, cont_len, migration, new_kv, pool)
        received = [shifted(part, "req", o + 1) for o, part in enumerate(outgoing)]
        return received, [(piece[0], ()) for piece in pieces]
    pieces = ((0, 1), (6, 7), (3,), (4, 5), (2,))
    one, four, two, three, two_straight = send_slots(pieces, cont_table, cont_len, migration, new_kv, pool)
    one = turned(one, "req", 1)
    four = shifted(four, "req", 4)
    two = turned(two, "req", 2)
    three = shifted(three, "req", 3)
    two_straight = shifted(two_straight, "req", 2)
    one_up = lifted(one, "req", (0,))
    two_up = lifted(two, "req", (0, 1))
    received = [one, one_up, four, two, two_up, three, two_straight]
    return received, [(0, (0,)), (6, ()), (3, (0, 1)), (4, ()), (2, ())]


def shards(
    hidden_in,
    query,
    new_kv,
    pool_cache,
    prompt_table,
    prompt_len,
    req_group,
    cont_table,
    cont_len,
    migration,
    diff_lambda,
    out_weight,
    norm_gain,
):
    cont_table, migration = cont_table.T, migration.T
    received, where = migrate(cont_table, cont_len, migration, new_kv, pool_cache)
    partial = attention(
        query, new_kv, pool_cache, prompt_table, prompt_len, req_group, cont_table, cont_len, diff_lambda, out_weight
    )
    if lax.axis_size("tp") == 2:
        parts = [partial, shifted(partial, "tp", 1)]
    else:
        parts = [lax.psum(partial, "tp")]
    hidden_out, normed_out = finish(hidden_in, norm_gain, parts)
    arrived = arrive(received, where)
    return (hidden_out, normed_out, arrived)


def solution(mesh):
    placed = (
        P("req", None),
        P("req", "tp"),
        P("req", "tp"),
        P("req", None, "tp"),
        P("req", None),
        P("req"),
        P("req"),
        P("req", None),
        P("req"),
        P("req", None),
        P("tp"),
        P("tp", None),
        P(),
    )
    return jax.shard_map(
        shards,
        mesh=mesh,
        in_specs=placed,
        out_specs=(P("req", None), P("req", None), P("req", None, "tp")),
        check_vma=False,
    )
```

```python
import functools

import jax
import jax.numpy as jnp
from jax import lax
from jax.experimental import pallas as pl
from jax.experimental.pallas import tpu as pltpu
from jax.sharding import PartitionSpec as P

MIG_REACH = 4
MIG_CAP = 2
KEY = 128
ROWS = 16

SMEM = pl.BlockSpec(memory_space=pltpu.SMEM)
VMEM = pl.BlockSpec(memory_space=pltpu.VMEM)
HBM = pl.BlockSpec(memory_space=pltpu.HBM)
VMEM_BYTES = 40 * 1024 * 1024
SMALL_VMEM_BYTES = 8 * 1024 * 1024


def pinned(*arrays):
    return [pltpu.with_memory_space_constraint(array, pltpu.HBM) for array in arrays]


def shifted(value, axis, steps):
    count = lax.axis_size(axis)
    pairs = [(source, (source + steps) % count) for source in range(count)]
    return lax.ppermute(value, axis, pairs)


def send_kernel(offsets, table_in, length_in, migration_in, new_in, pool, *refs):
    outs = refs[: len(offsets)]
    table, length, migration, holder, new_held, new_rows, sems, small_sems = refs[len(offsets) :]
    small = [
        pltpu.make_async_copy(source, target, small_sems.at[n])
        for n, (source, target) in enumerate(
            zip((table_in, length_in, migration_in, new_in), (table, length, migration, new_held))
        )
    ]
    for copy in small:
        copy.start()
    for copy in small[:3]:
        copy.wait()
    entries = migration.shape[1]
    pages, page = table.shape[0], pool.shape[1]
    for place in range(MIG_REACH * MIG_CAP):
        holder[place] = -1
    odd = lax.rem(lax.axis_index("tp"), 2)
    where = []
    for n, (on_even, on_odd) in enumerate(offsets):
        offset = on_even + odd * (on_odd - on_even)
        for i in range(MIG_CAP):
            where.append((n * MIG_CAP + i, (offset - 1) * MIG_CAP + i, outs[n].at[i]))
    for e in range(entries):
        rank = jnp.int32(0)
        for before in range(e):
            rank += (migration[1, before] == migration[1, e]).astype(jnp.int32)
        holder[(migration[1, e] - 1) * MIG_CAP + rank] = migration[0, e]

    def page_copy(n, place, out, j):
        slot = jnp.maximum(holder[place], 0)
        return pltpu.make_async_copy(pool.at[table[j, slot]], out.at[pl.ds(j * page, page)], sems.at[n, j])

    def used(place, j):
        slot = holder[place]
        return (slot >= 0) & (length[jnp.maximum(slot, 0)] >= j * page)

    for n, place, out in where:
        for j in range(pages):

            @pl.when(used(place, j))
            def _():
                page_copy(n, place, out, j).start()

    small[3].wait()
    new_rows[...] = new_held[...].astype(jnp.float32)
    for n, place, out in where:
        slot = holder[place]
        safe = jnp.maximum(slot, 0)
        last = jnp.where(slot >= 0, length[safe], -1)
        for j in range(pages):

            @pl.when(used(place, j))
            def _():
                page_copy(n, place, out, j).wait()

            for low in range(j * page, (j + 1) * page, ROWS):

                @pl.when(last < low)
                def _():
                    out[pl.ds(low, ROWS)] = jnp.zeros((ROWS, out.shape[1]), out.dtype)

                @pl.when((last >= low) & (last < low + ROWS))
                def _():
                    held = out[pl.ds(low, ROWS)].astype(jnp.float32)
                    pos = low + lax.broadcasted_iota(jnp.int32, held.shape, 0)
                    new = jnp.where(pos == last, new_rows[pl.ds(safe, 1)], 0.0)
                    out[pl.ds(low, ROWS)] = jnp.where(pos < last, held, new).astype(out.dtype)


def send_slots(cont_table, cont_len, migration, new_kv, pool, offsets):
    span = cont_table.shape[0] * pool.shape[1]
    width = pool.shape[2]
    return pl.pallas_call(
        functools.partial(send_kernel, offsets),
        out_shape=[jax.ShapeDtypeStruct((MIG_CAP, span, width), pool.dtype)] * len(offsets),
        in_specs=[HBM] * 5,
        out_specs=[VMEM] * len(offsets),
        scratch_shapes=[
            pltpu.SMEM(cont_table.shape, jnp.int32),
            pltpu.SMEM(cont_len.shape, jnp.int32),
            pltpu.SMEM(migration.shape, jnp.int32),
            pltpu.SMEM((MIG_REACH * MIG_CAP,), jnp.int32),
            pltpu.VMEM(new_kv.shape, new_kv.dtype),
            pltpu.VMEM(new_kv.shape, jnp.float32),
            pltpu.SemaphoreType.DMA((MIG_REACH * MIG_CAP, cont_table.shape[0])),
            pltpu.SemaphoreType.DMA((4,)),
        ],
        compiler_params=pltpu.CompilerParams(vmem_limit_bytes=VMEM_BYTES),
        name="send_slots",
    )(*pinned(cont_table, cont_len, migration, new_kv, pool))


def column(values, count):
    rows = lax.broadcasted_iota(jnp.int32, (count, 1), 0)
    out = jnp.zeros((count, 1), jnp.int32)
    for r in range(count):
        out = jnp.where(rows == r, values[r], out)
    return out


def attention_kernel(
    prompt_table, prompt_len, req_group, cont_table, cont_len, lam, query, new_ref, weight, pool, out, held, weight_held, sems
):
    groups, prompt_pages = prompt_table.shape
    cont_pages, reqs = cont_table.shape
    heads = lam.shape[0]
    page = pool.shape[1]
    span = prompt_pages * page
    own = cont_pages * page
    start = groups * span
    head_width = pool.shape[2] // heads
    value_width = head_width - 2 * KEY

    for g in range(groups):

        @pl.loop(0, prompt_pages)
        def _(j):
            at = pl.multiple_of(g * span + j * page, page)
            pltpu.make_async_copy(pool.at[prompt_table[g, j]], held.at[pl.ds(at, page)], sems.at[0]).start()

    @pl.loop(0, reqs)
    def _(r):
        for j in range(cont_pages):
            at = pl.multiple_of(start + r * own + j * page, page)
            pltpu.make_async_copy(pool.at[cont_table[j, r]], held.at[pl.ds(at, page)], sems.at[0]).start()

    weight_copy = pltpu.make_async_copy(weight, weight_held, sems.at[1])
    weight_copy.start()

    group_of = column(req_group, reqs)
    length_of = column(cont_len, reqs)
    biases = []
    pos = lax.broadcasted_iota(jnp.int32, (reqs, span), 1)
    for g in range(groups):
        live = (group_of == g) & (pos < prompt_len[g])
        biases.append(jnp.where(live, 0.0, -1e30))
    key = lax.broadcasted_iota(jnp.int32, (reqs, reqs * own), 1)
    pos = key - own * lax.broadcasted_iota(jnp.int32, (reqs, reqs * own), 0)
    biases.append(jnp.where((pos >= 0) & (pos < length_of), 0.0, -1e30))
    live = jnp.concatenate(biases, axis=1) == 0.0

    pltpu.make_async_copy(held, held, sems.at[0]).wait()

    scale = KEY**-0.5
    mixed = []
    for h in range(heads):
        first = h * head_width
        weights, new_weights = [], []
        for i in range(2):
            q = query[:, pl.ds((2 * h + i) * KEY, KEY)]
            cols = pl.ds(first + i * KEY, KEY)
            score = lax.dot_general(
                q, held[:, cols], (((1,), (1,)), ((), ())), preferred_element_type=jnp.float32
            )
            score = jnp.where(live, score * scale, -1e30)
            new = jnp.sum(q.astype(jnp.float32) * new_ref[:, cols].astype(jnp.float32), axis=1, keepdims=True) * scale
            top = jnp.maximum(jnp.max(score, axis=1, keepdims=True), new)
            score = jnp.exp(score - top)
            new = jnp.exp(new - top)
            inverse = 1.0 / (jnp.sum(score, axis=1, keepdims=True) + new)
            weights.append((score * inverse).astype(jnp.bfloat16))
            new_weights.append((new * inverse).astype(jnp.bfloat16).astype(jnp.float32))
        cols = pl.ds(first + 2 * KEY, value_width)
        mixture = jnp.dot(jnp.concatenate(weights, axis=0), held[:, cols], preferred_element_type=jnp.float32)
        new_value = new_ref[:, cols].astype(jnp.float32)
        one = mixture[:reqs] + new_weights[0] * new_value
        two = mixture[reqs:] + new_weights[1] * new_value
        diff = one - lam[h] * two
        norm = lax.rsqrt(jnp.mean(diff * diff, axis=1, keepdims=True) + 1e-05)
        mixed.append((diff * norm * 0.8).astype(jnp.bfloat16))
    weight_copy.wait()
    mixed = jnp.concatenate(mixed, axis=1)
    out[...] = jnp.dot(mixed, weight_held[...], preferred_element_type=jnp.float32).astype(out.dtype)


def attention(query, new_kv, pool, prompt_table, prompt_len, req_group, cont_table, cont_len, lam, weight):
    reqs = query.shape[0]
    page, width = pool.shape[1:]
    keys = (prompt_table.size + cont_table.size) * page
    return pl.pallas_call(
        attention_kernel,
        out_shape=jax.ShapeDtypeStruct((reqs, weight.shape[1]), jnp.bfloat16),
        in_specs=[SMEM] * 6 + [VMEM, VMEM, HBM, HBM],
        out_specs=VMEM,
        scratch_shapes=[
            pltpu.VMEM((keys, width), pool.dtype),
            pltpu.VMEM(weight.shape, weight.dtype),
            pltpu.SemaphoreType.DMA((2,)),
        ],
        compiler_params=pltpu.CompilerParams(vmem_limit_bytes=VMEM_BYTES),
        cost_estimate=pl.CostEstimate(
            flops=4 * reqs * keys * width + 2 * reqs * weight.size,
            bytes_accessed=2 * (keys * width + weight.size),
            transcendentals=reqs * keys * 2 * lam.shape[0],
        ),
        name="attention",
    )(prompt_table, prompt_len, req_group, cont_table, cont_len, lam, query, new_kv, *pinned(weight, pool))


def finish_kernel(count, hidden, gain, *refs):
    parts = refs[:count]
    hidden_out, normed_out = refs[count:]
    total = parts[0][...].astype(jnp.float32)
    for part in parts[1:]:
        total = total + part[...].astype(jnp.float32)
    summed = hidden[...].astype(jnp.float32) + total
    norm = lax.rsqrt(jnp.mean(summed * summed, axis=1, keepdims=True) + 1e-05)
    hidden_out[...] = summed.astype(hidden_out.dtype)
    normed_out[...] = (summed * norm * gain[...]).astype(normed_out.dtype)


def finish(hidden, gain, parts):
    shape = jax.ShapeDtypeStruct(hidden.shape, jnp.bfloat16)
    return pl.pallas_call(
        functools.partial(finish_kernel, len(parts)),
        out_shape=[shape, shape],
        in_specs=[VMEM] * (2 + len(parts)),
        out_specs=[VMEM, VMEM],
        compiler_params=pltpu.CompilerParams(vmem_limit_bytes=SMALL_VMEM_BYTES),
        name="finish",
    )(hidden, gain.reshape(1, -1), *parts)


def gather_kernel(choose, *refs):
    parts, out, sems = refs[:-2], refs[-2], refs[-1]
    for n, (place, options) in enumerate(choose()):
        target = out.at[pl.ds(place, MIG_CAP)]
        for part, taken in options:
            copy = pltpu.make_async_copy(parts[part], target, sems.at[n])
            if taken is None:
                copy.start()
            else:
                pl.when(taken)(copy.start)
    for n in range(MIG_REACH):
        pltpu.make_async_copy(parts[0], out.at[pl.ds(n * MIG_CAP, MIG_CAP)], sems.at[n]).wait()


def arrive(parts, choose):
    slots = MIG_REACH * MIG_CAP
    return pl.pallas_call(
        functools.partial(gather_kernel, choose),
        out_shape=jax.ShapeDtypeStruct((slots,) + parts[0].shape[1:], parts[0].dtype),
        in_specs=[VMEM] * len(parts),
        out_specs=HBM,
        scratch_shapes=[pltpu.SemaphoreType.DMA((MIG_REACH,))],
        compiler_params=pltpu.CompilerParams(vmem_limit_bytes=SMALL_VMEM_BYTES),
        name="arrive",
    )(*parts)


def routed(value, targets):
    count, width = lax.axis_size("req"), lax.axis_size("tp")
    pairs = []
    for s in range(count):
        for t in range(width):
            target = targets(s, t % 2)
            if target is not None:
                pairs.append((s * width + t, target % count * width + t))
    return lax.ppermute(value, ("req", "tp"), pairs)


def turn(s, steps):
    return s - s % MIG_REACH + (s + steps) % MIG_REACH


def route_first(s, odd):
    if not odd:
        return turn(s, 2)
    return s + 3 if s % MIG_REACH == 2 else turn(s, 3)


def route_second(s, odd):
    return turn(s, 2) if odd else s + 3


def lift_first(s, odd):
    return s + MIG_REACH if s % MIG_REACH in ((0, 2) if odd else (0, 1)) else None


def lift_second(s, odd):
    return s + MIG_REACH if odd and s % MIG_REACH in (0, 1) else None


def choose_straight():
    return [(n * MIG_CAP, [(n, None)]) for n in range(MIG_REACH)]


def choose_relayed():
    col = lax.rem(lax.axis_index("req"), MIG_REACH)
    odd = lax.rem(lax.axis_index("tp"), 2) == 1
    even = jnp.logical_not(odd)
    low, high = col < 2, col >= 2
    left, right = (col == 0) | (col == 2), (col == 1) | (col == 3)
    return [
        (0, [(5, None)]),
        (2, [(0, even & high), (2, even & low), (1, odd & high), (3, odd & low)]),
        (4, [(1, even), (0, odd & right), (2, odd & left)]),
        (6, [(4, None)]),
    ]


def migrate(cont_table, cont_len, migration, new_kv, pool):
    count, width = lax.axis_size("req"), lax.axis_size("tp")
    send = functools.partial(send_slots, cont_table, cont_len, migration, new_kv, pool)
    if MIG_REACH != 4 or count % MIG_REACH or count == MIG_REACH or width % 2:
        outgoing = send([(o, o) for o in range(1, MIG_REACH + 1)])
        return [shifted(part, "req", o + 1) for o, part in enumerate(outgoing)], choose_straight
    first, four, second, one = send([(2, 3), (4, 4), (3, 2), (1, 1)])
    first = routed(first, route_first)
    four = shifted(four, "req", 4)
    second = routed(second, route_second)
    one = shifted(one, "req", 1)
    return (first, second, four, one), choose_relayed


def shards(
    hidden_in,
    query,
    new_kv,
    pool_cache,
    prompt_table,
    prompt_len,
    req_group,
    cont_table,
    cont_len,
    migration,
    diff_lambda,
    out_weight,
    norm_gain,
):
    cont_table, migration = cont_table.T, migration.T
    received, choose = migrate(cont_table, cont_len, migration, new_kv, pool_cache)
    relayed = choose is choose_relayed
    if relayed:
        first, second, four, one = received
        first_up = routed(first, lift_first)
    partial = attention(
        query, new_kv, pool_cache, prompt_table, prompt_len, req_group, cont_table, cont_len, diff_lambda, out_weight
    )
    if relayed:
        second_up = routed(second, lift_second)
        received = (first, second, first_up, second_up, four, one)
    if lax.axis_size("tp") == 2:
        parts = [partial, shifted(partial, "tp", 1)]
    else:
        parts = [lax.psum(partial, "tp")]
    hidden_out, normed_out = finish(hidden_in, norm_gain, parts)
    arrived = arrive(received, choose)
    return (hidden_out, normed_out, arrived)


def solution(mesh):
    placed = (
        P("req", None),
        P("req", "tp"),
        P("req", "tp"),
        P("req", None, "tp"),
        P("req", None),
        P("req"),
        P("req"),
        P("req", None),
        P("req"),
        P("req", None),
        P("tp"),
        P("tp", None),
        P(),
    )
    return jax.shard_map(
        shards,
        mesh=mesh,
        in_specs=placed,
        out_specs=(P("req", None), P("req", None), P("req", None, "tp")),
        check_vma=False,
    )
```

```python
import functools

import jax
import jax.numpy as jnp
from jax import lax
from jax.experimental import pallas as pl
from jax.experimental.pallas import tpu as pltpu
from jax.sharding import PartitionSpec as P

MIG_REACH = 4
MIG_CAP = 2
KEY = 128
ROWS = 16

SMEM = pl.BlockSpec(memory_space=pltpu.SMEM)
VMEM = pl.BlockSpec(memory_space=pltpu.VMEM)
HBM = pl.BlockSpec(memory_space=pltpu.HBM)
VMEM_BYTES = 40 * 1024 * 1024
SMALL_VMEM_BYTES = 8 * 1024 * 1024


def pinned(*arrays):
    return [pltpu.with_memory_space_constraint(array, pltpu.HBM) for array in arrays]


def shifted(value, axis, steps):
    count = lax.axis_size(axis)
    pairs = [(source, (source + steps) % count) for source in range(count)]
    return lax.ppermute(value, axis, pairs)


def send_kernel(offsets, table_in, length_in, migration_in, new_in, pool, *refs):
    outs = refs[:MIG_REACH]
    table, length, migration, holder, new_held, new_rows, sems, small_sems = refs[MIG_REACH:]
    small = [
        pltpu.make_async_copy(source, target, small_sems.at[n])
        for n, (source, target) in enumerate(
            zip((table_in, length_in, migration_in, new_in), (table, length, migration, new_held))
        )
    ]
    for copy in small:
        copy.start()
    for copy in small[:3]:
        copy.wait()
    entries = migration.shape[1]
    pages, page = table.shape[0], pool.shape[1]
    for place in range(MIG_REACH * MIG_CAP):
        holder[place] = -1
    odd = lax.rem(lax.axis_index("req"), 2)
    where = []
    for n, (on_even, on_odd) in enumerate(offsets):
        offset = on_even + odd * (on_odd - on_even)
        for i in range(MIG_CAP):
            where.append((n * MIG_CAP + i, (offset - 1) * MIG_CAP + i, outs[n].at[i]))
    for e in range(entries):
        rank = jnp.int32(0)
        for before in range(e):
            rank += (migration[1, before] == migration[1, e]).astype(jnp.int32)
        holder[(migration[1, e] - 1) * MIG_CAP + rank] = migration[0, e]

    def page_copy(n, place, out, j):
        slot = jnp.maximum(holder[place], 0)
        return pltpu.make_async_copy(pool.at[table[j, slot]], out.at[pl.ds(j * page, page)], sems.at[n, j])

    def used(place, j):
        slot = holder[place]
        return (slot >= 0) & (length[jnp.maximum(slot, 0)] >= j * page)

    for n, place, out in where:
        for j in range(pages):

            @pl.when(used(place, j))
            def _():
                page_copy(n, place, out, j).start()

    small[3].wait()
    new_rows[...] = new_held[...].astype(jnp.float32)
    for n, place, out in where:
        slot = holder[place]
        safe = jnp.maximum(slot, 0)
        last = jnp.where(slot >= 0, length[safe], -1)
        for j in range(pages):

            @pl.when(used(place, j))
            def _():
                page_copy(n, place, out, j).wait()

            for low in range(j * page, (j + 1) * page, ROWS):

                @pl.when(last < low)
                def _():
                    out[pl.ds(low, ROWS)] = jnp.zeros((ROWS, out.shape[1]), out.dtype)

                @pl.when((last >= low) & (last < low + ROWS))
                def _():
                    held = out[pl.ds(low, ROWS)].astype(jnp.float32)
                    pos = low + lax.broadcasted_iota(jnp.int32, held.shape, 0)
                    new = jnp.where(pos == last, new_rows[pl.ds(safe, 1)], 0.0)
                    out[pl.ds(low, ROWS)] = jnp.where(pos < last, held, new).astype(out.dtype)


def send_slots(offsets, cont_table, cont_len, migration, new_kv, pool):
    span = cont_table.shape[0] * pool.shape[1]
    width = pool.shape[2]
    return pl.pallas_call(
        functools.partial(send_kernel, offsets),
        out_shape=[jax.ShapeDtypeStruct((MIG_CAP, span, width), pool.dtype)] * MIG_REACH,
        in_specs=[HBM] * 5,
        out_specs=[VMEM] * MIG_REACH,
        scratch_shapes=[
            pltpu.SMEM(cont_table.shape, jnp.int32),
            pltpu.SMEM(cont_len.shape, jnp.int32),
            pltpu.SMEM(migration.shape, jnp.int32),
            pltpu.SMEM((MIG_REACH * MIG_CAP,), jnp.int32),
            pltpu.VMEM(new_kv.shape, new_kv.dtype),
            pltpu.VMEM(new_kv.shape, jnp.float32),
            pltpu.SemaphoreType.DMA((MIG_REACH * MIG_CAP, cont_table.shape[0])),
            pltpu.SemaphoreType.DMA((4,)),
        ],
        compiler_params=pltpu.CompilerParams(vmem_limit_bytes=VMEM_BYTES),
        name="send_slots",
    )(*pinned(cont_table, cont_len, migration, new_kv, pool))


def column(values, count):
    rows = lax.broadcasted_iota(jnp.int32, (count, 1), 0)
    out = jnp.zeros((count, 1), jnp.int32)
    for r in range(count):
        out = jnp.where(rows == r, values[r], out)
    return out


def attention_kernel(low, prompt_table, prompt_len, req_group, cont_table, cont_len, lam, query, new_ref, *refs):
    prior = refs[:-6]
    weight, pool, out, held, weight_held, sems = refs[-6:]
    groups, prompt_pages = prompt_table.shape
    cont_pages, reqs = cont_table.shape
    page = pool.shape[1]
    span = prompt_pages * page
    own = cont_pages * page
    start = groups * span
    head_width = pool.shape[2] // lam.shape[0]
    value_width = head_width - 2 * KEY
    width = held.shape[1]
    heads = width // head_width
    columns = pl.ds(low * head_width, width)

    for g in range(groups):

        @pl.loop(0, prompt_pages)
        def _(j):
            at = pl.multiple_of(g * span + j * page, page)
            pltpu.make_async_copy(pool.at[prompt_table[g, j], :, columns], held.at[pl.ds(at, page)], sems.at[0]).start()

    @pl.loop(0, reqs)
    def _(r):
        for j in range(cont_pages):
            at = pl.multiple_of(start + r * own + j * page, page)
            pltpu.make_async_copy(pool.at[cont_table[j, r], :, columns], held.at[pl.ds(at, page)], sems.at[0]).start()

    rows = pl.ds(low * value_width, weight_held.shape[0])
    weight_copy = pltpu.make_async_copy(weight.at[rows], weight_held, sems.at[1])
    weight_copy.start()

    group_of = column(req_group, reqs)
    length_of = column(cont_len, reqs)
    biases = []
    pos = lax.broadcasted_iota(jnp.int32, (reqs, span), 1)
    for g in range(groups):
        live = (group_of == g) & (pos < prompt_len[g])
        biases.append(jnp.where(live, 0.0, -1e30))
    key = lax.broadcasted_iota(jnp.int32, (reqs, reqs * own), 1)
    pos = key - own * lax.broadcasted_iota(jnp.int32, (reqs, reqs * own), 0)
    biases.append(jnp.where((pos >= 0) & (pos < length_of), 0.0, -1e30))
    live = jnp.concatenate(biases, axis=1) == 0.0

    pltpu.make_async_copy(held, held, sems.at[0]).wait()

    scale = KEY**-0.5
    mixed = []
    for h in range(heads):
        first = h * head_width
        weights, new_weights = [], []
        for i in range(2):
            q = query[:, pl.ds((2 * (low + h) + i) * KEY, KEY)]
            cols = pl.ds(first + i * KEY, KEY)
            new_cols = pl.ds(low * head_width + first + i * KEY, KEY)
            score = lax.dot_general(
                q, held[:, cols], (((1,), (1,)), ((), ())), preferred_element_type=jnp.float32
            )
            score = jnp.where(live, score * scale, -1e30)
            new = jnp.sum(q.astype(jnp.float32) * new_ref[:, new_cols].astype(jnp.float32), axis=1, keepdims=True) * scale
            top = jnp.maximum(jnp.max(score, axis=1, keepdims=True), new)
            score = jnp.exp(score - top)
            new = jnp.exp(new - top)
            inverse = 1.0 / (jnp.sum(score, axis=1, keepdims=True) + new)
            weights.append((score * inverse).astype(jnp.bfloat16))
            new_weights.append((new * inverse).astype(jnp.bfloat16).astype(jnp.float32))
        cols = pl.ds(first + 2 * KEY, value_width)
        mixture = jnp.dot(jnp.concatenate(weights, axis=0), held[:, cols], preferred_element_type=jnp.float32)
        new_value = new_ref[:, pl.ds(low * head_width + first + 2 * KEY, value_width)].astype(jnp.float32)
        one = mixture[:reqs] + new_weights[0] * new_value
        two = mixture[reqs:] + new_weights[1] * new_value
        diff = one - lam[low + h] * two
        norm = lax.rsqrt(jnp.mean(diff * diff, axis=1, keepdims=True) + 1e-05)
        mixed.append((diff * norm * 0.8).astype(jnp.bfloat16))
    weight_copy.wait()
    mixed = jnp.concatenate(mixed, axis=1)
    product = jnp.dot(mixed, weight_held[...], preferred_element_type=jnp.float32)
    for part in prior:
        product = product + part[...]
    out[...] = product.astype(out.dtype)


def attention(query, new_kv, pool, prompt_table, prompt_len, req_group, cont_table, cont_len, lam, weight, low, high, prior):
    reqs = query.shape[0]
    page = pool.shape[1]
    heads = lam.shape[0]
    keys = (prompt_table.size + cont_table.size) * page
    width = pool.shape[2] // heads * (high - low)
    rows = weight.shape[0] // heads * (high - low)
    return pl.pallas_call(
        functools.partial(attention_kernel, low),
        out_shape=jax.ShapeDtypeStruct((reqs, weight.shape[1]), jnp.bfloat16 if high == heads else jnp.float32),
        in_specs=[SMEM] * 6 + [VMEM] * (2 + len(prior)) + [HBM, HBM],
        out_specs=VMEM,
        scratch_shapes=[
            pltpu.VMEM((keys, width), pool.dtype),
            pltpu.VMEM((rows, weight.shape[1]), weight.dtype),
            pltpu.SemaphoreType.DMA((2,)),
        ],
        compiler_params=pltpu.CompilerParams(vmem_limit_bytes=VMEM_BYTES),
        cost_estimate=pl.CostEstimate(
            flops=4 * reqs * keys * width + 2 * reqs * rows * weight.shape[1],
            bytes_accessed=2 * (keys * width + rows * weight.shape[1]),
            transcendentals=reqs * keys * 2 * (high - low),
        ),
        name="attention",
    )(prompt_table, prompt_len, req_group, cont_table, cont_len, lam, query, new_kv, *prior, *pinned(weight, pool))


def finish_kernel(count, hidden, gain, *refs):
    parts = refs[:count]
    hidden_out, normed_out = refs[count:]
    total = parts[0][...].astype(jnp.float32)
    for part in parts[1:]:
        total = total + part[...].astype(jnp.float32)
    summed = hidden[...].astype(jnp.float32) + total
    norm = lax.rsqrt(jnp.mean(summed * summed, axis=1, keepdims=True) + 1e-05)
    hidden_out[...] = summed.astype(hidden_out.dtype)
    normed_out[...] = (summed * norm * gain[...]).astype(normed_out.dtype)


def finish(hidden, gain, parts):
    shape = jax.ShapeDtypeStruct(hidden.shape, jnp.bfloat16)
    return pl.pallas_call(
        functools.partial(finish_kernel, len(parts)),
        out_shape=[shape, shape],
        in_specs=[VMEM] * (2 + len(parts)),
        out_specs=[VMEM, VMEM],
        compiler_params=pltpu.CompilerParams(vmem_limit_bytes=SMALL_VMEM_BYTES),
        name="finish",
    )(hidden, gain.reshape(1, -1), *parts)


def gather_kernel(choose, *refs):
    parts, out, sems = refs[:-2], refs[-2], refs[-1]
    for n, (place, options) in enumerate(choose()):
        target = out.at[pl.ds(place, MIG_CAP)]
        for part, taken in options:
            copy = pltpu.make_async_copy(parts[part], target, sems.at[n])
            if taken is None:
                copy.start()
            else:
                pl.when(taken)(copy.start)
    for n in range(MIG_REACH):
        pltpu.make_async_copy(parts[0], out.at[pl.ds(n * MIG_CAP, MIG_CAP)], sems.at[n]).wait()


def arrive(parts, choose):
    slots = MIG_REACH * MIG_CAP
    return pl.pallas_call(
        functools.partial(gather_kernel, choose),
        out_shape=jax.ShapeDtypeStruct((slots,) + parts[0].shape[1:], parts[0].dtype),
        in_specs=[VMEM] * len(parts),
        out_specs=HBM,
        scratch_shapes=[pltpu.SemaphoreType.DMA((MIG_REACH,))],
        compiler_params=pltpu.CompilerParams(vmem_limit_bytes=SMALL_VMEM_BYTES),
        name="arrive",
    )(*parts)


def routed(value, targets):
    count, width = lax.axis_size("req"), lax.axis_size("tp")
    pairs = []
    for s in range(count):
        for t in range(width):
            target = targets(s, t % 2)
            if target is not None:
                pairs.append((s * width + t, target % count * width + t))
    return lax.ppermute(value, ("req", "tp"), pairs)


def turn(s, steps):
    return s - s % MIG_REACH + (s + steps) % MIG_REACH


def route_early(s, odd):
    if s % 2 == 0:
        return s + 1
    return turn(s, 3) if odd else s + 3


def route_late(s, odd):
    return s + 3 if s % 2 == 0 else s + 1


def lift_two(s, odd):
    return s + MIG_REACH if s % MIG_REACH < 2 else None


def lift_early(s, odd):
    return s + MIG_REACH if odd and s % 2 == 0 else None


def choose_straight():
    return [(n * MIG_CAP, [(n, None)]) for n in range(MIG_REACH)]


def choose_relayed():
    col = lax.rem(lax.axis_index("req"), MIG_REACH)
    odd_core = lax.rem(lax.axis_index("tp"), 2) == 1
    odd = lax.rem(col, 2) == 1
    even = jnp.logical_not(odd)
    return [
        (0, [(2, odd), (4, even)]),
        (2, [(0, col >= 2), (1, col < 2)]),
        (4, [(4, odd), (2, even & jnp.logical_not(odd_core)), (3, even & odd_core)]),
        (6, [(5, None)]),
    ]


def can_relay():
    count = lax.axis_size("req")
    return MIG_REACH == 4 and count % MIG_REACH == 0 and count > MIG_REACH and lax.axis_size("tp") % 2 == 0


def shards(
    hidden_in,
    query,
    new_kv,
    pool_cache,
    prompt_table,
    prompt_len,
    req_group,
    cont_table,
    cont_len,
    migration,
    diff_lambda,
    out_weight,
    norm_gain,
):
    cont_table, migration = cont_table.T, migration.T
    heads = diff_lambda.shape[0]
    half = heads // 2
    attend = functools.partial(
        attention, query, new_kv, pool_cache, prompt_table, prompt_len, req_group, cont_table, cont_len, diff_lambda, out_weight
    )
    send = (cont_table, cont_len, migration, new_kv, pool_cache)
    prior = [attend(0, half, [])] if half else []
    if can_relay():
        two, four, early, late = send_slots(((2, 2), (4, 4), (1, 3), (3, 1)), *send)
        two = routed(two, lambda s, odd: turn(s, 2))
        four = shifted(four, "req", 4)
        early = routed(early, route_early)
        prior, two, early, late = lax.optimization_barrier((prior, two, early, late))
        two_up = routed(two, lift_two)
        early_up = routed(early, lift_early)
        late = routed(late, route_late)
        received, choose = (two, two_up, early, early_up, late, four), choose_relayed
    else:
        outgoing = send_slots(tuple((o, o) for o in range(1, MIG_REACH + 1)), *send)
        received = [shifted(part, "req", o + 1) for o, part in enumerate(outgoing)]
        choose = choose_straight
    partial = attend(half, heads, prior)
    if lax.axis_size("tp") == 2:
        parts = [partial, shifted(partial, "tp", 1)]
    else:
        parts = [lax.psum(partial, "tp")]
    hidden_out, normed_out = finish(hidden_in, norm_gain, parts)
    arrived = arrive(received, choose)
    return (hidden_out, normed_out, arrived)


def solution(mesh):
    placed = (
        P("req", None),
        P("req", "tp"),
        P("req", "tp"),
        P("req", None, "tp"),
        P("req", None),
        P("req"),
        P("req"),
        P("req", None),
        P("req"),
        P("req", None),
        P("tp"),
        P("tp", None),
        P(),
    )
    return jax.shard_map(
        shards,
        mesh=mesh,
        in_specs=placed,
        out_specs=(P("req", None), P("req", None), P("req", None, "tp")),
        check_vma=False,
    )
```

```python
import functools

import jax
import jax.numpy as jnp
from jax import lax
from jax.experimental import pallas as pl
from jax.experimental.pallas import tpu as pltpu
from jax.sharding import PartitionSpec as P

MIG_REACH = 4
MIG_CAP = 2
KEY = 128
ROWS = 16

SMEM = pl.BlockSpec(memory_space=pltpu.SMEM)
VMEM = pl.BlockSpec(memory_space=pltpu.VMEM)
HBM = pl.BlockSpec(memory_space=pltpu.HBM)
VMEM_BYTES = 40 * 1024 * 1024
SMALL_VMEM_BYTES = 8 * 1024 * 1024


def pinned(*arrays):
    return [pltpu.with_memory_space_constraint(array, pltpu.HBM) for array in arrays]


def shifted(value, axis, steps):
    count = lax.axis_size(axis)
    pairs = [(source, (source + steps) % count) for source in range(count)]
    return lax.ppermute(value, axis, pairs)


def send_kernel(offsets, table_in, length_in, migration_in, new_in, pool, *refs):
    outs = refs[:MIG_REACH]
    table, length, migration, holder, new_held, new_rows, sems, small_sems = refs[MIG_REACH:]
    small = [
        pltpu.make_async_copy(source, target, small_sems.at[n])
        for n, (source, target) in enumerate(
            zip((table_in, length_in, migration_in, new_in), (table, length, migration, new_held))
        )
    ]
    for copy in small:
        copy.start()
    for copy in small[:3]:
        copy.wait()
    entries = migration.shape[1]
    pages, page = table.shape[0], pool.shape[1]
    for place in range(MIG_REACH * MIG_CAP):
        holder[place] = -1
    odd = lax.rem(lax.axis_index("req"), 2)
    where = []
    for n, (on_even, on_odd) in enumerate(offsets):
        offset = on_even + odd * (on_odd - on_even)
        for i in range(MIG_CAP):
            where.append((n * MIG_CAP + i, (offset - 1) * MIG_CAP + i, outs[n].at[i]))
    for e in range(entries):
        rank = jnp.int32(0)
        for before in range(e):
            rank += (migration[1, before] == migration[1, e]).astype(jnp.int32)
        holder[(migration[1, e] - 1) * MIG_CAP + rank] = migration[0, e]

    def page_copy(n, place, out, j):
        slot = jnp.maximum(holder[place], 0)
        return pltpu.make_async_copy(pool.at[table[j, slot]], out.at[pl.ds(j * page, page)], sems.at[n, j])

    def used(place, j):
        slot = holder[place]
        return (slot >= 0) & (length[jnp.maximum(slot, 0)] >= j * page)

    for n, place, out in where:
        for j in range(pages):

            @pl.when(used(place, j))
            def _():
                page_copy(n, place, out, j).start()

    small[3].wait()
    new_rows[...] = new_held[...].astype(jnp.float32)
    for n, place, out in where:
        slot = holder[place]
        safe = jnp.maximum(slot, 0)
        last = jnp.where(slot >= 0, length[safe], -1)
        for j in range(pages):

            @pl.when(used(place, j))
            def _():
                page_copy(n, place, out, j).wait()

            for low in range(j * page, (j + 1) * page, ROWS):

                @pl.when(last < low)
                def _():
                    out[pl.ds(low, ROWS)] = jnp.zeros((ROWS, out.shape[1]), out.dtype)

                @pl.when((last >= low) & (last < low + ROWS))
                def _():
                    held = out[pl.ds(low, ROWS)].astype(jnp.float32)
                    pos = low + lax.broadcasted_iota(jnp.int32, held.shape, 0)
                    new = jnp.where(pos == last, new_rows[pl.ds(safe, 1)], 0.0)
                    out[pl.ds(low, ROWS)] = jnp.where(pos < last, held, new).astype(out.dtype)


def send_slots(offsets, cont_table, cont_len, migration, new_kv, pool):
    span = cont_table.shape[0] * pool.shape[1]
    width = pool.shape[2]
    return pl.pallas_call(
        functools.partial(send_kernel, offsets),
        out_shape=[jax.ShapeDtypeStruct((MIG_CAP, span, width), pool.dtype)] * MIG_REACH,
        in_specs=[HBM] * 5,
        out_specs=[VMEM] * MIG_REACH,
        scratch_shapes=[
            pltpu.SMEM(cont_table.shape, jnp.int32),
            pltpu.SMEM(cont_len.shape, jnp.int32),
            pltpu.SMEM(migration.shape, jnp.int32),
            pltpu.SMEM((MIG_REACH * MIG_CAP,), jnp.int32),
            pltpu.VMEM(new_kv.shape, new_kv.dtype),
            pltpu.VMEM(new_kv.shape, jnp.float32),
            pltpu.SemaphoreType.DMA((MIG_REACH * MIG_CAP, cont_table.shape[0])),
            pltpu.SemaphoreType.DMA((4,)),
        ],
        compiler_params=pltpu.CompilerParams(vmem_limit_bytes=VMEM_BYTES),
        name="send_slots",
    )(*pinned(cont_table, cont_len, migration, new_kv, pool))


def column(values, count):
    rows = lax.broadcasted_iota(jnp.int32, (count, 1), 0)
    out = jnp.zeros((count, 1), jnp.int32)
    for r in range(count):
        out = jnp.where(rows == r, values[r], out)
    return out


def attention_kernel(low, prompt_table, prompt_len, req_group, cont_table, cont_len, lam, query, new_ref, *refs):
    prior = refs[:-6]
    weight, pool, out, held, weight_held, sems = refs[-6:]
    groups, prompt_pages = prompt_table.shape
    cont_pages, reqs = cont_table.shape
    page = pool.shape[1]
    span = prompt_pages * page
    own = cont_pages * page
    start = groups * span
    head_width = pool.shape[2] // lam.shape[0]
    value_width = head_width - 2 * KEY
    width = held.shape[1]
    heads = width // head_width
    columns = pl.ds(low * head_width, width)

    for g in range(groups):

        @pl.loop(0, prompt_pages)
        def _(j):
            at = pl.multiple_of(g * span + j * page, page)
            pltpu.make_async_copy(pool.at[prompt_table[g, j], :, columns], held.at[pl.ds(at, page)], sems.at[0]).start()

    @pl.loop(0, reqs)
    def _(r):
        for j in range(cont_pages):
            at = pl.multiple_of(start + r * own + j * page, page)
            pltpu.make_async_copy(pool.at[cont_table[j, r], :, columns], held.at[pl.ds(at, page)], sems.at[0]).start()

    rows = pl.ds(low * value_width, weight_held.shape[0])
    weight_copy = pltpu.make_async_copy(weight.at[rows], weight_held, sems.at[1])
    weight_copy.start()

    group_of = column(req_group, reqs)
    length_of = column(cont_len, reqs)
    biases = []
    pos = lax.broadcasted_iota(jnp.int32, (reqs, span), 1)
    for g in range(groups):
        live = (group_of == g) & (pos < prompt_len[g])
        biases.append(jnp.where(live, 0.0, -1e30))
    key = lax.broadcasted_iota(jnp.int32, (reqs, reqs * own), 1)
    pos = key - own * lax.broadcasted_iota(jnp.int32, (reqs, reqs * own), 0)
    biases.append(jnp.where((pos >= 0) & (pos < length_of), 0.0, -1e30))
    live = jnp.concatenate(biases, axis=1) == 0.0

    pltpu.make_async_copy(held, held, sems.at[0]).wait()

    scale = KEY**-0.5
    mixed = []
    for h in range(heads):
        first = h * head_width
        weights, new_weights = [], []
        for i in range(2):
            q = query[:, pl.ds((2 * (low + h) + i) * KEY, KEY)]
            cols = pl.ds(first + i * KEY, KEY)
            new_cols = pl.ds(low * head_width + first + i * KEY, KEY)
            score = lax.dot_general(
                q, held[:, cols], (((1,), (1,)), ((), ())), preferred_element_type=jnp.float32
            )
            score = jnp.where(live, score * scale, -1e30)
            new = jnp.sum(q.astype(jnp.float32) * new_ref[:, new_cols].astype(jnp.float32), axis=1, keepdims=True) * scale
            top = jnp.maximum(jnp.max(score, axis=1, keepdims=True), new)
            score = jnp.exp(score - top)
            new = jnp.exp(new - top)
            inverse = 1.0 / (jnp.sum(score, axis=1, keepdims=True) + new)
            weights.append((score * inverse).astype(jnp.bfloat16))
            new_weights.append((new * inverse).astype(jnp.bfloat16).astype(jnp.float32))
        cols = pl.ds(first + 2 * KEY, value_width)
        mixture = jnp.dot(jnp.concatenate(weights, axis=0), held[:, cols], preferred_element_type=jnp.float32)
        new_value = new_ref[:, pl.ds(low * head_width + first + 2 * KEY, value_width)].astype(jnp.float32)
        one = mixture[:reqs] + new_weights[0] * new_value
        two = mixture[reqs:] + new_weights[1] * new_value
        diff = one - lam[low + h] * two
        norm = lax.rsqrt(jnp.mean(diff * diff, axis=1, keepdims=True) + 1e-05)
        mixed.append((diff * norm * 0.8).astype(jnp.bfloat16))
    weight_copy.wait()
    mixed = jnp.concatenate(mixed, axis=1)
    product = jnp.dot(mixed, weight_held[...], preferred_element_type=jnp.float32)
    for part in prior:
        product = product + part[...]
    out[...] = product.astype(out.dtype)


def attention(query, new_kv, pool, prompt_table, prompt_len, req_group, cont_table, cont_len, lam, weight, low, high, prior):
    reqs = query.shape[0]
    page = pool.shape[1]
    heads = lam.shape[0]
    keys = (prompt_table.size + cont_table.size) * page
    width = pool.shape[2] // heads * (high - low)
    rows = weight.shape[0] // heads * (high - low)
    return pl.pallas_call(
        functools.partial(attention_kernel, low),
        out_shape=jax.ShapeDtypeStruct((reqs, weight.shape[1]), jnp.bfloat16 if high == heads else jnp.float32),
        in_specs=[SMEM] * 6 + [VMEM] * (2 + len(prior)) + [HBM, HBM],
        out_specs=VMEM,
        scratch_shapes=[
            pltpu.VMEM((keys, width), pool.dtype),
            pltpu.VMEM((rows, weight.shape[1]), weight.dtype),
            pltpu.SemaphoreType.DMA((2,)),
        ],
        compiler_params=pltpu.CompilerParams(vmem_limit_bytes=VMEM_BYTES),
        cost_estimate=pl.CostEstimate(
            flops=4 * reqs * keys * width + 2 * reqs * rows * weight.shape[1],
            bytes_accessed=2 * (keys * width + rows * weight.shape[1]),
            transcendentals=reqs * keys * 2 * (high - low),
        ),
        name="attention",
    )(prompt_table, prompt_len, req_group, cont_table, cont_len, lam, query, new_kv, *prior, *pinned(weight, pool))


def finish_kernel(count, hidden, gain, *refs):
    parts = refs[:count]
    hidden_out, normed_out = refs[count:]
    total = parts[0][...].astype(jnp.float32)
    for part in parts[1:]:
        total = total + part[...].astype(jnp.float32)
    summed = hidden[...].astype(jnp.float32) + total
    norm = lax.rsqrt(jnp.mean(summed * summed, axis=1, keepdims=True) + 1e-05)
    hidden_out[...] = summed.astype(hidden_out.dtype)
    normed_out[...] = (summed * norm * gain[...]).astype(normed_out.dtype)


def finish(hidden, gain, parts):
    shape = jax.ShapeDtypeStruct(hidden.shape, jnp.bfloat16)
    return pl.pallas_call(
        functools.partial(finish_kernel, len(parts)),
        out_shape=[shape, shape],
        in_specs=[VMEM] * (2 + len(parts)),
        out_specs=[VMEM, VMEM],
        compiler_params=pltpu.CompilerParams(vmem_limit_bytes=SMALL_VMEM_BYTES),
        name="finish",
    )(hidden, gain.reshape(1, -1), *parts)


def gather_kernel(choose, *refs):
    parts, out, sems = refs[:-2], refs[-2], refs[-1]
    for n, (place, options) in enumerate(choose()):
        target = out.at[pl.ds(place, MIG_CAP)]
        for part, taken in options:
            copy = pltpu.make_async_copy(parts[part], target, sems.at[n])
            if taken is None:
                copy.start()
            else:
                pl.when(taken)(copy.start)
    for n in range(MIG_REACH):
        pltpu.make_async_copy(parts[0], out.at[pl.ds(n * MIG_CAP, MIG_CAP)], sems.at[n]).wait()


def arrive(parts, choose):
    slots = MIG_REACH * MIG_CAP
    return pl.pallas_call(
        functools.partial(gather_kernel, choose),
        out_shape=jax.ShapeDtypeStruct((slots,) + parts[0].shape[1:], parts[0].dtype),
        in_specs=[VMEM] * len(parts),
        out_specs=HBM,
        scratch_shapes=[pltpu.SemaphoreType.DMA((MIG_REACH,))],
        compiler_params=pltpu.CompilerParams(vmem_limit_bytes=SMALL_VMEM_BYTES),
        name="arrive",
    )(*parts)


def routed(value, targets):
    count, width = lax.axis_size("req"), lax.axis_size("tp")
    pairs = []
    for s in range(count):
        for t in range(width):
            target = targets(s, t % 2)
            if target is not None:
                pairs.append((s * width + t, target % count * width + t))
    return lax.ppermute(value, ("req", "tp"), pairs)


def turn(s, steps):
    return s - s % MIG_REACH + (s + steps) % MIG_REACH


def route_early(s, odd):
    if s % 2 == 0:
        return s + 1
    return turn(s, 3) if odd else s + 3


def route_late(s, odd):
    return s + 3 if s % 2 == 0 else s + 1


def lift_two(s, odd):
    return s + MIG_REACH if s % MIG_REACH < 2 else None


def lift_early(s, odd):
    return s + MIG_REACH if odd and s % 2 == 0 else None


def choose_straight():
    return [(n * MIG_CAP, [(n, None)]) for n in range(MIG_REACH)]


def choose_relayed():
    col = lax.rem(lax.axis_index("req"), MIG_REACH)
    odd_core = lax.rem(lax.axis_index("tp"), 2) == 1
    odd = lax.rem(col, 2) == 1
    even = jnp.logical_not(odd)
    return [
        (0, [(2, odd), (4, even)]),
        (2, [(0, col >= 2), (1, col < 2)]),
        (4, [(4, odd), (2, even & jnp.logical_not(odd_core)), (3, even & odd_core)]),
        (6, [(5, None)]),
    ]


def can_relay():
    count = lax.axis_size("req")
    return MIG_REACH == 4 and count % MIG_REACH == 0 and count > MIG_REACH and lax.axis_size("tp") % 2 == 0


def shards(
    hidden_in,
    query,
    new_kv,
    pool_cache,
    prompt_table,
    prompt_len,
    req_group,
    cont_table,
    cont_len,
    migration,
    diff_lambda,
    out_weight,
    norm_gain,
):
    cont_table, migration = cont_table.T, migration.T
    heads = diff_lambda.shape[0]
    half = heads // 2
    attend = functools.partial(
        attention, query, new_kv, pool_cache, prompt_table, prompt_len, req_group, cont_table, cont_len, diff_lambda, out_weight
    )
    send = (cont_table, cont_len, migration, new_kv, pool_cache)
    prior = [attend(0, half, [])] if half else []
    if can_relay():
        two, four, early, late = send_slots(((2, 2), (4, 4), (1, 3), (3, 1)), *send)
        two = routed(two, lambda s, odd: turn(s, 2))
        four = shifted(four, "req", 4)
        early = routed(early, route_early)
        prior, two = lax.optimization_barrier((prior, two))
        two_up = routed(two, lift_two)
        two, late = lax.optimization_barrier((two, late))
        late = routed(late, route_late)
        early_up = routed(early, lift_early)
        received, choose = (two, two_up, early, early_up, late, four), choose_relayed
    else:
        outgoing = send_slots(tuple((o, o) for o in range(1, MIG_REACH + 1)), *send)
        received = [shifted(part, "req", o + 1) for o, part in enumerate(outgoing)]
        choose = choose_straight
    partial = attend(half, heads, prior)
    if lax.axis_size("tp") == 2:
        parts = [partial, shifted(partial, "tp", 1)]
    else:
        parts = [lax.psum(partial, "tp")]
    hidden_out, normed_out = finish(hidden_in, norm_gain, parts)
    arrived = arrive(received, choose)
    return (hidden_out, normed_out, arrived)


def solution(mesh):
    placed = (
        P("req", None),
        P("req", "tp"),
        P("req", "tp"),
        P("req", None, "tp"),
        P("req", None),
        P("req"),
        P("req"),
        P("req", None),
        P("req"),
        P("req", None),
        P("tp"),
        P("tp", None),
        P(),
    )
    return jax.shard_map(
        shards,
        mesh=mesh,
        in_specs=placed,
        out_specs=(P("req", None), P("req", None), P("req", None, "tp")),
        check_vma=False,
    )
```

```python
import functools

import jax
import jax.numpy as jnp
from jax import lax
from jax.experimental import pallas as pl
from jax.experimental.pallas import tpu as pltpu
from jax.sharding import PartitionSpec as P

MIG_REACH = 4
MIG_CAP = 2
KEY = 128
ROWS = 16

SMEM = pl.BlockSpec(memory_space=pltpu.SMEM)
VMEM = pl.BlockSpec(memory_space=pltpu.VMEM)
HBM = pl.BlockSpec(memory_space=pltpu.HBM)
VMEM_BYTES = 40 * 1024 * 1024
SMALL_VMEM_BYTES = 8 * 1024 * 1024


def pinned(*arrays):
    return [pltpu.with_memory_space_constraint(array, pltpu.HBM) for array in arrays]


def shifted(value, axis, steps):
    count = lax.axis_size(axis)
    pairs = [(source, (source + steps) % count) for source in range(count)]
    return lax.ppermute(value, axis, pairs)


def send_kernel(offsets, table_in, length_in, migration_in, new_in, pool, *refs):
    outs = refs[: len(offsets)]
    table, length, migration, holder, new_held, new_rows, sems, small_sems = refs[len(offsets) :]
    small = [
        pltpu.make_async_copy(source, target, small_sems.at[n])
        for n, (source, target) in enumerate(
            zip((table_in, length_in, migration_in, new_in), (table, length, migration, new_held))
        )
    ]
    for copy in small:
        copy.start()
    for copy in small[:3]:
        copy.wait()
    entries = migration.shape[1]
    pages, page = table.shape[0], pool.shape[1]
    for place in range(MIG_REACH * MIG_CAP):
        holder[place] = -1
    odd_req, odd_tp = lax.rem(lax.axis_index("req"), 2), lax.rem(lax.axis_index("tp"), 2)
    where = []
    for n, by_req in enumerate(offsets):
        even, odd = [on[0] + odd_tp * (on[1] - on[0]) for on in by_req]
        offset = even + odd_req * (odd - even)
        for i in range(MIG_CAP):
            where.append((n * MIG_CAP + i, (offset - 1) * MIG_CAP + i, outs[n].at[i]))
    for e in range(entries):
        rank = jnp.int32(0)
        for before in range(e):
            rank += (migration[1, before] == migration[1, e]).astype(jnp.int32)
        holder[(migration[1, e] - 1) * MIG_CAP + rank] = migration[0, e]

    def page_copy(n, place, out, j):
        slot = jnp.maximum(holder[place], 0)
        return pltpu.make_async_copy(pool.at[table[j, slot]], out.at[pl.ds(j * page, page)], sems.at[n, j])

    def used(place, j):
        slot = holder[place]
        return (slot >= 0) & (length[jnp.maximum(slot, 0)] >= j * page)

    for n, place, out in where:
        for j in range(pages):

            @pl.when(used(place, j))
            def _():
                page_copy(n, place, out, j).start()

    small[3].wait()
    new_rows[...] = new_held[...].astype(jnp.float32)
    for n, place, out in where:
        slot = holder[place]
        safe = jnp.maximum(slot, 0)
        last = jnp.where(slot >= 0, length[safe], -1)
        for j in range(pages):

            @pl.when(used(place, j))
            def _():
                page_copy(n, place, out, j).wait()

            for low in range(j * page, (j + 1) * page, ROWS):

                @pl.when(last < low)
                def _():
                    out[pl.ds(low, ROWS)] = jnp.zeros((ROWS, out.shape[1]), out.dtype)

                @pl.when((last >= low) & (last < low + ROWS))
                def _():
                    held = out[pl.ds(low, ROWS)].astype(jnp.float32)
                    pos = low + lax.broadcasted_iota(jnp.int32, held.shape, 0)
                    new = jnp.where(pos == last, new_rows[pl.ds(safe, 1)], 0.0)
                    out[pl.ds(low, ROWS)] = jnp.where(pos < last, held, new).astype(out.dtype)


def send_slots(offsets, cont_table, cont_len, migration, new_kv, pool):
    span = cont_table.shape[0] * pool.shape[1]
    width = pool.shape[2]
    return pl.pallas_call(
        functools.partial(send_kernel, offsets),
        out_shape=[jax.ShapeDtypeStruct((MIG_CAP, span, width), pool.dtype)] * len(offsets),
        in_specs=[HBM] * 5,
        out_specs=[VMEM] * len(offsets),
        scratch_shapes=[
            pltpu.SMEM(cont_table.shape, jnp.int32),
            pltpu.SMEM(cont_len.shape, jnp.int32),
            pltpu.SMEM(migration.shape, jnp.int32),
            pltpu.SMEM((MIG_REACH * MIG_CAP,), jnp.int32),
            pltpu.VMEM(new_kv.shape, new_kv.dtype),
            pltpu.VMEM(new_kv.shape, jnp.float32),
            pltpu.SemaphoreType.DMA((len(offsets) * MIG_CAP, cont_table.shape[0])),
            pltpu.SemaphoreType.DMA((4,)),
        ],
        compiler_params=pltpu.CompilerParams(vmem_limit_bytes=VMEM_BYTES),
        name="send_slots",
    )(*pinned(cont_table, cont_len, migration, new_kv, pool))


def column(values, count):
    rows = lax.broadcasted_iota(jnp.int32, (count, 1), 0)
    out = jnp.zeros((count, 1), jnp.int32)
    for r in range(count):
        out = jnp.where(rows == r, values[r], out)
    return out


def attention_kernel(low, prompt_table, prompt_len, req_group, cont_table, cont_len, lam, query, new_ref, *refs):
    prior = refs[:-6]
    weight, pool, out, held, weight_held, sems = refs[-6:]
    groups, prompt_pages = prompt_table.shape
    cont_pages, reqs = cont_table.shape
    page = pool.shape[1]
    span = prompt_pages * page
    own = cont_pages * page
    start = groups * span
    head_width = pool.shape[2] // lam.shape[0]
    value_width = head_width - 2 * KEY
    width = held.shape[1]
    heads = width // head_width
    columns = pl.ds(low * head_width, width)

    for g in range(groups):

        @pl.loop(0, prompt_pages)
        def _(j):
            at = pl.multiple_of(g * span + j * page, page)
            pltpu.make_async_copy(pool.at[prompt_table[g, j], :, columns], held.at[pl.ds(at, page)], sems.at[0]).start()

    @pl.loop(0, reqs)
    def _(r):
        for j in range(cont_pages):
            at = pl.multiple_of(start + r * own + j * page, page)
            pltpu.make_async_copy(pool.at[cont_table[j, r], :, columns], held.at[pl.ds(at, page)], sems.at[0]).start()

    rows = pl.ds(low * value_width, weight_held.shape[0])
    weight_copy = pltpu.make_async_copy(weight.at[rows], weight_held, sems.at[1])
    weight_copy.start()

    group_of = column(req_group, reqs)
    length_of = column(cont_len, reqs)
    biases = []
    pos = lax.broadcasted_iota(jnp.int32, (reqs, span), 1)
    for g in range(groups):
        live = (group_of == g) & (pos < prompt_len[g])
        biases.append(jnp.where(live, 0.0, -1e30))
    key = lax.broadcasted_iota(jnp.int32, (reqs, reqs * own), 1)
    pos = key - own * lax.broadcasted_iota(jnp.int32, (reqs, reqs * own), 0)
    biases.append(jnp.where((pos >= 0) & (pos < length_of), 0.0, -1e30))
    live = jnp.concatenate(biases, axis=1) == 0.0

    pltpu.make_async_copy(held, held, sems.at[0]).wait()

    scale = KEY**-0.5
    mixed = []
    for h in range(heads):
        first = h * head_width
        weights, new_weights = [], []
        for i in range(2):
            q = query[:, pl.ds((2 * (low + h) + i) * KEY, KEY)]
            cols = pl.ds(first + i * KEY, KEY)
            new_cols = pl.ds(low * head_width + first + i * KEY, KEY)
            score = lax.dot_general(
                q, held[:, cols], (((1,), (1,)), ((), ())), preferred_element_type=jnp.float32
            )
            score = jnp.where(live, score * scale, -1e30)
            new = jnp.sum(q.astype(jnp.float32) * new_ref[:, new_cols].astype(jnp.float32), axis=1, keepdims=True) * scale
            top = jnp.maximum(jnp.max(score, axis=1, keepdims=True), new)
            score = jnp.exp(score - top)
            new = jnp.exp(new - top)
            inverse = 1.0 / (jnp.sum(score, axis=1, keepdims=True) + new)
            weights.append((score * inverse).astype(jnp.bfloat16))
            new_weights.append((new * inverse).astype(jnp.bfloat16).astype(jnp.float32))
        cols = pl.ds(first + 2 * KEY, value_width)
        mixture = jnp.dot(jnp.concatenate(weights, axis=0), held[:, cols], preferred_element_type=jnp.float32)
        new_value = new_ref[:, pl.ds(low * head_width + first + 2 * KEY, value_width)].astype(jnp.float32)
        one = mixture[:reqs] + new_weights[0] * new_value
        two = mixture[reqs:] + new_weights[1] * new_value
        diff = one - lam[low + h] * two
        norm = lax.rsqrt(jnp.mean(diff * diff, axis=1, keepdims=True) + 1e-05)
        mixed.append((diff * norm * 0.8).astype(jnp.bfloat16))
    weight_copy.wait()
    mixed = jnp.concatenate(mixed, axis=1)
    product = jnp.dot(mixed, weight_held[...], preferred_element_type=jnp.float32)
    for part in prior:
        product = product + part[...]
    out[...] = product.astype(out.dtype)


def attention(query, new_kv, pool, prompt_table, prompt_len, req_group, cont_table, cont_len, lam, weight, low, high, prior):
    reqs = query.shape[0]
    page = pool.shape[1]
    heads = lam.shape[0]
    keys = (prompt_table.size + cont_table.size) * page
    width = pool.shape[2] // heads * (high - low)
    rows = weight.shape[0] // heads * (high - low)
    return pl.pallas_call(
        functools.partial(attention_kernel, low),
        out_shape=jax.ShapeDtypeStruct((reqs, weight.shape[1]), jnp.bfloat16 if high == heads else jnp.float32),
        in_specs=[SMEM] * 6 + [VMEM] * (2 + len(prior)) + [HBM, HBM],
        out_specs=VMEM,
        scratch_shapes=[
            pltpu.VMEM((keys, width), pool.dtype),
            pltpu.VMEM((rows, weight.shape[1]), weight.dtype),
            pltpu.SemaphoreType.DMA((2,)),
        ],
        compiler_params=pltpu.CompilerParams(vmem_limit_bytes=VMEM_BYTES),
        cost_estimate=pl.CostEstimate(
            flops=4 * reqs * keys * width + 2 * reqs * rows * weight.shape[1],
            bytes_accessed=2 * (keys * width + rows * weight.shape[1]),
            transcendentals=reqs * keys * 2 * (high - low),
        ),
        name="attention",
    )(prompt_table, prompt_len, req_group, cont_table, cont_len, lam, query, new_kv, *prior, *pinned(weight, pool))


def finish_kernel(count, hidden, gain, *refs):
    parts = refs[:count]
    hidden_out, normed_out = refs[count:]
    total = parts[0][...].astype(jnp.float32)
    for part in parts[1:]:
        total = total + part[...].astype(jnp.float32)
    summed = hidden[...].astype(jnp.float32) + total
    norm = lax.rsqrt(jnp.mean(summed * summed, axis=1, keepdims=True) + 1e-05)
    hidden_out[...] = summed.astype(hidden_out.dtype)
    normed_out[...] = (summed * norm * gain[...]).astype(normed_out.dtype)


def finish(hidden, gain, parts):
    shape = jax.ShapeDtypeStruct(hidden.shape, jnp.bfloat16)
    return pl.pallas_call(
        functools.partial(finish_kernel, len(parts)),
        out_shape=[shape, shape],
        in_specs=[VMEM] * (2 + len(parts)),
        out_specs=[VMEM, VMEM],
        compiler_params=pltpu.CompilerParams(vmem_limit_bytes=SMALL_VMEM_BYTES),
        name="finish",
    )(hidden, gain.reshape(1, -1), *parts)


def gather_kernel(choose, count, *refs):
    parts, out, sems = refs[:count], refs[-2], refs[-1]
    copies = [
        (pltpu.make_async_copy(parts[part], out.at[pl.ds(place, MIG_CAP)], sems.at[n]), taken)
        for n, (place, part, taken) in enumerate(choose())
    ]
    for copy, taken in copies:
        pl.when(taken)(copy.start)
    for copy, taken in copies:
        pl.when(taken)(copy.wait)


def arrive(parts, choose, rest=None):
    slots = MIG_REACH * MIG_CAP
    extra = [] if rest is None else pinned(rest)
    return pl.pallas_call(
        functools.partial(gather_kernel, choose, len(parts)),
        out_shape=jax.ShapeDtypeStruct((slots,) + parts[0].shape[1:], parts[0].dtype),
        in_specs=[VMEM] * len(parts) + [HBM] * len(extra),
        out_specs=HBM,
        scratch_shapes=[pltpu.SemaphoreType.DMA((2 * MIG_REACH,))],
        input_output_aliases={len(parts): 0} if extra else {},
        compiler_params=pltpu.CompilerParams(vmem_limit_bytes=SMALL_VMEM_BYTES),
        name="arrive",
    )(*parts, *extra)


def routed(value, targets):
    count, width = lax.axis_size("req"), lax.axis_size("tp")
    pairs = []
    for s in range(count):
        for t in range(width):
            target = targets(s, t % 2)
            if target is not None:
                pairs.append((s * width + t, target % count * width + t))
    return lax.ppermute(value, ("req", "tp"), pairs)


def turn(s, steps):
    return s - s % MIG_REACH + (s + steps) % MIG_REACH


def route_first(s, odd):
    if not odd:
        return turn(s, 2)
    return turn(s, 3) if s % 2 else s + 1


def route_second(s, odd):
    if odd:
        return turn(s, 2)
    return None if s % 2 else s + 1


def route_three(s, odd):
    return s + 3 if s % 2 and not odd else None


def route_late(s, odd):
    return s + 1 if s % 2 else s + 3


def lift_first(s, odd):
    return s + MIG_REACH if s % MIG_REACH in ((0, 2) if odd else (0, 1)) else None


def lift_second(s, odd):
    return s + MIG_REACH if odd and s % MIG_REACH < 2 else None


def choose_straight():
    return [(n * MIG_CAP, n, True) for n in range(MIG_REACH)]


def where_am_i():
    col = lax.rem(lax.axis_index("req"), MIG_REACH)
    odd = lax.rem(col, 2) == 1
    odd_core = lax.rem(lax.axis_index("tp"), 2) == 1
    return odd, jnp.logical_not(odd), odd_core, jnp.logical_not(odd_core), col < 2, col >= 2


def choose_sooner():
    odd, even, odd_core, even_core, low, high = where_am_i()
    return [
        (0, 1, odd & even_core),
        (0, 0, odd & odd_core),
        (2, 0, high & even_core),
        (2, 2, low & even_core),
        (2, 1, high & odd_core),
        (4, 3, even & even_core),
        (4, 2, even & odd_core),
        (6, 4, True),
    ]


def choose_later():
    odd, even, odd_core, even_core, low, high = where_am_i()
    return [(0, 1, even), (2, 0, low & odd_core), (4, 1, odd)]


def can_relay():
    count = lax.axis_size("req")
    return MIG_REACH == 4 and count % MIG_REACH == 0 and count > MIG_REACH and lax.axis_size("tp") % 2 == 0


def shards(
    hidden_in,
    query,
    new_kv,
    pool_cache,
    prompt_table,
    prompt_len,
    req_group,
    cont_table,
    cont_len,
    migration,
    diff_lambda,
    out_weight,
    norm_gain,
):
    cont_table, migration = cont_table.T, migration.T
    heads = diff_lambda.shape[0]
    half = heads // 2
    attend = functools.partial(
        attention, query, new_kv, pool_cache, prompt_table, prompt_len, req_group, cont_table, cont_len, diff_lambda, out_weight
    )
    send = (cont_table, cont_len, migration, new_kv, pool_cache)
    prior = [attend(0, half, [])] if half else []
    if can_relay():
        first, four, second = send_slots((((2, 1), (2, 3)), ((4, 4), (4, 4)), ((1, 2), (3, 2))), *send)
        first = routed(first, route_first)
        four = shifted(four, "req", 4)
        three = routed(second, route_three)
        second = routed(second, route_second)
        prior, first = lax.optimization_barrier((prior, first))
        first_up = routed(first, lift_first)
        first, cont_len_late = lax.optimization_barrier((first, cont_len))
        (late,) = send_slots((((3, 3), (1, 1)),), cont_table, cont_len_late, *send[2:])
        late, second = lax.optimization_barrier((late, second))
        second_up = routed(second, lift_second)
        prior, second, late = lax.optimization_barrier((prior, second, late))
        late = routed(late, route_late)
    else:
        outgoing = send_slots(tuple(((o, o), (o, o)) for o in range(1, MIG_REACH + 1)), *send)
        arrived = arrive([shifted(part, "req", o + 1) for o, part in enumerate(outgoing)], choose_straight)
    partial = attend(half, heads, prior)
    if can_relay():
        partial, four = lax.optimization_barrier((partial, four))
        sooner = arrive((first, second, first_up, three, four), choose_sooner)
        arrived = arrive((second_up, late), choose_later, sooner)
    if lax.axis_size("tp") == 2:
        parts = [partial, shifted(partial, "tp", 1)]
    else:
        parts = [lax.psum(partial, "tp")]
    hidden_out, normed_out = finish(hidden_in, norm_gain, parts)
    return (hidden_out, normed_out, arrived)


def solution(mesh):
    placed = (
        P("req", None),
        P("req", "tp"),
        P("req", "tp"),
        P("req", None, "tp"),
        P("req", None),
        P("req"),
        P("req"),
        P("req", None),
        P("req"),
        P("req", None),
        P("tp"),
        P("tp", None),
        P(),
    )
    return jax.shard_map(
        shards,
        mesh=mesh,
        in_specs=placed,
        out_specs=(P("req", None), P("req", None), P("req", None, "tp")),
        check_vma=False,
    )
```

```python
import functools

import jax
import jax.numpy as jnp
from jax import lax
from jax.experimental import pallas as pl
from jax.experimental.pallas import tpu as pltpu
from jax.sharding import PartitionSpec as P

MIG_REACH = 4
MIG_CAP = 2
KEY = 128
ROWS = 16

SMEM = pl.BlockSpec(memory_space=pltpu.SMEM)
VMEM = pl.BlockSpec(memory_space=pltpu.VMEM)
HBM = pl.BlockSpec(memory_space=pltpu.HBM)
VMEM_BYTES = 40 * 1024 * 1024
SMALL_VMEM_BYTES = 8 * 1024 * 1024


def pinned(*arrays):
    return [pltpu.with_memory_space_constraint(array, pltpu.HBM) for array in arrays]


def shifted(value, axis, steps):
    count = lax.axis_size(axis)
    pairs = [(source, (source + steps) % count) for source in range(count)]
    return lax.ppermute(value, axis, pairs)


def send_kernel(offsets, table_in, length_in, migration_in, new_in, pool, *refs):
    outs = refs[: len(offsets)]
    table, length, migration, holder, new_held, new_rows, sems, small_sems = refs[len(offsets) :]
    small = [
        pltpu.make_async_copy(source, target, small_sems.at[n])
        for n, (source, target) in enumerate(
            zip((table_in, length_in, migration_in, new_in), (table, length, migration, new_held))
        )
    ]
    for copy in small:
        copy.start()
    for copy in small[:3]:
        copy.wait()
    entries = migration.shape[1]
    pages, page = table.shape[0], pool.shape[1]
    for place in range(MIG_REACH * MIG_CAP):
        holder[place] = -1
    odd_req, odd_tp = lax.rem(lax.axis_index("req"), 2), lax.rem(lax.axis_index("tp"), 2)
    where = []
    for n, by_req in enumerate(offsets):
        even, odd = [on[0] + odd_tp * (on[1] - on[0]) for on in by_req]
        offset = even + odd_req * (odd - even)
        for i in range(MIG_CAP):
            where.append((n * MIG_CAP + i, (offset - 1) * MIG_CAP + i, outs[n].at[i]))
    for e in range(entries):
        rank = jnp.int32(0)
        for before in range(e):
            rank += (migration[1, before] == migration[1, e]).astype(jnp.int32)
        holder[(migration[1, e] - 1) * MIG_CAP + rank] = migration[0, e]

    def page_copy(n, place, out, j):
        slot = jnp.maximum(holder[place], 0)
        return pltpu.make_async_copy(pool.at[table[j, slot]], out.at[pl.ds(j * page, page)], sems.at[n, j])

    def used(place, j):
        slot = holder[place]
        return (slot >= 0) & (length[jnp.maximum(slot, 0)] >= j * page)

    for n, place, out in where:
        for j in range(pages):

            @pl.when(used(place, j))
            def _():
                page_copy(n, place, out, j).start()

    small[3].wait()
    new_rows[...] = new_held[...].astype(jnp.float32)
    for n, place, out in where:
        slot = holder[place]
        safe = jnp.maximum(slot, 0)
        last = jnp.where(slot >= 0, length[safe], -1)
        for j in range(pages):

            @pl.when(used(place, j))
            def _():
                page_copy(n, place, out, j).wait()

            for low in range(j * page, (j + 1) * page, ROWS):

                @pl.when(last < low)
                def _():
                    out[pl.ds(low, ROWS)] = jnp.zeros((ROWS, out.shape[1]), out.dtype)

                @pl.when((last >= low) & (last < low + ROWS))
                def _():
                    held = out[pl.ds(low, ROWS)].astype(jnp.float32)
                    pos = low + lax.broadcasted_iota(jnp.int32, held.shape, 0)
                    new = jnp.where(pos == last, new_rows[pl.ds(safe, 1)], 0.0)
                    out[pl.ds(low, ROWS)] = jnp.where(pos < last, held, new).astype(out.dtype)


def send_slots(offsets, cont_table, cont_len, migration, new_kv, pool):
    span = cont_table.shape[0] * pool.shape[1]
    width = pool.shape[2]
    return pl.pallas_call(
        functools.partial(send_kernel, offsets),
        out_shape=[jax.ShapeDtypeStruct((MIG_CAP, span, width), pool.dtype)] * len(offsets),
        in_specs=[HBM] * 5,
        out_specs=[VMEM] * len(offsets),
        scratch_shapes=[
            pltpu.SMEM(cont_table.shape, jnp.int32),
            pltpu.SMEM(cont_len.shape, jnp.int32),
            pltpu.SMEM(migration.shape, jnp.int32),
            pltpu.SMEM((MIG_REACH * MIG_CAP,), jnp.int32),
            pltpu.VMEM(new_kv.shape, new_kv.dtype),
            pltpu.VMEM(new_kv.shape, jnp.float32),
            pltpu.SemaphoreType.DMA((len(offsets) * MIG_CAP, cont_table.shape[0])),
            pltpu.SemaphoreType.DMA((4,)),
        ],
        compiler_params=pltpu.CompilerParams(vmem_limit_bytes=VMEM_BYTES),
        name="send_slots",
    )(*pinned(cont_table, cont_len, migration, new_kv, pool))


def column(values, count):
    rows = lax.broadcasted_iota(jnp.int32, (count, 1), 0)
    out = jnp.zeros((count, 1), jnp.int32)
    for r in range(count):
        out = jnp.where(rows == r, values[r], out)
    return out


def attention_kernel(low, prompt_table, prompt_len, req_group, cont_table, cont_len, lam, query, new_ref, *refs):
    prior = refs[:-6]
    weight, pool, out, held, weight_held, sems = refs[-6:]
    groups, prompt_pages = prompt_table.shape
    cont_pages, reqs = cont_table.shape
    page = pool.shape[1]
    span = prompt_pages * page
    own = cont_pages * page
    start = groups * span
    head_width = pool.shape[2] // lam.shape[0]
    value_width = head_width - 2 * KEY
    width = held.shape[1]
    heads = width // head_width
    columns = pl.ds(low * head_width, width)

    for g in range(groups):

        @pl.loop(0, prompt_pages)
        def _(j):
            at = pl.multiple_of(g * span + j * page, page)
            pltpu.make_async_copy(pool.at[prompt_table[g, j], :, columns], held.at[pl.ds(at, page)], sems.at[0]).start()

    @pl.loop(0, reqs)
    def _(r):
        for j in range(cont_pages):
            at = pl.multiple_of(start + r * own + j * page, page)
            pltpu.make_async_copy(pool.at[cont_table[j, r], :, columns], held.at[pl.ds(at, page)], sems.at[0]).start()

    rows = pl.ds(low * value_width, weight_held.shape[0])
    weight_copy = pltpu.make_async_copy(weight.at[rows], weight_held, sems.at[1])
    weight_copy.start()

    group_of = column(req_group, reqs)
    length_of = column(cont_len, reqs)
    biases = []
    pos = lax.broadcasted_iota(jnp.int32, (reqs, span), 1)
    for g in range(groups):
        live = (group_of == g) & (pos < prompt_len[g])
        biases.append(jnp.where(live, 0.0, -1e30))
    key = lax.broadcasted_iota(jnp.int32, (reqs, reqs * own), 1)
    pos = key - own * lax.broadcasted_iota(jnp.int32, (reqs, reqs * own), 0)
    biases.append(jnp.where((pos >= 0) & (pos < length_of), 0.0, -1e30))
    live = jnp.concatenate(biases, axis=1) == 0.0

    pltpu.make_async_copy(held, held, sems.at[0]).wait()

    scale = KEY**-0.5
    mixed = []
    for h in range(heads):
        first = h * head_width
        weights, new_weights = [], []
        for i in range(2):
            q = query[:, pl.ds((2 * (low + h) + i) * KEY, KEY)]
            cols = pl.ds(first + i * KEY, KEY)
            new_cols = pl.ds(low * head_width + first + i * KEY, KEY)
            score = lax.dot_general(
                q, held[:, cols], (((1,), (1,)), ((), ())), preferred_element_type=jnp.float32
            )
            score = jnp.where(live, score * scale, -1e30)
            new = jnp.sum(q.astype(jnp.float32) * new_ref[:, new_cols].astype(jnp.float32), axis=1, keepdims=True) * scale
            top = jnp.maximum(jnp.max(score, axis=1, keepdims=True), new)
            score = jnp.exp(score - top)
            new = jnp.exp(new - top)
            inverse = 1.0 / (jnp.sum(score, axis=1, keepdims=True) + new)
            weights.append((score * inverse).astype(jnp.bfloat16))
            new_weights.append((new * inverse).astype(jnp.bfloat16).astype(jnp.float32))
        cols = pl.ds(first + 2 * KEY, value_width)
        mixture = jnp.dot(jnp.concatenate(weights, axis=0), held[:, cols], preferred_element_type=jnp.float32)
        new_value = new_ref[:, pl.ds(low * head_width + first + 2 * KEY, value_width)].astype(jnp.float32)
        one = mixture[:reqs] + new_weights[0] * new_value
        two = mixture[reqs:] + new_weights[1] * new_value
        diff = one - lam[low + h] * two
        norm = lax.rsqrt(jnp.mean(diff * diff, axis=1, keepdims=True) + 1e-05)
        mixed.append((diff * norm * 0.8).astype(jnp.bfloat16))
    weight_copy.wait()
    mixed = jnp.concatenate(mixed, axis=1)
    product = jnp.dot(mixed, weight_held[...], preferred_element_type=jnp.float32)
    for part in prior:
        product = product + part[...]
    out[...] = product.astype(out.dtype)


def attention(query, new_kv, pool, prompt_table, prompt_len, req_group, cont_table, cont_len, lam, weight, low, high, prior):
    reqs = query.shape[0]
    page = pool.shape[1]
    heads = lam.shape[0]
    keys = (prompt_table.size + cont_table.size) * page
    width = pool.shape[2] // heads * (high - low)
    rows = weight.shape[0] // heads * (high - low)
    return pl.pallas_call(
        functools.partial(attention_kernel, low),
        out_shape=jax.ShapeDtypeStruct((reqs, weight.shape[1]), jnp.bfloat16 if high == heads else jnp.float32),
        in_specs=[SMEM] * 6 + [VMEM] * (2 + len(prior)) + [HBM, HBM],
        out_specs=VMEM,
        scratch_shapes=[
            pltpu.VMEM((keys, width), pool.dtype),
            pltpu.VMEM((rows, weight.shape[1]), weight.dtype),
            pltpu.SemaphoreType.DMA((2,)),
        ],
        compiler_params=pltpu.CompilerParams(vmem_limit_bytes=VMEM_BYTES),
        cost_estimate=pl.CostEstimate(
            flops=4 * reqs * keys * width + 2 * reqs * rows * weight.shape[1],
            bytes_accessed=2 * (keys * width + rows * weight.shape[1]),
            transcendentals=reqs * keys * 2 * (high - low),
        ),
        name="attention",
    )(prompt_table, prompt_len, req_group, cont_table, cont_len, lam, query, new_kv, *prior, *pinned(weight, pool))


def finish_kernel(count, hidden, gain, *refs):
    parts = refs[:count]
    hidden_out, normed_out = refs[count:]
    total = parts[0][...].astype(jnp.float32)
    for part in parts[1:]:
        total = total + part[...].astype(jnp.float32)
    summed = hidden[...].astype(jnp.float32) + total
    norm = lax.rsqrt(jnp.mean(summed * summed, axis=1, keepdims=True) + 1e-05)
    hidden_out[...] = summed.astype(hidden_out.dtype)
    normed_out[...] = (summed * norm * gain[...]).astype(normed_out.dtype)


def finish(hidden, gain, parts):
    shape = jax.ShapeDtypeStruct(hidden.shape, jnp.bfloat16)
    return pl.pallas_call(
        functools.partial(finish_kernel, len(parts)),
        out_shape=[shape, shape],
        in_specs=[VMEM] * (2 + len(parts)),
        out_specs=[VMEM, VMEM],
        compiler_params=pltpu.CompilerParams(vmem_limit_bytes=SMALL_VMEM_BYTES),
        name="finish",
    )(hidden, gain.reshape(1, -1), *parts)


def gather_kernel(choose, count, *refs):
    parts, out, sems = refs[:count], refs[-2], refs[-1]
    copies = [
        (pltpu.make_async_copy(parts[part], out.at[pl.ds(place, MIG_CAP)], sems.at[n]), taken)
        for n, (place, part, taken) in enumerate(choose())
    ]
    for copy, taken in copies:
        pl.when(taken)(copy.start)
    for copy, taken in copies:
        pl.when(taken)(copy.wait)


def arrive(parts, choose, rest=None):
    slots = MIG_REACH * MIG_CAP
    extra = [] if rest is None else pinned(rest)
    return pl.pallas_call(
        functools.partial(gather_kernel, choose, len(parts)),
        out_shape=jax.ShapeDtypeStruct((slots,) + parts[0].shape[1:], parts[0].dtype),
        in_specs=[VMEM] * len(parts) + [HBM] * len(extra),
        out_specs=HBM,
        scratch_shapes=[pltpu.SemaphoreType.DMA((2 * MIG_REACH,))],
        input_output_aliases={len(parts): 0} if extra else {},
        compiler_params=pltpu.CompilerParams(vmem_limit_bytes=SMALL_VMEM_BYTES),
        name="arrive",
    )(*parts, *extra)


def routed(value, targets):
    count, width = lax.axis_size("req"), lax.axis_size("tp")
    pairs = []
    for s in range(count):
        for t in range(width):
            target = targets(s, t % 2)
            if target is not None:
                pairs.append((s * width + t, target % count * width + t))
    return lax.ppermute(value, ("req", "tp"), pairs)


def turn(s, steps):
    return s - s % MIG_REACH + (s + steps) % MIG_REACH


def route_first(s, odd):
    if not odd:
        return turn(s, 2)
    return turn(s, 3) if s % 2 else s + 1


def route_second(s, odd):
    if odd:
        return turn(s, 2)
    return None if s % 2 else s + 1


def route_three(s, odd):
    return s + 3 if s % 2 and not odd else None


def route_late(s, odd):
    return s + 1 if s % 2 else s + 3


def lift_first(s, odd):
    return s + MIG_REACH if s % MIG_REACH in ((0, 2) if odd else (0, 1)) else None


def lift_second(s, odd):
    return s + MIG_REACH if odd and s % MIG_REACH < 2 else None


def choose_straight():
    return [(n * MIG_CAP, n, True) for n in range(MIG_REACH)]


def where_am_i():
    col = lax.rem(lax.axis_index("req"), MIG_REACH)
    odd = lax.rem(col, 2) == 1
    odd_core = lax.rem(lax.axis_index("tp"), 2) == 1
    return odd, jnp.logical_not(odd), odd_core, jnp.logical_not(odd_core), col < 2, col >= 2


def choose_sooner():
    odd, even, odd_core, even_core, low, high = where_am_i()
    return [
        (0, 1, odd & even_core),
        (0, 0, odd & odd_core),
        (2, 0, high & even_core),
        (2, 2, low & even_core),
        (2, 1, high & odd_core),
        (4, 3, even & even_core),
        (4, 2, even & odd_core),
        (6, 4, True),
    ]


def choose_later():
    odd, even, odd_core, even_core, low, high = where_am_i()
    return [(0, 1, even), (2, 0, low & odd_core), (4, 1, odd)]


def can_relay():
    count = lax.axis_size("req")
    return MIG_REACH == 4 and count % MIG_REACH == 0 and count > MIG_REACH and lax.axis_size("tp") % 2 == 0


def shards(
    hidden_in,
    query,
    new_kv,
    pool_cache,
    prompt_table,
    prompt_len,
    req_group,
    cont_table,
    cont_len,
    migration,
    diff_lambda,
    out_weight,
    norm_gain,
):
    cont_table, migration = cont_table.T, migration.T
    heads = diff_lambda.shape[0]
    few = heads // 4
    attend = functools.partial(
        attention, query, new_kv, pool_cache, prompt_table, prompt_len, req_group, cont_table, cont_len, diff_lambda, out_weight
    )
    send = (cont_table, cont_len, migration, new_kv, pool_cache)
    prior = [attend(0, few, [])] if few else []
    if can_relay():
        first, four, second = send_slots((((2, 1), (2, 3)), ((4, 4), (4, 4)), ((1, 2), (3, 2))), *send)
        first = routed(first, route_first)
        four = shifted(four, "req", 4)
        three = routed(second, route_three)
        second = routed(second, route_second)
        prior, first = lax.optimization_barrier((prior, first))
        first_up = routed(first, lift_first)
        first, cont_len_late = lax.optimization_barrier((first, cont_len))
        (late,) = send_slots((((3, 3), (1, 1)),), cont_table, cont_len_late, *send[2:])
        late, second = lax.optimization_barrier((late, second))
        second_up = routed(second, lift_second)
        prior, second, late = lax.optimization_barrier((prior, second, late))
        late = routed(late, route_late)
    else:
        outgoing = send_slots(tuple(((o, o), (o, o)) for o in range(1, MIG_REACH + 1)), *send)
        arrived = arrive([shifted(part, "req", o + 1) for o, part in enumerate(outgoing)], choose_straight)
    partial = attend(few, heads, prior)
    if can_relay():
        partial, four = lax.optimization_barrier((partial, four))
        sooner = arrive((first, second, first_up, three, four), choose_sooner)
        arrived = arrive((second_up, late), choose_later, sooner)
    if lax.axis_size("tp") == 2:
        parts = [partial, shifted(partial, "tp", 1)]
    else:
        parts = [lax.psum(partial, "tp")]
    hidden_out, normed_out = finish(hidden_in, norm_gain, parts)
    return (hidden_out, normed_out, arrived)


def solution(mesh):
    placed = (
        P("req", None),
        P("req", "tp"),
        P("req", "tp"),
        P("req", None, "tp"),
        P("req", None),
        P("req"),
        P("req"),
        P("req", None),
        P("req"),
        P("req", None),
        P("tp"),
        P("tp", None),
        P(),
    )
    return jax.shard_map(
        shards,
        mesh=mesh,
        in_specs=placed,
        out_specs=(P("req", None), P("req", None), P("req", None, "tp")),
        check_vma=False,
    )
```

```python
import functools

import jax
import jax.numpy as jnp
from jax import lax
from jax.experimental import pallas as pl
from jax.experimental.pallas import tpu as pltpu
from jax.sharding import PartitionSpec as P

MIG_REACH = 4
MIG_CAP = 2
KEY = 128
ROWS = 16

SMEM = pl.BlockSpec(memory_space=pltpu.SMEM)
VMEM = pl.BlockSpec(memory_space=pltpu.VMEM)
HBM = pl.BlockSpec(memory_space=pltpu.HBM)
VMEM_BYTES = 40 * 1024 * 1024
SMALL_VMEM_BYTES = 8 * 1024 * 1024


def pinned(*arrays):
    return [pltpu.with_memory_space_constraint(array, pltpu.HBM) for array in arrays]


def shifted(value, axis, steps):
    count = lax.axis_size(axis)
    pairs = [(source, (source + steps) % count) for source in range(count)]
    return lax.ppermute(value, axis, pairs)


def send_kernel(offsets, table_in, length_in, migration_in, new_in, pool, *refs):
    outs = refs[:MIG_REACH]
    table, length, migration, holder, new_held, new_rows, sems, small_sems = refs[MIG_REACH:]
    small = [
        pltpu.make_async_copy(source, target, small_sems.at[n])
        for n, (source, target) in enumerate(
            zip((table_in, length_in, migration_in, new_in), (table, length, migration, new_held))
        )
    ]
    for copy in small:
        copy.start()
    for copy in small[:3]:
        copy.wait()
    entries = migration.shape[1]
    pages, page = table.shape[0], pool.shape[1]
    for place in range(MIG_REACH * MIG_CAP):
        holder[place] = -1
    odd = lax.rem(lax.axis_index("req"), 2)
    where = []
    for n, (on_even, on_odd) in enumerate(offsets):
        offset = on_even + odd * (on_odd - on_even)
        for i in range(MIG_CAP):
            where.append((n * MIG_CAP + i, (offset - 1) * MIG_CAP + i, outs[n].at[i]))
    for e in range(entries):
        rank = jnp.int32(0)
        for before in range(e):
            rank += (migration[1, before] == migration[1, e]).astype(jnp.int32)
        holder[(migration[1, e] - 1) * MIG_CAP + rank] = migration[0, e]

    def page_copy(n, place, out, j):
        slot = jnp.maximum(holder[place], 0)
        return pltpu.make_async_copy(pool.at[table[j, slot]], out.at[pl.ds(j * page, page)], sems.at[n, j])

    def used(place, j):
        slot = holder[place]
        return (slot >= 0) & (length[jnp.maximum(slot, 0)] >= j * page)

    for n, place, out in where:
        for j in range(pages):

            @pl.when(used(place, j))
            def _():
                page_copy(n, place, out, j).start()

    small[3].wait()
    new_rows[...] = new_held[...].astype(jnp.float32)
    for n, place, out in where:
        slot = holder[place]
        safe = jnp.maximum(slot, 0)
        last = jnp.where(slot >= 0, length[safe], -1)
        for j in range(pages):

            @pl.when(used(place, j))
            def _():
                page_copy(n, place, out, j).wait()

            for low in range(j * page, (j + 1) * page, ROWS):

                @pl.when(last < low)
                def _():
                    out[pl.ds(low, ROWS)] = jnp.zeros((ROWS, out.shape[1]), out.dtype)

                @pl.when((last >= low) & (last < low + ROWS))
                def _():
                    held = out[pl.ds(low, ROWS)].astype(jnp.float32)
                    pos = low + lax.broadcasted_iota(jnp.int32, held.shape, 0)
                    new = jnp.where(pos == last, new_rows[pl.ds(safe, 1)], 0.0)
                    out[pl.ds(low, ROWS)] = jnp.where(pos < last, held, new).astype(out.dtype)


def send_slots(offsets, cont_table, cont_len, migration, new_kv, pool):
    span = cont_table.shape[0] * pool.shape[1]
    width = pool.shape[2]
    return pl.pallas_call(
        functools.partial(send_kernel, offsets),
        out_shape=[jax.ShapeDtypeStruct((MIG_CAP, span, width), pool.dtype)] * MIG_REACH,
        in_specs=[HBM] * 5,
        out_specs=[VMEM] * MIG_REACH,
        scratch_shapes=[
            pltpu.SMEM(cont_table.shape, jnp.int32),
            pltpu.SMEM(cont_len.shape, jnp.int32),
            pltpu.SMEM(migration.shape, jnp.int32),
            pltpu.SMEM((MIG_REACH * MIG_CAP,), jnp.int32),
            pltpu.VMEM(new_kv.shape, new_kv.dtype),
            pltpu.VMEM(new_kv.shape, jnp.float32),
            pltpu.SemaphoreType.DMA((MIG_REACH * MIG_CAP, cont_table.shape[0])),
            pltpu.SemaphoreType.DMA((4,)),
        ],
        compiler_params=pltpu.CompilerParams(vmem_limit_bytes=VMEM_BYTES),
        name="send_slots",
    )(*pinned(cont_table, cont_len, migration, new_kv, pool))


def column(values, count):
    rows = lax.broadcasted_iota(jnp.int32, (count, 1), 0)
    out = jnp.zeros((count, 1), jnp.int32)
    for r in range(count):
        out = jnp.where(rows == r, values[r], out)
    return out


def attention_kernel(low, prompt_table, prompt_len, req_group, cont_table, cont_len, lam, query, new_ref, *refs):
    prior = refs[:-6]
    weight, pool, out, held, weight_held, sems = refs[-6:]
    groups, prompt_pages = prompt_table.shape
    cont_pages, reqs = cont_table.shape
    page = pool.shape[1]
    span = prompt_pages * page
    own = cont_pages * page
    start = groups * span
    head_width = pool.shape[2] // lam.shape[0]
    value_width = head_width - 2 * KEY
    width = held.shape[1]
    heads = width // head_width
    columns = pl.ds(low * head_width, width)

    for g in range(groups):

        @pl.loop(0, prompt_pages)
        def _(j):
            at = pl.multiple_of(g * span + j * page, page)
            pltpu.make_async_copy(pool.at[prompt_table[g, j], :, columns], held.at[pl.ds(at, page)], sems.at[0]).start()

    @pl.loop(0, reqs)
    def _(r):
        for j in range(cont_pages):
            at = pl.multiple_of(start + r * own + j * page, page)
            pltpu.make_async_copy(pool.at[cont_table[j, r], :, columns], held.at[pl.ds(at, page)], sems.at[0]).start()

    rows = pl.ds(low * value_width, weight_held.shape[0])
    weight_copy = pltpu.make_async_copy(weight.at[rows], weight_held, sems.at[1])
    weight_copy.start()

    group_of = column(req_group, reqs)
    length_of = column(cont_len, reqs)
    biases = []
    pos = lax.broadcasted_iota(jnp.int32, (reqs, span), 1)
    for g in range(groups):
        live = (group_of == g) & (pos < prompt_len[g])
        biases.append(jnp.where(live, 0.0, -1e30))
    key = lax.broadcasted_iota(jnp.int32, (reqs, reqs * own), 1)
    pos = key - own * lax.broadcasted_iota(jnp.int32, (reqs, reqs * own), 0)
    biases.append(jnp.where((pos >= 0) & (pos < length_of), 0.0, -1e30))
    live = jnp.concatenate(biases, axis=1) == 0.0

    pltpu.make_async_copy(held, held, sems.at[0]).wait()

    scale = KEY**-0.5
    mixed = []
    for h in range(heads):
        first = h * head_width
        weights, new_weights = [], []
        for i in range(2):
            q = query[:, pl.ds((2 * (low + h) + i) * KEY, KEY)]
            cols = pl.ds(first + i * KEY, KEY)
            new_cols = pl.ds(low * head_width + first + i * KEY, KEY)
            score = lax.dot_general(
                q, held[:, cols], (((1,), (1,)), ((), ())), preferred_element_type=jnp.float32
            )
            score = jnp.where(live, score * scale, -1e30)
            new = jnp.sum(q.astype(jnp.float32) * new_ref[:, new_cols].astype(jnp.float32), axis=1, keepdims=True) * scale
            top = jnp.maximum(jnp.max(score, axis=1, keepdims=True), new)
            score = jnp.exp(score - top)
            new = jnp.exp(new - top)
            inverse = 1.0 / (jnp.sum(score, axis=1, keepdims=True) + new)
            weights.append((score * inverse).astype(jnp.bfloat16))
            new_weights.append((new * inverse).astype(jnp.bfloat16).astype(jnp.float32))
        cols = pl.ds(first + 2 * KEY, value_width)
        mixture = jnp.dot(jnp.concatenate(weights, axis=0), held[:, cols], preferred_element_type=jnp.float32)
        new_value = new_ref[:, pl.ds(low * head_width + first + 2 * KEY, value_width)].astype(jnp.float32)
        one = mixture[:reqs] + new_weights[0] * new_value
        two = mixture[reqs:] + new_weights[1] * new_value
        diff = one - lam[low + h] * two
        norm = lax.rsqrt(jnp.mean(diff * diff, axis=1, keepdims=True) + 1e-05)
        mixed.append((diff * norm * 0.8).astype(jnp.bfloat16))
    weight_copy.wait()
    mixed = jnp.concatenate(mixed, axis=1)
    product = jnp.dot(mixed, weight_held[...], preferred_element_type=jnp.float32)
    for part in prior:
        product = product + part[...]
    out[...] = product.astype(out.dtype)


def attention(query, new_kv, pool, prompt_table, prompt_len, req_group, cont_table, cont_len, lam, weight, low, high, prior):
    reqs = query.shape[0]
    page = pool.shape[1]
    heads = lam.shape[0]
    keys = (prompt_table.size + cont_table.size) * page
    width = pool.shape[2] // heads * (high - low)
    rows = weight.shape[0] // heads * (high - low)
    return pl.pallas_call(
        functools.partial(attention_kernel, low),
        out_shape=jax.ShapeDtypeStruct((reqs, weight.shape[1]), jnp.bfloat16 if high == heads else jnp.float32),
        in_specs=[SMEM] * 6 + [VMEM] * (2 + len(prior)) + [HBM, HBM],
        out_specs=VMEM,
        scratch_shapes=[
            pltpu.VMEM((keys, width), pool.dtype),
            pltpu.VMEM((rows, weight.shape[1]), weight.dtype),
            pltpu.SemaphoreType.DMA((2,)),
        ],
        compiler_params=pltpu.CompilerParams(vmem_limit_bytes=VMEM_BYTES),
        cost_estimate=pl.CostEstimate(
            flops=4 * reqs * keys * width + 2 * reqs * rows * weight.shape[1],
            bytes_accessed=2 * (keys * width + rows * weight.shape[1]),
            transcendentals=reqs * keys * 2 * (high - low),
        ),
        name="attention",
    )(prompt_table, prompt_len, req_group, cont_table, cont_len, lam, query, new_kv, *prior, *pinned(weight, pool))


def finish_kernel(count, hidden, gain, *refs):
    parts = refs[:count]
    hidden_out, normed_out = refs[count:]
    total = parts[0][...].astype(jnp.float32)
    for part in parts[1:]:
        total = total + part[...].astype(jnp.float32)
    summed = hidden[...].astype(jnp.float32) + total
    norm = lax.rsqrt(jnp.mean(summed * summed, axis=1, keepdims=True) + 1e-05)
    hidden_out[...] = summed.astype(hidden_out.dtype)
    normed_out[...] = (summed * norm * gain[...]).astype(normed_out.dtype)


def finish(hidden, gain, parts):
    shape = jax.ShapeDtypeStruct(hidden.shape, jnp.bfloat16)
    return pl.pallas_call(
        functools.partial(finish_kernel, len(parts)),
        out_shape=[shape, shape],
        in_specs=[VMEM] * (2 + len(parts)),
        out_specs=[VMEM, VMEM],
        compiler_params=pltpu.CompilerParams(vmem_limit_bytes=SMALL_VMEM_BYTES),
        name="finish",
    )(hidden, gain.reshape(1, -1), *parts)


def gather_kernel(choose, *refs):
    parts, out, sems = refs[:-2], refs[-2], refs[-1]
    for n, (place, options) in enumerate(choose()):
        target = out.at[pl.ds(place, MIG_CAP)]
        for part, taken in options:
            copy = pltpu.make_async_copy(parts[part], target, sems.at[n])
            if taken is None:
                copy.start()
            else:
                pl.when(taken)(copy.start)
    for n in range(MIG_REACH):
        pltpu.make_async_copy(parts[0], out.at[pl.ds(n * MIG_CAP, MIG_CAP)], sems.at[n]).wait()


def arrive(parts, choose):
    slots = MIG_REACH * MIG_CAP
    return pl.pallas_call(
        functools.partial(gather_kernel, choose),
        out_shape=jax.ShapeDtypeStruct((slots,) + parts[0].shape[1:], parts[0].dtype),
        in_specs=[VMEM] * len(parts),
        out_specs=HBM,
        scratch_shapes=[pltpu.SemaphoreType.DMA((MIG_REACH,))],
        compiler_params=pltpu.CompilerParams(vmem_limit_bytes=SMALL_VMEM_BYTES),
        name="arrive",
    )(*parts)


def routed(value, targets):
    count, width = lax.axis_size("req"), lax.axis_size("tp")
    pairs = []
    for s in range(count):
        for t in range(width):
            target = targets(s, t % 2) % count
            pairs.append((s * width + t, target * width + (t ^ 1 if target == s else t)))
    return lax.ppermute(value, ("req", "tp"), pairs)


def turn(s, steps):
    return s - s % MIG_REACH + (s + steps) % MIG_REACH


def route_early(s, odd):
    if s % 2 == 0:
        return s + 1
    return turn(s, 3) if odd else s + 3


def route_late(s, odd):
    return s + 3 if s % 2 == 0 else s + 1


def lift_two(s, odd):
    return s + MIG_REACH if s % MIG_REACH < 2 else s


def lift_early(s, odd):
    if s % 2:
        return s
    return s + MIG_REACH if odd else turn(s, 2)


def choose_straight():
    return [(n * MIG_CAP, [(n, None)]) for n in range(MIG_REACH)]


def choose_relayed():
    col = lax.rem(lax.axis_index("req"), MIG_REACH)
    odd_core = lax.rem(lax.axis_index("tp"), 2) == 1
    odd = lax.rem(col, 2) == 1
    even = jnp.logical_not(odd)
    return [
        (0, [(2, odd), (4, even)]),
        (2, [(0, col >= 2), (1, col < 2)]),
        (4, [(4, odd), (2, even & jnp.logical_not(odd_core)), (3, even & odd_core)]),
        (6, [(5, None)]),
    ]


def can_relay():
    count = lax.axis_size("req")
    return MIG_REACH == 4 and count % MIG_REACH == 0 and count > MIG_REACH and lax.axis_size("tp") % 2 == 0


def shards(
    hidden_in,
    query,
    new_kv,
    pool_cache,
    prompt_table,
    prompt_len,
    req_group,
    cont_table,
    cont_len,
    migration,
    diff_lambda,
    out_weight,
    norm_gain,
):
    cont_table, migration = cont_table.T, migration.T
    heads = diff_lambda.shape[0]
    half = heads // 2
    attend = functools.partial(
        attention, query, new_kv, pool_cache, prompt_table, prompt_len, req_group, cont_table, cont_len, diff_lambda, out_weight
    )
    send = (cont_table, cont_len, migration, new_kv, pool_cache)
    prior = [attend(0, half, [])] if half else []
    if can_relay():
        two, four, early, late = send_slots(((2, 2), (4, 4), (1, 3), (3, 1)), *send)
        two = routed(two, lambda s, odd: turn(s, 2))
        four = shifted(four, "req", 4)
        early = routed(early, route_early)
        prior, two = lax.optimization_barrier((prior, two))
        two_up = routed(two, lift_two)
        two, late = lax.optimization_barrier((two, late))
        late = routed(late, route_late)
        early_up = routed(early, lift_early)
        received, choose = (two, two_up, early, early_up, late, four), choose_relayed
    else:
        outgoing = send_slots(tuple((o, o) for o in range(1, MIG_REACH + 1)), *send)
        received = [shifted(part, "req", o + 1) for o, part in enumerate(outgoing)]
        choose = choose_straight
    partial = attend(half, heads, prior)
    if lax.axis_size("tp") == 2:
        parts = [partial, shifted(partial, "tp", 1)]
    else:
        parts = [lax.psum(partial, "tp")]
    hidden_out, normed_out = finish(hidden_in, norm_gain, parts)
    arrived = arrive(received, choose)
    return (hidden_out, normed_out, arrived)


def solution(mesh):
    placed = (
        P("req", None),
        P("req", "tp"),
        P("req", "tp"),
        P("req", None, "tp"),
        P("req", None),
        P("req"),
        P("req"),
        P("req", None),
        P("req"),
        P("req", None),
        P("tp"),
        P("tp", None),
        P(),
    )
    return jax.shard_map(
        shards,
        mesh=mesh,
        in_specs=placed,
        out_specs=(P("req", None), P("req", None), P("req", None, "tp")),
        check_vma=False,
    )
```

```python
import functools

import jax
import jax.numpy as jnp
from jax import lax
from jax.experimental import pallas as pl
from jax.experimental.pallas import tpu as pltpu
from jax.sharding import PartitionSpec as P

MIG_REACH = 4
MIG_CAP = 2
KEY = 128
ROWS = 16

SMEM = pl.BlockSpec(memory_space=pltpu.SMEM)
VMEM = pl.BlockSpec(memory_space=pltpu.VMEM)
HBM = pl.BlockSpec(memory_space=pltpu.HBM)
VMEM_BYTES = 40 * 1024 * 1024
SMALL_VMEM_BYTES = 8 * 1024 * 1024


def pinned(*arrays):
    return [pltpu.with_memory_space_constraint(array, pltpu.HBM) for array in arrays]


def shifted(value, axis, steps):
    count = lax.axis_size(axis)
    pairs = [(source, (source + steps) % count) for source in range(count)]
    return lax.ppermute(value, axis, pairs)


def send_kernel(offsets, table_in, length_in, migration_in, new_in, pool, *refs):
    outs = refs[:MIG_REACH]
    table, length, migration, holder, new_held, new_rows, sems, small_sems = refs[MIG_REACH:]
    small = [
        pltpu.make_async_copy(source, target, small_sems.at[n])
        for n, (source, target) in enumerate(
            zip((table_in, length_in, migration_in, new_in), (table, length, migration, new_held))
        )
    ]
    for copy in small:
        copy.start()
    for copy in small[:3]:
        copy.wait()
    entries = migration.shape[1]
    pages, page = table.shape[0], pool.shape[1]
    for place in range(MIG_REACH * MIG_CAP):
        holder[place] = -1
    odd = lax.rem(lax.axis_index("req"), 2)
    where = []
    for n, (on_even, on_odd) in enumerate(offsets):
        offset = on_even + odd * (on_odd - on_even)
        for i in range(MIG_CAP):
            where.append((n * MIG_CAP + i, (offset - 1) * MIG_CAP + i, outs[n].at[i]))
    for e in range(entries):
        rank = jnp.int32(0)
        for before in range(e):
            rank += (migration[1, before] == migration[1, e]).astype(jnp.int32)
        holder[(migration[1, e] - 1) * MIG_CAP + rank] = migration[0, e]

    def page_copy(n, place, out, j):
        slot = jnp.maximum(holder[place], 0)
        return pltpu.make_async_copy(pool.at[table[j, slot]], out.at[pl.ds(j * page, page)], sems.at[n, j])

    def used(place, j):
        slot = holder[place]
        return (slot >= 0) & (length[jnp.maximum(slot, 0)] >= j * page)

    for n, place, out in where:
        for j in range(pages):

            @pl.when(used(place, j))
            def _():
                page_copy(n, place, out, j).start()

    small[3].wait()
    new_rows[...] = new_held[...].astype(jnp.float32)
    for n, place, out in where:
        slot = holder[place]
        safe = jnp.maximum(slot, 0)
        last = jnp.where(slot >= 0, length[safe], -1)
        for j in range(pages):

            @pl.when(used(place, j))
            def _():
                page_copy(n, place, out, j).wait()

            for low in range(j * page, (j + 1) * page, ROWS):

                @pl.when(last < low)
                def _():
                    out[pl.ds(low, ROWS)] = jnp.zeros((ROWS, out.shape[1]), out.dtype)

                @pl.when((last >= low) & (last < low + ROWS))
                def _():
                    held = out[pl.ds(low, ROWS)].astype(jnp.float32)
                    pos = low + lax.broadcasted_iota(jnp.int32, held.shape, 0)
                    new = jnp.where(pos == last, new_rows[pl.ds(safe, 1)], 0.0)
                    out[pl.ds(low, ROWS)] = jnp.where(pos < last, held, new).astype(out.dtype)


def send_slots(offsets, cont_table, cont_len, migration, new_kv, pool):
    span = cont_table.shape[0] * pool.shape[1]
    width = pool.shape[2]
    return pl.pallas_call(
        functools.partial(send_kernel, offsets),
        out_shape=[jax.ShapeDtypeStruct((MIG_CAP, span, width), pool.dtype)] * MIG_REACH,
        in_specs=[HBM] * 5,
        out_specs=[VMEM] * MIG_REACH,
        scratch_shapes=[
            pltpu.SMEM(cont_table.shape, jnp.int32),
            pltpu.SMEM(cont_len.shape, jnp.int32),
            pltpu.SMEM(migration.shape, jnp.int32),
            pltpu.SMEM((MIG_REACH * MIG_CAP,), jnp.int32),
            pltpu.VMEM(new_kv.shape, new_kv.dtype),
            pltpu.VMEM(new_kv.shape, jnp.float32),
            pltpu.SemaphoreType.DMA((MIG_REACH * MIG_CAP, cont_table.shape[0])),
            pltpu.SemaphoreType.DMA((4,)),
        ],
        compiler_params=pltpu.CompilerParams(vmem_limit_bytes=VMEM_BYTES),
        name="send_slots",
    )(*pinned(cont_table, cont_len, migration, new_kv, pool))


def column(values, count):
    rows = lax.broadcasted_iota(jnp.int32, (count, 1), 0)
    out = jnp.zeros((count, 1), jnp.int32)
    for r in range(count):
        out = jnp.where(rows == r, values[r], out)
    return out


def attention_kernel(low, prompt_table, prompt_len, req_group, cont_table, cont_len, lam, query, new_ref, *refs):
    prior = refs[:-6]
    weight, pool, out, held, weight_held, sems = refs[-6:]
    groups, prompt_pages = prompt_table.shape
    cont_pages, reqs = cont_table.shape
    page = pool.shape[1]
    span = prompt_pages * page
    own = cont_pages * page
    start = groups * span
    head_width = pool.shape[2] // lam.shape[0]
    value_width = head_width - 2 * KEY
    width = held.shape[1]
    heads = width // head_width
    columns = pl.ds(low * head_width, width)

    for g in range(groups):

        @pl.loop(0, prompt_pages)
        def _(j):
            at = pl.multiple_of(g * span + j * page, page)
            pltpu.make_async_copy(pool.at[prompt_table[g, j], :, columns], held.at[pl.ds(at, page)], sems.at[0]).start()

    @pl.loop(0, reqs)
    def _(r):
        for j in range(cont_pages):
            at = pl.multiple_of(start + r * own + j * page, page)
            pltpu.make_async_copy(pool.at[cont_table[j, r], :, columns], held.at[pl.ds(at, page)], sems.at[0]).start()

    rows = pl.ds(low * value_width, weight_held.shape[0])
    weight_copy = pltpu.make_async_copy(weight.at[rows], weight_held, sems.at[1])
    weight_copy.start()

    group_of = column(req_group, reqs)
    length_of = column(cont_len, reqs)
    biases = []
    pos = lax.broadcasted_iota(jnp.int32, (reqs, span), 1)
    for g in range(groups):
        live = (group_of == g) & (pos < prompt_len[g])
        biases.append(jnp.where(live, 0.0, -1e30))
    key = lax.broadcasted_iota(jnp.int32, (reqs, reqs * own), 1)
    pos = key - own * lax.broadcasted_iota(jnp.int32, (reqs, reqs * own), 0)
    biases.append(jnp.where((pos >= 0) & (pos < length_of), 0.0, -1e30))
    live = jnp.concatenate(biases, axis=1) == 0.0

    pltpu.make_async_copy(held, held, sems.at[0]).wait()

    scale = KEY**-0.5
    mixed = []
    for h in range(heads):
        first = h * head_width
        weights, new_weights = [], []
        for i in range(2):
            q = query[:, pl.ds((2 * (low + h) + i) * KEY, KEY)]
            cols = pl.ds(first + i * KEY, KEY)
            new_cols = pl.ds(low * head_width + first + i * KEY, KEY)
            score = lax.dot_general(
                q, held[:, cols], (((1,), (1,)), ((), ())), preferred_element_type=jnp.float32
            )
            score = jnp.where(live, score * scale, -1e30)
            new = jnp.sum(q.astype(jnp.float32) * new_ref[:, new_cols].astype(jnp.float32), axis=1, keepdims=True) * scale
            top = jnp.maximum(jnp.max(score, axis=1, keepdims=True), new)
            score = jnp.exp(score - top)
            new = jnp.exp(new - top)
            inverse = 1.0 / (jnp.sum(score, axis=1, keepdims=True) + new)
            weights.append((score * inverse).astype(jnp.bfloat16))
            new_weights.append((new * inverse).astype(jnp.bfloat16).astype(jnp.float32))
        cols = pl.ds(first + 2 * KEY, value_width)
        mixture = jnp.dot(jnp.concatenate(weights, axis=0), held[:, cols], preferred_element_type=jnp.float32)
        new_value = new_ref[:, pl.ds(low * head_width + first + 2 * KEY, value_width)].astype(jnp.float32)
        one = mixture[:reqs] + new_weights[0] * new_value
        two = mixture[reqs:] + new_weights[1] * new_value
        diff = one - lam[low + h] * two
        norm = lax.rsqrt(jnp.mean(diff * diff, axis=1, keepdims=True) + 1e-05)
        mixed.append((diff * norm * 0.8).astype(jnp.bfloat16))
    weight_copy.wait()
    mixed = jnp.concatenate(mixed, axis=1)
    product = jnp.dot(mixed, weight_held[...], preferred_element_type=jnp.float32)
    for part in prior:
        product = product + part[...]
    out[...] = product.astype(out.dtype)


def attention(query, new_kv, pool, prompt_table, prompt_len, req_group, cont_table, cont_len, lam, weight, low, high, prior):
    reqs = query.shape[0]
    page = pool.shape[1]
    heads = lam.shape[0]
    keys = (prompt_table.size + cont_table.size) * page
    width = pool.shape[2] // heads * (high - low)
    rows = weight.shape[0] // heads * (high - low)
    return pl.pallas_call(
        functools.partial(attention_kernel, low),
        out_shape=jax.ShapeDtypeStruct((reqs, weight.shape[1]), jnp.bfloat16 if high == heads else jnp.float32),
        in_specs=[SMEM] * 6 + [VMEM] * (2 + len(prior)) + [HBM, HBM],
        out_specs=VMEM,
        scratch_shapes=[
            pltpu.VMEM((keys, width), pool.dtype),
            pltpu.VMEM((rows, weight.shape[1]), weight.dtype),
            pltpu.SemaphoreType.DMA((2,)),
        ],
        compiler_params=pltpu.CompilerParams(vmem_limit_bytes=VMEM_BYTES),
        cost_estimate=pl.CostEstimate(
            flops=4 * reqs * keys * width + 2 * reqs * rows * weight.shape[1],
            bytes_accessed=2 * (keys * width + rows * weight.shape[1]),
            transcendentals=reqs * keys * 2 * (high - low),
        ),
        name="attention",
    )(prompt_table, prompt_len, req_group, cont_table, cont_len, lam, query, new_kv, *prior, *pinned(weight, pool))


def finish_kernel(count, hidden, gain, *refs):
    parts = refs[:count]
    hidden_out, normed_out = refs[count:]
    total = parts[0][...].astype(jnp.float32)
    for part in parts[1:]:
        total = total + part[...].astype(jnp.float32)
    summed = hidden[...].astype(jnp.float32) + total
    norm = lax.rsqrt(jnp.mean(summed * summed, axis=1, keepdims=True) + 1e-05)
    hidden_out[...] = summed.astype(hidden_out.dtype)
    normed_out[...] = (summed * norm * gain[...]).astype(normed_out.dtype)


def finish(hidden, gain, parts):
    shape = jax.ShapeDtypeStruct(hidden.shape, jnp.bfloat16)
    return pl.pallas_call(
        functools.partial(finish_kernel, len(parts)),
        out_shape=[shape, shape],
        in_specs=[VMEM] * (2 + len(parts)),
        out_specs=[VMEM, VMEM],
        compiler_params=pltpu.CompilerParams(vmem_limit_bytes=SMALL_VMEM_BYTES),
        name="finish",
    )(hidden, gain.reshape(1, -1), *parts)


def gather_kernel(choose, *refs):
    parts, out, sems = refs[:-2], refs[-2], refs[-1]
    for n, (place, options) in enumerate(choose()):
        target = out.at[pl.ds(place, MIG_CAP)]
        for part, taken in options:
            copy = pltpu.make_async_copy(parts[part], target, sems.at[n])
            if taken is None:
                copy.start()
            else:
                pl.when(taken)(copy.start)
    for n in range(MIG_REACH):
        pltpu.make_async_copy(parts[0], out.at[pl.ds(n * MIG_CAP, MIG_CAP)], sems.at[n]).wait()


def arrive(parts, choose):
    slots = MIG_REACH * MIG_CAP
    return pl.pallas_call(
        functools.partial(gather_kernel, choose),
        out_shape=jax.ShapeDtypeStruct((slots,) + parts[0].shape[1:], parts[0].dtype),
        in_specs=[VMEM] * len(parts),
        out_specs=HBM,
        scratch_shapes=[pltpu.SemaphoreType.DMA((MIG_REACH,))],
        compiler_params=pltpu.CompilerParams(vmem_limit_bytes=SMALL_VMEM_BYTES),
        name="arrive",
    )(*parts)


def routed(value, targets):
    count, width = lax.axis_size("req"), lax.axis_size("tp")
    pairs = []
    for s in range(count):
        for t in range(width):
            target = targets(s, t % 2)
            if target is not None:
                target = target % count
                pairs.append((s * width + t, target * width + (t ^ 1 if target == s else t)))
    return lax.ppermute(value, ("req", "tp"), pairs)


def turn(s, steps):
    return s - s % MIG_REACH + (s + steps) % MIG_REACH


def route_early(s, odd):
    if s % 2 == 0:
        return s + 1
    return turn(s, 3) if odd else s + 3


def route_late(s, odd):
    return s + 3 if s % 2 == 0 else s + 1


def lift_two(s, odd):
    return s + MIG_REACH if s % MIG_REACH < 2 else s


def lift_early(s, odd):
    return s + MIG_REACH if odd and s % 2 == 0 else None


def choose_straight():
    return [(n * MIG_CAP, [(n, None)]) for n in range(MIG_REACH)]


def choose_relayed():
    col = lax.rem(lax.axis_index("req"), MIG_REACH)
    odd_core = lax.rem(lax.axis_index("tp"), 2) == 1
    odd = lax.rem(col, 2) == 1
    even = jnp.logical_not(odd)
    return [
        (0, [(2, odd), (4, even)]),
        (2, [(0, col >= 2), (1, col < 2)]),
        (4, [(4, odd), (2, even & jnp.logical_not(odd_core)), (3, even & odd_core)]),
        (6, [(5, None)]),
    ]


def can_relay():
    count = lax.axis_size("req")
    return MIG_REACH == 4 and count % MIG_REACH == 0 and count > MIG_REACH and lax.axis_size("tp") % 2 == 0


def shards(
    hidden_in,
    query,
    new_kv,
    pool_cache,
    prompt_table,
    prompt_len,
    req_group,
    cont_table,
    cont_len,
    migration,
    diff_lambda,
    out_weight,
    norm_gain,
):
    cont_table, migration = cont_table.T, migration.T
    heads = diff_lambda.shape[0]
    half = heads // 2
    attend = functools.partial(
        attention, query, new_kv, pool_cache, prompt_table, prompt_len, req_group, cont_table, cont_len, diff_lambda, out_weight
    )
    send = (cont_table, cont_len, migration, new_kv, pool_cache)
    prior = [attend(0, half, [])] if half else []
    if can_relay():
        two, four, early, late = send_slots(((2, 2), (4, 4), (1, 3), (3, 1)), *send)
        two = routed(two, lambda s, odd: turn(s, 2))
        four = shifted(four, "req", 4)
        early = routed(early, route_early)
        prior, two = lax.optimization_barrier((prior, two))
        two_up = routed(two, lift_two)
        two, late = lax.optimization_barrier((two, late))
        late = routed(late, route_late)
        early_up = routed(early, lift_early)
        received, choose = (two, two_up, early, early_up, late, four), choose_relayed
    else:
        outgoing = send_slots(tuple((o, o) for o in range(1, MIG_REACH + 1)), *send)
        received = [shifted(part, "req", o + 1) for o, part in enumerate(outgoing)]
        choose = choose_straight
    partial = attend(half, heads, prior)
    if lax.axis_size("tp") == 2:
        parts = [partial, shifted(partial, "tp", 1)]
    else:
        parts = [lax.psum(partial, "tp")]
    hidden_out, normed_out = finish(hidden_in, norm_gain, parts)
    arrived = arrive(received, choose)
    return (hidden_out, normed_out, arrived)


def solution(mesh):
    placed = (
        P("req", None),
        P("req", "tp"),
        P("req", "tp"),
        P("req", None, "tp"),
        P("req", None),
        P("req"),
        P("req"),
        P("req", None),
        P("req"),
        P("req", None),
        P("tp"),
        P("tp", None),
        P(),
    )
    return jax.shard_map(
        shards,
        mesh=mesh,
        in_specs=placed,
        out_specs=(P("req", None), P("req", None), P("req", None, "tp")),
        check_vma=False,
    )
```

```python
import functools

import jax
import jax.numpy as jnp
from jax import lax
from jax.experimental import pallas as pl
from jax.experimental.pallas import tpu as pltpu
from jax.sharding import PartitionSpec as P

MIG_REACH = 4
MIG_CAP = 2
KEY = 128
ROWS = 16

SMEM = pl.BlockSpec(memory_space=pltpu.SMEM)
VMEM = pl.BlockSpec(memory_space=pltpu.VMEM)
HBM = pl.BlockSpec(memory_space=pltpu.HBM)
VMEM_BYTES = 40 * 1024 * 1024
SMALL_VMEM_BYTES = 8 * 1024 * 1024


def pinned(*arrays):
    return [pltpu.with_memory_space_constraint(array, pltpu.HBM) for array in arrays]


def shifted(value, axis, steps):
    count = lax.axis_size(axis)
    pairs = [(source, (source + steps) % count) for source in range(count)]
    return lax.ppermute(value, axis, pairs)


def send_kernel(offsets, table_in, length_in, migration_in, new_in, pool, *refs):
    outs = refs[:MIG_REACH]
    table, length, migration, holder, new_held, new_rows, sems, small_sems = refs[MIG_REACH:]
    small = [
        pltpu.make_async_copy(source, target, small_sems.at[n])
        for n, (source, target) in enumerate(
            zip((table_in, length_in, migration_in, new_in), (table, length, migration, new_held))
        )
    ]
    for copy in small:
        copy.start()
    for copy in small[:3]:
        copy.wait()
    entries = migration.shape[1]
    pages, page = table.shape[0], pool.shape[1]
    for place in range(MIG_REACH * MIG_CAP):
        holder[place] = -1
    odd = lax.rem(lax.axis_index("req"), 2)
    where = []
    for n, (on_even, on_odd) in enumerate(offsets):
        offset = on_even + odd * (on_odd - on_even)
        for i in range(MIG_CAP):
            where.append((n * MIG_CAP + i, (offset - 1) * MIG_CAP + i, outs[n].at[i]))
    for e in range(entries):
        rank = jnp.int32(0)
        for before in range(e):
            rank += (migration[1, before] == migration[1, e]).astype(jnp.int32)
        holder[(migration[1, e] - 1) * MIG_CAP + rank] = migration[0, e]

    def page_copy(n, place, out, j):
        slot = jnp.maximum(holder[place], 0)
        return pltpu.make_async_copy(pool.at[table[j, slot]], out.at[pl.ds(j * page, page)], sems.at[n, j])

    def used(place, j):
        slot = holder[place]
        return (slot >= 0) & (length[jnp.maximum(slot, 0)] >= j * page)

    for n, place, out in where:
        for j in range(pages):

            @pl.when(used(place, j))
            def _():
                page_copy(n, place, out, j).start()

    small[3].wait()
    new_rows[...] = new_held[...].astype(jnp.float32)
    for n, place, out in where:
        slot = holder[place]
        safe = jnp.maximum(slot, 0)
        last = jnp.where(slot >= 0, length[safe], -1)
        for j in range(pages):

            @pl.when(used(place, j))
            def _():
                page_copy(n, place, out, j).wait()

            for low in range(j * page, (j + 1) * page, ROWS):

                @pl.when(last < low)
                def _():
                    out[pl.ds(low, ROWS)] = jnp.zeros((ROWS, out.shape[1]), out.dtype)

                @pl.when((last >= low) & (last < low + ROWS))
                def _():
                    held = out[pl.ds(low, ROWS)].astype(jnp.float32)
                    pos = low + lax.broadcasted_iota(jnp.int32, held.shape, 0)
                    new = jnp.where(pos == last, new_rows[pl.ds(safe, 1)], 0.0)
                    out[pl.ds(low, ROWS)] = jnp.where(pos < last, held, new).astype(out.dtype)


def send_slots(offsets, cont_table, cont_len, migration, new_kv, pool):
    span = cont_table.shape[0] * pool.shape[1]
    width = pool.shape[2]
    return pl.pallas_call(
        functools.partial(send_kernel, offsets),
        out_shape=[jax.ShapeDtypeStruct((MIG_CAP, span, width), pool.dtype)] * MIG_REACH,
        in_specs=[HBM] * 5,
        out_specs=[VMEM] * MIG_REACH,
        scratch_shapes=[
            pltpu.SMEM(cont_table.shape, jnp.int32),
            pltpu.SMEM(cont_len.shape, jnp.int32),
            pltpu.SMEM(migration.shape, jnp.int32),
            pltpu.SMEM((MIG_REACH * MIG_CAP,), jnp.int32),
            pltpu.VMEM(new_kv.shape, new_kv.dtype),
            pltpu.VMEM(new_kv.shape, jnp.float32),
            pltpu.SemaphoreType.DMA((MIG_REACH * MIG_CAP, cont_table.shape[0])),
            pltpu.SemaphoreType.DMA((4,)),
        ],
        compiler_params=pltpu.CompilerParams(vmem_limit_bytes=VMEM_BYTES),
        name="send_slots",
    )(*pinned(cont_table, cont_len, migration, new_kv, pool))


def column(values, count):
    rows = lax.broadcasted_iota(jnp.int32, (count, 1), 0)
    out = jnp.zeros((count, 1), jnp.int32)
    for r in range(count):
        out = jnp.where(rows == r, values[r], out)
    return out


def attention_kernel(low, prompt_table, prompt_len, req_group, cont_table, cont_len, lam, query, new_ref, *refs):
    prior = refs[:-6]
    weight, pool, out, held, weight_held, sems = refs[-6:]
    groups, prompt_pages = prompt_table.shape
    cont_pages, reqs = cont_table.shape
    page = pool.shape[1]
    span = prompt_pages * page
    own = cont_pages * page
    start = groups * span
    head_width = pool.shape[2] // lam.shape[0]
    value_width = head_width - 2 * KEY
    width = held.shape[1]
    heads = width // head_width
    columns = pl.ds(low * head_width, width)

    for g in range(groups):

        @pl.loop(0, prompt_pages)
        def _(j):
            at = pl.multiple_of(g * span + j * page, page)
            pltpu.make_async_copy(pool.at[prompt_table[g, j], :, columns], held.at[pl.ds(at, page)], sems.at[0]).start()

    @pl.loop(0, reqs)
    def _(r):
        for j in range(cont_pages):
            at = pl.multiple_of(start + r * own + j * page, page)
            pltpu.make_async_copy(pool.at[cont_table[j, r], :, columns], held.at[pl.ds(at, page)], sems.at[0]).start()

    rows = pl.ds(low * value_width, weight_held.shape[0])
    weight_copy = pltpu.make_async_copy(weight.at[rows], weight_held, sems.at[1])
    weight_copy.start()

    group_of = column(req_group, reqs)
    length_of = column(cont_len, reqs)
    biases = []
    pos = lax.broadcasted_iota(jnp.int32, (reqs, span), 1)
    for g in range(groups):
        live = (group_of == g) & (pos < prompt_len[g])
        biases.append(jnp.where(live, 0.0, -1e30))
    key = lax.broadcasted_iota(jnp.int32, (reqs, reqs * own), 1)
    pos = key - own * lax.broadcasted_iota(jnp.int32, (reqs, reqs * own), 0)
    biases.append(jnp.where((pos >= 0) & (pos < length_of), 0.0, -1e30))
    live = jnp.concatenate(biases, axis=1) == 0.0

    pltpu.make_async_copy(held, held, sems.at[0]).wait()

    scale = KEY**-0.5
    mixed = []
    for h in range(heads):
        first = h * head_width
        weights, new_weights = [], []
        for i in range(2):
            q = query[:, pl.ds((2 * (low + h) + i) * KEY, KEY)]
            cols = pl.ds(first + i * KEY, KEY)
            new_cols = pl.ds(low * head_width + first + i * KEY, KEY)
            score = lax.dot_general(
                q, held[:, cols], (((1,), (1,)), ((), ())), preferred_element_type=jnp.float32
            )
            score = jnp.where(live, score * scale, -1e30)
            new = jnp.sum(q.astype(jnp.float32) * new_ref[:, new_cols].astype(jnp.float32), axis=1, keepdims=True) * scale
            top = jnp.maximum(jnp.max(score, axis=1, keepdims=True), new)
            score = jnp.exp(score - top)
            new = jnp.exp(new - top)
            inverse = 1.0 / (jnp.sum(score, axis=1, keepdims=True) + new)
            weights.append((score * inverse).astype(jnp.bfloat16))
            new_weights.append((new * inverse).astype(jnp.bfloat16).astype(jnp.float32))
        cols = pl.ds(first + 2 * KEY, value_width)
        mixture = jnp.dot(jnp.concatenate(weights, axis=0), held[:, cols], preferred_element_type=jnp.float32)
        new_value = new_ref[:, pl.ds(low * head_width + first + 2 * KEY, value_width)].astype(jnp.float32)
        one = mixture[:reqs] + new_weights[0] * new_value
        two = mixture[reqs:] + new_weights[1] * new_value
        diff = one - lam[low + h] * two
        norm = lax.rsqrt(jnp.mean(diff * diff, axis=1, keepdims=True) + 1e-05)
        mixed.append((diff * norm * 0.8).astype(jnp.bfloat16))
    weight_copy.wait()
    mixed = jnp.concatenate(mixed, axis=1)
    product = jnp.dot(mixed, weight_held[...], preferred_element_type=jnp.float32)
    for part in prior:
        product = product + part[...]
    out[...] = product.astype(out.dtype)


def attention(query, new_kv, pool, prompt_table, prompt_len, req_group, cont_table, cont_len, lam, weight, low, high, prior):
    reqs = query.shape[0]
    page = pool.shape[1]
    heads = lam.shape[0]
    keys = (prompt_table.size + cont_table.size) * page
    width = pool.shape[2] // heads * (high - low)
    rows = weight.shape[0] // heads * (high - low)
    return pl.pallas_call(
        functools.partial(attention_kernel, low),
        out_shape=jax.ShapeDtypeStruct((reqs, weight.shape[1]), jnp.bfloat16 if high == heads else jnp.float32),
        in_specs=[SMEM] * 6 + [VMEM] * (2 + len(prior)) + [HBM, HBM],
        out_specs=VMEM,
        scratch_shapes=[
            pltpu.VMEM((keys, width), pool.dtype),
            pltpu.VMEM((rows, weight.shape[1]), weight.dtype),
            pltpu.SemaphoreType.DMA((2,)),
        ],
        compiler_params=pltpu.CompilerParams(vmem_limit_bytes=VMEM_BYTES),
        cost_estimate=pl.CostEstimate(
            flops=4 * reqs * keys * width + 2 * reqs * rows * weight.shape[1],
            bytes_accessed=2 * (keys * width + rows * weight.shape[1]),
            transcendentals=reqs * keys * 2 * (high - low),
        ),
        name="attention",
    )(prompt_table, prompt_len, req_group, cont_table, cont_len, lam, query, new_kv, *prior, *pinned(weight, pool))


def finish_kernel(count, hidden, gain, *refs):
    parts = refs[:count]
    hidden_out, normed_out = refs[count:]
    total = parts[0][...].astype(jnp.float32)
    for part in parts[1:]:
        total = total + part[...].astype(jnp.float32)
    summed = hidden[...].astype(jnp.float32) + total
    norm = lax.rsqrt(jnp.mean(summed * summed, axis=1, keepdims=True) + 1e-05)
    hidden_out[...] = summed.astype(hidden_out.dtype)
    normed_out[...] = (summed * norm * gain[...]).astype(normed_out.dtype)


def finish(hidden, gain, parts):
    shape = jax.ShapeDtypeStruct(hidden.shape, jnp.bfloat16)
    return pl.pallas_call(
        functools.partial(finish_kernel, len(parts)),
        out_shape=[shape, shape],
        in_specs=[VMEM] * (2 + len(parts)),
        out_specs=[VMEM, VMEM],
        compiler_params=pltpu.CompilerParams(vmem_limit_bytes=SMALL_VMEM_BYTES),
        name="finish",
    )(hidden, gain.reshape(1, -1), *parts)


def gather_kernel(choose, count, *refs):
    parts, out, sems = refs[:count], refs[-2], refs[-1]
    copies = [
        (pltpu.make_async_copy(parts[part], out.at[pl.ds(place, MIG_CAP)], sems.at[n]), taken)
        for n, (place, part, taken) in enumerate(choose())
    ]
    for copy, taken in copies:
        pl.when(taken)(copy.start)
    for copy, taken in copies:
        pl.when(taken)(copy.wait)


def arrive(parts, choose, rest=None):
    slots = MIG_REACH * MIG_CAP
    extra = [] if rest is None else pinned(rest)
    return pl.pallas_call(
        functools.partial(gather_kernel, choose, len(parts)),
        out_shape=jax.ShapeDtypeStruct((slots,) + parts[0].shape[1:], parts[0].dtype),
        in_specs=[VMEM] * len(parts) + [HBM] * len(extra),
        out_specs=HBM,
        scratch_shapes=[pltpu.SemaphoreType.DMA((2 * MIG_REACH,))],
        input_output_aliases={len(parts): 0} if extra else {},
        compiler_params=pltpu.CompilerParams(vmem_limit_bytes=SMALL_VMEM_BYTES),
        name="arrive",
    )(*parts, *extra)


def routed(value, targets):
    count, width = lax.axis_size("req"), lax.axis_size("tp")
    pairs = []
    for s in range(count):
        for t in range(width):
            target = targets(s, t % 2)
            if target is not None:
                target = target % count
                pairs.append((s * width + t, target * width + (t ^ 1 if target == s else t)))
    return lax.ppermute(value, ("req", "tp"), pairs)


def turn(s, steps):
    return s - s % MIG_REACH + (s + steps) % MIG_REACH


def route_early(s, odd):
    if s % 2 == 0:
        return s + 1
    return turn(s, 3) if odd else s + 3


def route_late(s, odd):
    return s + 3 if s % 2 == 0 else s + 1


def lift_two(s, odd):
    return s + MIG_REACH if s % MIG_REACH < 2 else s


def lift_early(s, odd):
    return s + MIG_REACH if odd and s % 2 == 0 else None


def choose_straight():
    return [(n * MIG_CAP, n, True) for n in range(MIG_REACH)]


def where_am_i():
    col = lax.rem(lax.axis_index("req"), MIG_REACH)
    odd = lax.rem(col, 2) == 1
    odd_core = lax.rem(lax.axis_index("tp"), 2) == 1
    return col, odd, jnp.logical_not(odd), odd_core


def choose_sooner():
    col, odd, even, odd_core = where_am_i()
    return [
        (0, 1, odd),
        (0, 2, even),
        (2, 0, col >= 2),
        (4, 2, odd),
        (4, 1, even & jnp.logical_not(odd_core)),
        (6, 3, True),
    ]


def choose_later():
    col, odd, even, odd_core = where_am_i()
    return [(2, 0, col < 2), (4, 1, even & odd_core)]


def can_relay():
    count = lax.axis_size("req")
    return MIG_REACH == 4 and count % MIG_REACH == 0 and count > MIG_REACH and lax.axis_size("tp") % 2 == 0


def shards(
    hidden_in,
    query,
    new_kv,
    pool_cache,
    prompt_table,
    prompt_len,
    req_group,
    cont_table,
    cont_len,
    migration,
    diff_lambda,
    out_weight,
    norm_gain,
):
    cont_table, migration = cont_table.T, migration.T
    heads = diff_lambda.shape[0]
    half = heads // 2
    attend = functools.partial(
        attention, query, new_kv, pool_cache, prompt_table, prompt_len, req_group, cont_table, cont_len, diff_lambda, out_weight
    )
    send = (cont_table, cont_len, migration, new_kv, pool_cache)
    prior = [attend(0, half, [])] if half else []
    if can_relay():
        two, four, early, late = send_slots(((2, 2), (4, 4), (1, 3), (3, 1)), *send)
        two = routed(two, lambda s, odd: turn(s, 2))
        four = shifted(four, "req", 4)
        early = routed(early, route_early)
        prior, two, late = lax.optimization_barrier((prior, two, late))
        two_up = routed(two, lift_two)
        late = routed(late, route_late)
        early_up = routed(early, lift_early)
    else:
        outgoing = send_slots(tuple((o, o) for o in range(1, MIG_REACH + 1)), *send)
        arrived = arrive([shifted(part, "req", o + 1) for o, part in enumerate(outgoing)], choose_straight)
    partial = attend(half, heads, prior)
    if lax.axis_size("tp") == 2:
        parts = [partial, shifted(partial, "tp", 1)]
    else:
        parts = [lax.psum(partial, "tp")]
    hidden_out, normed_out = finish(hidden_in, norm_gain, parts)
    if can_relay():
        sooner = arrive((two, early, late, four), choose_sooner)
        arrived = arrive((two_up, early_up), choose_later, sooner)
    return (hidden_out, normed_out, arrived)


def solution(mesh):
    placed = (
        P("req", None),
        P("req", "tp"),
        P("req", "tp"),
        P("req", None, "tp"),
        P("req", None),
        P("req"),
        P("req"),
        P("req", None),
        P("req"),
        P("req", None),
        P("tp"),
        P("tp", None),
        P(),
    )
    return jax.shard_map(
        shards,
        mesh=mesh,
        in_specs=placed,
        out_specs=(P("req", None), P("req", None), P("req", None, "tp")),
        check_vma=False,
    )
```

```python
import functools

import jax
import jax.numpy as jnp
from jax import lax
from jax.experimental import pallas as pl
from jax.experimental.pallas import tpu as pltpu
from jax.sharding import PartitionSpec as P

MIG_REACH = 4
MIG_CAP = 2
KEY = 128
ROWS = 16

SMEM = pl.BlockSpec(memory_space=pltpu.SMEM)
VMEM = pl.BlockSpec(memory_space=pltpu.VMEM)
HBM = pl.BlockSpec(memory_space=pltpu.HBM)
VMEM_BYTES = 40 * 1024 * 1024
SMALL_VMEM_BYTES = 8 * 1024 * 1024


def pinned(*arrays):
    return [pltpu.with_memory_space_constraint(array, pltpu.HBM) for array in arrays]


def shifted(value, axis, steps):
    count = lax.axis_size(axis)
    pairs = [(source, (source + steps) % count) for source in range(count)]
    return lax.ppermute(value, axis, pairs)


def send_kernel(offsets, table_in, length_in, migration_in, new_in, pool, *refs):
    outs = refs[:MIG_REACH]
    table, length, migration, holder, new_held, new_rows, sems, small_sems = refs[MIG_REACH:]
    small = [
        pltpu.make_async_copy(source, target, small_sems.at[n])
        for n, (source, target) in enumerate(
            zip((table_in, length_in, migration_in, new_in), (table, length, migration, new_held))
        )
    ]
    for copy in small:
        copy.start()
    for copy in small[:3]:
        copy.wait()
    entries = migration.shape[1]
    pages, page = table.shape[0], pool.shape[1]
    for place in range(MIG_REACH * MIG_CAP):
        holder[place] = -1
    odd = lax.rem(lax.axis_index("req"), 2)
    where = []
    for n, (on_even, on_odd) in enumerate(offsets):
        offset = on_even + odd * (on_odd - on_even)
        for i in range(MIG_CAP):
            where.append((n * MIG_CAP + i, (offset - 1) * MIG_CAP + i, outs[n].at[i]))
    for e in range(entries):
        rank = jnp.int32(0)
        for before in range(e):
            rank += (migration[1, before] == migration[1, e]).astype(jnp.int32)
        holder[(migration[1, e] - 1) * MIG_CAP + rank] = migration[0, e]

    def page_copy(n, place, out, j):
        slot = jnp.maximum(holder[place], 0)
        return pltpu.make_async_copy(pool.at[table[j, slot]], out.at[pl.ds(j * page, page)], sems.at[n, j])

    def used(place, j):
        slot = holder[place]
        return (slot >= 0) & (length[jnp.maximum(slot, 0)] >= j * page)

    for n, place, out in where:
        for j in range(pages):

            @pl.when(used(place, j))
            def _():
                page_copy(n, place, out, j).start()

    small[3].wait()
    new_rows[...] = new_held[...].astype(jnp.float32)
    for n, place, out in where:
        slot = holder[place]
        safe = jnp.maximum(slot, 0)
        last = jnp.where(slot >= 0, length[safe], -1)
        for j in range(pages):

            @pl.when(used(place, j))
            def _():
                page_copy(n, place, out, j).wait()

            for low in range(j * page, (j + 1) * page, ROWS):

                @pl.when(last < low)
                def _():
                    out[pl.ds(low, ROWS)] = jnp.zeros((ROWS, out.shape[1]), out.dtype)

                @pl.when((last >= low) & (last < low + ROWS))
                def _():
                    held = out[pl.ds(low, ROWS)].astype(jnp.float32)
                    pos = low + lax.broadcasted_iota(jnp.int32, held.shape, 0)
                    new = jnp.where(pos == last, new_rows[pl.ds(safe, 1)], 0.0)
                    out[pl.ds(low, ROWS)] = jnp.where(pos < last, held, new).astype(out.dtype)


def send_slots(offsets, cont_table, cont_len, migration, new_kv, pool):
    span = cont_table.shape[0] * pool.shape[1]
    width = pool.shape[2]
    return pl.pallas_call(
        functools.partial(send_kernel, offsets),
        out_shape=[jax.ShapeDtypeStruct((MIG_CAP, span, width), pool.dtype)] * MIG_REACH,
        in_specs=[HBM] * 5,
        out_specs=[VMEM] * MIG_REACH,
        scratch_shapes=[
            pltpu.SMEM(cont_table.shape, jnp.int32),
            pltpu.SMEM(cont_len.shape, jnp.int32),
            pltpu.SMEM(migration.shape, jnp.int32),
            pltpu.SMEM((MIG_REACH * MIG_CAP,), jnp.int32),
            pltpu.VMEM(new_kv.shape, new_kv.dtype),
            pltpu.VMEM(new_kv.shape, jnp.float32),
            pltpu.SemaphoreType.DMA((MIG_REACH * MIG_CAP, cont_table.shape[0])),
            pltpu.SemaphoreType.DMA((4,)),
        ],
        compiler_params=pltpu.CompilerParams(vmem_limit_bytes=VMEM_BYTES),
        name="send_slots",
    )(*pinned(cont_table, cont_len, migration, new_kv, pool))


def column(values, count):
    rows = lax.broadcasted_iota(jnp.int32, (count, 1), 0)
    out = jnp.zeros((count, 1), jnp.int32)
    for r in range(count):
        out = jnp.where(rows == r, values[r], out)
    return out


def attention_kernel(low, prompt_table, prompt_len, req_group, cont_table, cont_len, lam, query, new_ref, *refs):
    prior = refs[:-6]
    weight, pool, out, held, weight_held, sems = refs[-6:]
    groups, prompt_pages = prompt_table.shape
    cont_pages, reqs = cont_table.shape
    page = pool.shape[1]
    span = prompt_pages * page
    own = cont_pages * page
    start = groups * span
    head_width = pool.shape[2] // lam.shape[0]
    value_width = head_width - 2 * KEY
    width = held.shape[1]
    heads = width // head_width
    columns = pl.ds(low * head_width, width)

    for g in range(groups):

        @pl.loop(0, prompt_pages)
        def _(j):
            at = pl.multiple_of(g * span + j * page, page)
            pltpu.make_async_copy(pool.at[prompt_table[g, j], :, columns], held.at[pl.ds(at, page)], sems.at[0]).start()

    @pl.loop(0, reqs)
    def _(r):
        for j in range(cont_pages):
            at = pl.multiple_of(start + r * own + j * page, page)
            pltpu.make_async_copy(pool.at[cont_table[j, r], :, columns], held.at[pl.ds(at, page)], sems.at[0]).start()

    rows = pl.ds(low * value_width, weight_held.shape[0])
    weight_copy = pltpu.make_async_copy(weight.at[rows], weight_held, sems.at[1])
    weight_copy.start()

    group_of = column(req_group, reqs)
    length_of = column(cont_len, reqs)
    biases = []
    pos = lax.broadcasted_iota(jnp.int32, (reqs, span), 1)
    for g in range(groups):
        live = (group_of == g) & (pos < prompt_len[g])
        biases.append(jnp.where(live, 0.0, -1e30))
    key = lax.broadcasted_iota(jnp.int32, (reqs, reqs * own), 1)
    pos = key - own * lax.broadcasted_iota(jnp.int32, (reqs, reqs * own), 0)
    biases.append(jnp.where((pos >= 0) & (pos < length_of), 0.0, -1e30))
    live = jnp.concatenate(biases, axis=1) == 0.0

    pltpu.make_async_copy(held, held, sems.at[0]).wait()

    scale = KEY**-0.5
    mixed = []
    for h in range(heads):
        first = h * head_width
        weights, new_weights = [], []
        for i in range(2):
            q = query[:, pl.ds((2 * (low + h) + i) * KEY, KEY)]
            cols = pl.ds(first + i * KEY, KEY)
            new_cols = pl.ds(low * head_width + first + i * KEY, KEY)
            score = lax.dot_general(
                q, held[:, cols], (((1,), (1,)), ((), ())), preferred_element_type=jnp.float32
            )
            score = jnp.where(live, score * scale, -1e30)
            new = jnp.sum(q.astype(jnp.float32) * new_ref[:, new_cols].astype(jnp.float32), axis=1, keepdims=True) * scale
            top = jnp.maximum(jnp.max(score, axis=1, keepdims=True), new)
            score = jnp.exp(score - top)
            new = jnp.exp(new - top)
            inverse = 1.0 / (jnp.sum(score, axis=1, keepdims=True) + new)
            weights.append((score * inverse).astype(jnp.bfloat16))
            new_weights.append((new * inverse).astype(jnp.bfloat16).astype(jnp.float32))
        cols = pl.ds(first + 2 * KEY, value_width)
        mixture = jnp.dot(jnp.concatenate(weights, axis=0), held[:, cols], preferred_element_type=jnp.float32)
        new_value = new_ref[:, pl.ds(low * head_width + first + 2 * KEY, value_width)].astype(jnp.float32)
        one = mixture[:reqs] + new_weights[0] * new_value
        two = mixture[reqs:] + new_weights[1] * new_value
        diff = one - lam[low + h] * two
        norm = lax.rsqrt(jnp.mean(diff * diff, axis=1, keepdims=True) + 1e-05)
        mixed.append((diff * norm * 0.8).astype(jnp.bfloat16))
    weight_copy.wait()
    mixed = jnp.concatenate(mixed, axis=1)
    product = jnp.dot(mixed, weight_held[...], preferred_element_type=jnp.float32)
    for part in prior:
        product = product + part[...]
    out[...] = product.astype(out.dtype)


def attention(query, new_kv, pool, prompt_table, prompt_len, req_group, cont_table, cont_len, lam, weight, low, high, prior):
    reqs = query.shape[0]
    page = pool.shape[1]
    heads = lam.shape[0]
    keys = (prompt_table.size + cont_table.size) * page
    width = pool.shape[2] // heads * (high - low)
    rows = weight.shape[0] // heads * (high - low)
    return pl.pallas_call(
        functools.partial(attention_kernel, low),
        out_shape=jax.ShapeDtypeStruct((reqs, weight.shape[1]), jnp.bfloat16 if high == heads else jnp.float32),
        in_specs=[SMEM] * 6 + [VMEM] * (2 + len(prior)) + [HBM, HBM],
        out_specs=VMEM,
        scratch_shapes=[
            pltpu.VMEM((keys, width), pool.dtype),
            pltpu.VMEM((rows, weight.shape[1]), weight.dtype),
            pltpu.SemaphoreType.DMA((2,)),
        ],
        compiler_params=pltpu.CompilerParams(vmem_limit_bytes=VMEM_BYTES),
        cost_estimate=pl.CostEstimate(
            flops=4 * reqs * keys * width + 2 * reqs * rows * weight.shape[1],
            bytes_accessed=2 * (keys * width + rows * weight.shape[1]),
            transcendentals=reqs * keys * 2 * (high - low),
        ),
        name="attention",
    )(prompt_table, prompt_len, req_group, cont_table, cont_len, lam, query, new_kv, *prior, *pinned(weight, pool))


def finish_kernel(count, hidden, gain, *refs):
    parts = refs[:count]
    hidden_out, normed_out = refs[count:]
    total = parts[0][...].astype(jnp.float32)
    for part in parts[1:]:
        total = total + part[...].astype(jnp.float32)
    summed = hidden[...].astype(jnp.float32) + total
    norm = lax.rsqrt(jnp.mean(summed * summed, axis=1, keepdims=True) + 1e-05)
    hidden_out[...] = summed.astype(hidden_out.dtype)
    normed_out[...] = (summed * norm * gain[...]).astype(normed_out.dtype)


def finish(hidden, gain, parts):
    shape = jax.ShapeDtypeStruct(hidden.shape, jnp.bfloat16)
    return pl.pallas_call(
        functools.partial(finish_kernel, len(parts)),
        out_shape=[shape, shape],
        in_specs=[VMEM] * (2 + len(parts)),
        out_specs=[VMEM, VMEM],
        compiler_params=pltpu.CompilerParams(vmem_limit_bytes=SMALL_VMEM_BYTES),
        name="finish",
    )(hidden, gain.reshape(1, -1), *parts)


def gather_kernel(choose, count, *refs):
    parts, out, sems = refs[:count], refs[-2], refs[-1]
    copies = [
        (pltpu.make_async_copy(parts[part], out.at[pl.ds(place, MIG_CAP)], sems.at[n]), taken)
        for n, (place, part, taken) in enumerate(choose())
    ]
    for copy, taken in copies:
        pl.when(taken)(copy.start)
    for copy, taken in copies:
        pl.when(taken)(copy.wait)


def arrive(parts, choose, rest=None):
    slots = MIG_REACH * MIG_CAP
    extra = [] if rest is None else pinned(rest)
    return pl.pallas_call(
        functools.partial(gather_kernel, choose, len(parts)),
        out_shape=jax.ShapeDtypeStruct((slots,) + parts[0].shape[1:], parts[0].dtype),
        in_specs=[VMEM] * len(parts) + [HBM] * len(extra),
        out_specs=HBM,
        scratch_shapes=[pltpu.SemaphoreType.DMA((2 * MIG_REACH,))],
        input_output_aliases={len(parts): 0} if extra else {},
        compiler_params=pltpu.CompilerParams(vmem_limit_bytes=SMALL_VMEM_BYTES),
        name="arrive",
    )(*parts, *extra)


def routed(value, targets):
    count, width = lax.axis_size("req"), lax.axis_size("tp")
    pairs = []
    for s in range(count):
        for t in range(width):
            target = targets(s, t % 2)
            if target is not None:
                target = target % count
                pairs.append((s * width + t, target * width + (t ^ 1 if target == s else t)))
    return lax.ppermute(value, ("req", "tp"), pairs)


def turn(s, steps):
    return s - s % MIG_REACH + (s + steps) % MIG_REACH


def route_early(s, odd):
    if s % 2 == 0:
        return s + 1
    return turn(s, 3) if odd else s + 3


def route_late(s, odd):
    return s + 3 if s % 2 == 0 else s + 1


def lift_two(s, odd):
    return s + MIG_REACH if s % MIG_REACH < 2 else s


def lift_early(s, odd):
    return s + MIG_REACH if odd and s % 2 == 0 else None


def choose_straight():
    return [(n * MIG_CAP, n, True) for n in range(MIG_REACH)]


def where_am_i():
    col = lax.rem(lax.axis_index("req"), MIG_REACH)
    odd = lax.rem(col, 2) == 1
    odd_core = lax.rem(lax.axis_index("tp"), 2) == 1
    return col, odd, jnp.logical_not(odd), odd_core


def choose_sooner():
    col, odd, even, odd_core = where_am_i()
    return [(0, 2, odd), (2, 0, col >= 2), (2, 1, col < 2), (4, 2, even & jnp.logical_not(odd_core)), (6, 3, True)]


def choose_later():
    col, odd, even, odd_core = where_am_i()
    return [(0, 1, even), (4, 1, odd), (4, 0, even & odd_core)]


def can_relay():
    count = lax.axis_size("req")
    return MIG_REACH == 4 and count % MIG_REACH == 0 and count > MIG_REACH and lax.axis_size("tp") % 2 == 0


def shards(
    hidden_in,
    query,
    new_kv,
    pool_cache,
    prompt_table,
    prompt_len,
    req_group,
    cont_table,
    cont_len,
    migration,
    diff_lambda,
    out_weight,
    norm_gain,
):
    cont_table, migration = cont_table.T, migration.T
    heads = diff_lambda.shape[0]
    half = heads // 2
    attend = functools.partial(
        attention, query, new_kv, pool_cache, prompt_table, prompt_len, req_group, cont_table, cont_len, diff_lambda, out_weight
    )
    send = (cont_table, cont_len, migration, new_kv, pool_cache)
    prior = [attend(0, half, [])] if half else []
    if can_relay():
        two, four, early, late = send_slots(((2, 2), (4, 4), (1, 3), (3, 1)), *send)
        two = routed(two, lambda s, odd: turn(s, 2))
        four = shifted(four, "req", 4)
        early = routed(early, route_early)
        prior, two, late = lax.optimization_barrier((prior, two, late))
        two_up = routed(two, lift_two)
        late = routed(late, route_late)
        early_up = routed(early, lift_early)
    else:
        outgoing = send_slots(tuple((o, o) for o in range(1, MIG_REACH + 1)), *send)
        arrived = arrive([shifted(part, "req", o + 1) for o, part in enumerate(outgoing)], choose_straight)
    partial = attend(half, heads, prior)
    if lax.axis_size("tp") == 2:
        parts = [partial, shifted(partial, "tp", 1)]
    else:
        parts = [lax.psum(partial, "tp")]
    hidden_out, normed_out = finish(hidden_in, norm_gain, parts)
    if can_relay():
        sooner = arrive((two, two_up, early, four), choose_sooner)
        arrived = arrive((early_up, late), choose_later, sooner)
    return (hidden_out, normed_out, arrived)


def solution(mesh):
    placed = (
        P("req", None),
        P("req", "tp"),
        P("req", "tp"),
        P("req", None, "tp"),
        P("req", None),
        P("req"),
        P("req"),
        P("req", None),
        P("req"),
        P("req", None),
        P("tp"),
        P("tp", None),
        P(),
    )
    return jax.shard_map(
        shards,
        mesh=mesh,
        in_specs=placed,
        out_specs=(P("req", None), P("req", None), P("req", None, "tp")),
        check_vma=False,
    )
```

```python
import functools

import jax
import jax.numpy as jnp
from jax import lax
from jax.experimental import pallas as pl
from jax.experimental.pallas import tpu as pltpu
from jax.sharding import PartitionSpec as P

MIG_REACH = 4
MIG_CAP = 2
KEY = 128
ROWS = 16

SMEM = pl.BlockSpec(memory_space=pltpu.SMEM)
VMEM = pl.BlockSpec(memory_space=pltpu.VMEM)
HBM = pl.BlockSpec(memory_space=pltpu.HBM)
VMEM_BYTES = 40 * 1024 * 1024
SMALL_VMEM_BYTES = 8 * 1024 * 1024


def pinned(*arrays):
    return [pltpu.with_memory_space_constraint(array, pltpu.HBM) for array in arrays]


def shifted(value, axis, steps):
    count = lax.axis_size(axis)
    pairs = [(source, (source + steps) % count) for source in range(count)]
    return lax.ppermute(value, axis, pairs)


def send_kernel(offsets, table_in, length_in, migration_in, new_in, pool, *refs):
    outs = refs[: len(offsets)]
    table, length, migration, holder, new_held, new_rows, sems, small_sems = refs[len(offsets) :]
    small = [
        pltpu.make_async_copy(source, target, small_sems.at[n])
        for n, (source, target) in enumerate(
            zip((table_in, length_in, migration_in, new_in), (table, length, migration, new_held))
        )
    ]
    for copy in small:
        copy.start()
    for copy in small[:3]:
        copy.wait()
    entries = migration.shape[1]
    pages, page = table.shape[0], pool.shape[1]
    for place in range(MIG_REACH * MIG_CAP):
        holder[place] = -1
    odd = lax.rem(lax.axis_index("req"), 2)
    where = []
    for n, (on_even, on_odd) in enumerate(offsets):
        offset = on_even + odd * (on_odd - on_even)
        for i in range(MIG_CAP):
            where.append((n * MIG_CAP + i, (offset - 1) * MIG_CAP + i, outs[n].at[i]))
    for e in range(entries):
        rank = jnp.int32(0)
        for before in range(e):
            rank += (migration[1, before] == migration[1, e]).astype(jnp.int32)
        holder[(migration[1, e] - 1) * MIG_CAP + rank] = migration[0, e]

    def last_of(place):
        slot = holder[place]
        return jnp.where(slot >= 0, length[jnp.maximum(slot, 0)], -1)

    def block_copy(n, place, out, low):
        source = pool.at[table[low // page, jnp.maximum(holder[place], 0)], pl.ds(low % page, ROWS)]
        return pltpu.make_async_copy(source, out.at[pl.ds(low, ROWS)], sems.at[n, low // ROWS])

    lows = range(0, pages * page, ROWS)
    for n, place, out in where:
        for low in lows:

            @pl.when(last_of(place) >= low)
            def _():
                block_copy(n, place, out, low).start()

    for n, place, out in where:
        for low in lows:

            @pl.when(last_of(place) < low)
            def _():
                out[pl.ds(low, ROWS)] = jnp.zeros((ROWS, out.shape[1]), out.dtype)

    small[3].wait()
    new_rows[...] = new_held[...].astype(jnp.float32)
    for n, place, out in where:
        last = last_of(place)
        safe = jnp.maximum(holder[place], 0)
        for low in lows:

            @pl.when(last >= low)
            def _():
                block_copy(n, place, out, low).wait()

            @pl.when((last >= low) & (last < low + ROWS))
            def _():
                held = out[pl.ds(low, ROWS)].astype(jnp.float32)
                pos = low + lax.broadcasted_iota(jnp.int32, held.shape, 0)
                new = jnp.where(pos == last, new_rows[pl.ds(safe, 1)], 0.0)
                out[pl.ds(low, ROWS)] = jnp.where(pos < last, held, new).astype(out.dtype)


def send_slots(offsets, cont_table, cont_len, migration, new_kv, pool):
    span = cont_table.shape[0] * pool.shape[1]
    width = pool.shape[2]
    return pl.pallas_call(
        functools.partial(send_kernel, offsets),
        out_shape=[jax.ShapeDtypeStruct((MIG_CAP, span, width), pool.dtype)] * len(offsets),
        in_specs=[HBM] * 5,
        out_specs=[VMEM] * len(offsets),
        scratch_shapes=[
            pltpu.SMEM(cont_table.shape, jnp.int32),
            pltpu.SMEM(cont_len.shape, jnp.int32),
            pltpu.SMEM(migration.shape, jnp.int32),
            pltpu.SMEM((MIG_REACH * MIG_CAP,), jnp.int32),
            pltpu.VMEM(new_kv.shape, new_kv.dtype),
            pltpu.VMEM(new_kv.shape, jnp.float32),
            pltpu.SemaphoreType.DMA((len(offsets) * MIG_CAP, span // ROWS)),
            pltpu.SemaphoreType.DMA((4,)),
        ],
        compiler_params=pltpu.CompilerParams(vmem_limit_bytes=VMEM_BYTES),
        name="send_slots",
    )(*pinned(cont_table, cont_len, migration, new_kv, pool))


def column(values, count):
    rows = lax.broadcasted_iota(jnp.int32, (count, 1), 0)
    out = jnp.zeros((count, 1), jnp.int32)
    for r in range(count):
        out = jnp.where(rows == r, values[r], out)
    return out


def attention_kernel(low, prompt_table, prompt_len, req_group, cont_table, cont_len, lam, query, new_ref, *refs):
    prior = refs[:-6]
    weight, pool, out, held, weight_held, sems = refs[-6:]
    groups, prompt_pages = prompt_table.shape
    cont_pages, reqs = cont_table.shape
    page = pool.shape[1]
    span = prompt_pages * page
    own = cont_pages * page
    start = groups * span
    head_width = pool.shape[2] // lam.shape[0]
    value_width = head_width - 2 * KEY
    width = held.shape[1]
    heads = width // head_width
    columns = pl.ds(low * head_width, width)

    for g in range(groups):

        @pl.loop(0, prompt_pages)
        def _(j):
            at = pl.multiple_of(g * span + j * page, page)
            pltpu.make_async_copy(pool.at[prompt_table[g, j], :, columns], held.at[pl.ds(at, page)], sems.at[0]).start()

    @pl.loop(0, reqs)
    def _(r):
        for j in range(cont_pages):
            at = pl.multiple_of(start + r * own + j * page, page)
            pltpu.make_async_copy(pool.at[cont_table[j, r], :, columns], held.at[pl.ds(at, page)], sems.at[0]).start()

    rows = pl.ds(low * value_width, weight_held.shape[0])
    weight_copy = pltpu.make_async_copy(weight.at[rows], weight_held, sems.at[1])
    weight_copy.start()

    group_of = column(req_group, reqs)
    length_of = column(cont_len, reqs)
    biases = []
    pos = lax.broadcasted_iota(jnp.int32, (reqs, span), 1)
    for g in range(groups):
        live = (group_of == g) & (pos < prompt_len[g])
        biases.append(jnp.where(live, 0.0, -1e30))
    key = lax.broadcasted_iota(jnp.int32, (reqs, reqs * own), 1)
    pos = key - own * lax.broadcasted_iota(jnp.int32, (reqs, reqs * own), 0)
    biases.append(jnp.where((pos >= 0) & (pos < length_of), 0.0, -1e30))
    live = jnp.concatenate(biases, axis=1) == 0.0

    pltpu.make_async_copy(held, held, sems.at[0]).wait()

    scale = KEY**-0.5
    mixed = []
    for h in range(heads):
        first = h * head_width
        weights, new_weights = [], []
        for i in range(2):
            q = query[:, pl.ds((2 * (low + h) + i) * KEY, KEY)]
            cols = pl.ds(first + i * KEY, KEY)
            new_cols = pl.ds(low * head_width + first + i * KEY, KEY)
            score = lax.dot_general(
                q, held[:, cols], (((1,), (1,)), ((), ())), preferred_element_type=jnp.float32
            )
            score = jnp.where(live, score * scale, -1e30)
            new = jnp.sum(q.astype(jnp.float32) * new_ref[:, new_cols].astype(jnp.float32), axis=1, keepdims=True) * scale
            top = jnp.maximum(jnp.max(score, axis=1, keepdims=True), new)
            score = jnp.exp(score - top)
            new = jnp.exp(new - top)
            inverse = 1.0 / (jnp.sum(score, axis=1, keepdims=True) + new)
            weights.append((score * inverse).astype(jnp.bfloat16))
            new_weights.append((new * inverse).astype(jnp.bfloat16).astype(jnp.float32))
        cols = pl.ds(first + 2 * KEY, value_width)
        mixture = jnp.dot(jnp.concatenate(weights, axis=0), held[:, cols], preferred_element_type=jnp.float32)
        new_value = new_ref[:, pl.ds(low * head_width + first + 2 * KEY, value_width)].astype(jnp.float32)
        one = mixture[:reqs] + new_weights[0] * new_value
        two = mixture[reqs:] + new_weights[1] * new_value
        diff = one - lam[low + h] * two
        norm = lax.rsqrt(jnp.mean(diff * diff, axis=1, keepdims=True) + 1e-05)
        mixed.append((diff * norm * 0.8).astype(jnp.bfloat16))
    weight_copy.wait()
    mixed = jnp.concatenate(mixed, axis=1)
    product = jnp.dot(mixed, weight_held[...], preferred_element_type=jnp.float32)
    for part in prior:
        product = product + part[...]
    out[...] = product.astype(out.dtype)


def attention(query, new_kv, pool, prompt_table, prompt_len, req_group, cont_table, cont_len, lam, weight, low, high, prior):
    reqs = query.shape[0]
    page = pool.shape[1]
    heads = lam.shape[0]
    keys = (prompt_table.size + cont_table.size) * page
    width = pool.shape[2] // heads * (high - low)
    rows = weight.shape[0] // heads * (high - low)
    return pl.pallas_call(
        functools.partial(attention_kernel, low),
        out_shape=jax.ShapeDtypeStruct((reqs, weight.shape[1]), jnp.bfloat16 if high == heads else jnp.float32),
        in_specs=[SMEM] * 6 + [VMEM] * (2 + len(prior)) + [HBM, HBM],
        out_specs=VMEM,
        scratch_shapes=[
            pltpu.VMEM((keys, width), pool.dtype),
            pltpu.VMEM((rows, weight.shape[1]), weight.dtype),
            pltpu.SemaphoreType.DMA((2,)),
        ],
        compiler_params=pltpu.CompilerParams(vmem_limit_bytes=VMEM_BYTES),
        cost_estimate=pl.CostEstimate(
            flops=4 * reqs * keys * width + 2 * reqs * rows * weight.shape[1],
            bytes_accessed=2 * (keys * width + rows * weight.shape[1]),
            transcendentals=reqs * keys * 2 * (high - low),
        ),
        name="attention",
    )(prompt_table, prompt_len, req_group, cont_table, cont_len, lam, query, new_kv, *prior, *pinned(weight, pool))


def finish_kernel(count, hidden, gain, *refs):
    parts = refs[:count]
    hidden_out, normed_out = refs[count:]
    total = parts[0][...].astype(jnp.float32)
    for part in parts[1:]:
        total = total + part[...].astype(jnp.float32)
    summed = hidden[...].astype(jnp.float32) + total
    norm = lax.rsqrt(jnp.mean(summed * summed, axis=1, keepdims=True) + 1e-05)
    hidden_out[...] = summed.astype(hidden_out.dtype)
    normed_out[...] = (summed * norm * gain[...]).astype(normed_out.dtype)


def finish(hidden, gain, parts):
    shape = jax.ShapeDtypeStruct(hidden.shape, jnp.bfloat16)
    return pl.pallas_call(
        functools.partial(finish_kernel, len(parts)),
        out_shape=[shape, shape],
        in_specs=[VMEM] * (2 + len(parts)),
        out_specs=[VMEM, VMEM],
        compiler_params=pltpu.CompilerParams(vmem_limit_bytes=SMALL_VMEM_BYTES),
        name="finish",
    )(hidden, gain.reshape(1, -1), *parts)


def gather_kernel(choose, count, *refs):
    parts, out, sems = refs[:count], refs[-2], refs[-1]
    copies = [
        (pltpu.make_async_copy(parts[part], out.at[pl.ds(place, MIG_CAP)], sems.at[n]), taken)
        for n, (place, part, taken) in enumerate(choose())
    ]
    for copy, taken in copies:
        pl.when(taken)(copy.start)
    for copy, taken in copies:
        pl.when(taken)(copy.wait)


def arrive(parts, choose, rest=None):
    slots = MIG_REACH * MIG_CAP
    extra = [] if rest is None else pinned(rest)
    return pl.pallas_call(
        functools.partial(gather_kernel, choose, len(parts)),
        out_shape=jax.ShapeDtypeStruct((slots,) + parts[0].shape[1:], parts[0].dtype),
        in_specs=[VMEM] * len(parts) + [HBM] * len(extra),
        out_specs=HBM,
        scratch_shapes=[pltpu.SemaphoreType.DMA((2 * MIG_REACH,))],
        input_output_aliases={len(parts): 0} if extra else {},
        compiler_params=pltpu.CompilerParams(vmem_limit_bytes=SMALL_VMEM_BYTES),
        name="arrive",
    )(*parts, *extra)


def routed(value, targets):
    count, width = lax.axis_size("req"), lax.axis_size("tp")
    pairs = []
    for s in range(count):
        for t in range(width):
            target = targets(s, t % 2)
            if target is not None:
                target = target % count
                pairs.append((s * width + t, target * width + (t ^ 1 if target == s else t)))
    return lax.ppermute(value, ("req", "tp"), pairs)


def turn(s, steps):
    return s - s % MIG_REACH + (s + steps) % MIG_REACH


def route_early(s, odd):
    if s % 2 == 0:
        return s + 1
    return turn(s, 3) if odd else s + 3


def route_late(s, odd):
    return s + 3 if s % 2 == 0 else s + 1


def lift_two(s, odd):
    return s + MIG_REACH if s % MIG_REACH < 2 else s


def lift_early(s, odd):
    return s + MIG_REACH if odd and s % 2 == 0 else None


def choose_straight():
    return [(n * MIG_CAP, n, True) for n in range(MIG_REACH)]


def where_am_i():
    col = lax.rem(lax.axis_index("req"), MIG_REACH)
    odd = lax.rem(col, 2) == 1
    odd_core = lax.rem(lax.axis_index("tp"), 2) == 1
    return col, odd, jnp.logical_not(odd), odd_core


def choose_sooner():
    col, odd, even, odd_core = where_am_i()
    return [(0, 2, odd), (2, 0, col >= 2), (2, 1, col < 2), (4, 2, even & jnp.logical_not(odd_core)), (6, 3, True)]


def choose_later():
    col, odd, even, odd_core = where_am_i()
    return [(0, 1, even), (4, 1, odd), (4, 0, even & odd_core)]


def can_relay():
    count = lax.axis_size("req")
    return MIG_REACH == 4 and count % MIG_REACH == 0 and count > MIG_REACH and lax.axis_size("tp") % 2 == 0


def shards(
    hidden_in,
    query,
    new_kv,
    pool_cache,
    prompt_table,
    prompt_len,
    req_group,
    cont_table,
    cont_len,
    migration,
    diff_lambda,
    out_weight,
    norm_gain,
):
    cont_table, migration = cont_table.T, migration.T
    heads = diff_lambda.shape[0]
    half = heads // 2
    attend = functools.partial(
        attention, query, new_kv, pool_cache, prompt_table, prompt_len, req_group, cont_table, cont_len, diff_lambda, out_weight
    )
    send = (cont_table, cont_len, migration, new_kv, pool_cache)
    prior = [attend(0, half, [])] if half else []
    if can_relay():
        two, four, early = send_slots(((2, 2), (4, 4), (1, 3)), *send)
        two = routed(two, lambda s, odd: turn(s, 2))
        four = shifted(four, "req", 4)
        early = routed(early, route_early)
        prior, later_len = lax.optimization_barrier((prior, cont_len))
        (late,) = send_slots(((3, 1),), cont_table, later_len, *send[2:])
        prior, two, late = lax.optimization_barrier((prior, two, late))
        two_up = routed(two, lift_two)
        late = routed(late, route_late)
        early_up = routed(early, lift_early)
    else:
        outgoing = send_slots(tuple((o, o) for o in range(1, MIG_REACH + 1)), *send)
        arrived = arrive([shifted(part, "req", o + 1) for o, part in enumerate(outgoing)], choose_straight)
    partial = attend(half, heads, prior)
    if lax.axis_size("tp") == 2:
        parts = [partial, shifted(partial, "tp", 1)]
    else:
        parts = [lax.psum(partial, "tp")]
    hidden_out, normed_out = finish(hidden_in, norm_gain, parts)
    if can_relay():
        sooner = arrive((two, two_up, early, four), choose_sooner)
        arrived = arrive((early_up, late), choose_later, sooner)
    return (hidden_out, normed_out, arrived)


def solution(mesh):
    placed = (
        P("req", None),
        P("req", "tp"),
        P("req", "tp"),
        P("req", None, "tp"),
        P("req", None),
        P("req"),
        P("req"),
        P("req", None),
        P("req"),
        P("req", None),
        P("tp"),
        P("tp", None),
        P(),
    )
    return jax.shard_map(
        shards,
        mesh=mesh,
        in_specs=placed,
        out_specs=(P("req", None), P("req", None), P("req", None, "tp")),
        check_vma=False,
    )
```

```python
import functools

import jax
import jax.numpy as jnp
from jax import lax
from jax.experimental import pallas as pl
from jax.experimental.pallas import tpu as pltpu
from jax.sharding import PartitionSpec as P

MIG_REACH = 4
MIG_CAP = 2
KEY = 128
ROWS = 16

SMEM = pl.BlockSpec(memory_space=pltpu.SMEM)
VMEM = pl.BlockSpec(memory_space=pltpu.VMEM)
HBM = pl.BlockSpec(memory_space=pltpu.HBM)
VMEM_BYTES = 40 * 1024 * 1024
SMALL_VMEM_BYTES = 8 * 1024 * 1024


def pinned(*arrays):
    return [pltpu.with_memory_space_constraint(array, pltpu.HBM) for array in arrays]


def shifted(value, axis, steps):
    count = lax.axis_size(axis)
    pairs = [(source, (source + steps) % count) for source in range(count)]
    return lax.ppermute(value, axis, pairs)


def send_kernel(offsets, table_in, length_in, migration_in, new_in, pool, *refs):
    outs = refs[: len(offsets)]
    table, length, migration, holder, new_held, new_rows, sems, small_sems = refs[len(offsets) :]
    small = [
        pltpu.make_async_copy(source, target, small_sems.at[n])
        for n, (source, target) in enumerate(
            zip((table_in, length_in, migration_in, new_in), (table, length, migration, new_held))
        )
    ]
    for copy in small:
        copy.start()
    for copy in small[:3]:
        copy.wait()
    entries = migration.shape[1]
    pages, page = table.shape[0], pool.shape[1]
    for place in range(MIG_REACH * MIG_CAP):
        holder[place] = -1
    odd = lax.rem(lax.axis_index("req"), 2)
    where = []
    for n, (on_even, on_odd) in enumerate(offsets):
        offset = on_even + odd * (on_odd - on_even)
        for i in range(MIG_CAP):
            where.append((n * MIG_CAP + i, (offset - 1) * MIG_CAP + i, outs[n].at[i]))
    for e in range(entries):
        rank = jnp.int32(0)
        for before in range(e):
            rank += (migration[1, before] == migration[1, e]).astype(jnp.int32)
        holder[(migration[1, e] - 1) * MIG_CAP + rank] = migration[0, e]

    def last_of(place):
        slot = holder[place]
        return jnp.where(slot >= 0, length[jnp.maximum(slot, 0)], -1)

    def block_copy(n, place, out, low):
        source = pool.at[table[low // page, jnp.maximum(holder[place], 0)], pl.ds(low % page, ROWS)]
        return pltpu.make_async_copy(source, out.at[pl.ds(low, ROWS)], sems.at[n, low // ROWS])

    lows = range(0, pages * page, ROWS)
    for n, place, out in where:
        for low in lows:

            @pl.when(last_of(place) >= low)
            def _():
                block_copy(n, place, out, low).start()

    for n, place, out in where:
        for low in lows:

            @pl.when(last_of(place) < low)
            def _():
                out[pl.ds(low, ROWS)] = jnp.zeros((ROWS, out.shape[1]), out.dtype)

    small[3].wait()
    new_rows[...] = new_held[...].astype(jnp.float32)
    for n, place, out in where:
        last = last_of(place)
        safe = jnp.maximum(holder[place], 0)
        for low in lows:

            @pl.when(last >= low)
            def _():
                block_copy(n, place, out, low).wait()

            @pl.when((last >= low) & (last < low + ROWS))
            def _():
                held = out[pl.ds(low, ROWS)].astype(jnp.float32)
                pos = low + lax.broadcasted_iota(jnp.int32, held.shape, 0)
                new = jnp.where(pos == last, new_rows[pl.ds(safe, 1)], 0.0)
                out[pl.ds(low, ROWS)] = jnp.where(pos < last, held, new).astype(out.dtype)


def send_slots(offsets, cont_table, cont_len, migration, new_kv, pool):
    span = cont_table.shape[0] * pool.shape[1]
    width = pool.shape[2]
    return pl.pallas_call(
        functools.partial(send_kernel, offsets),
        out_shape=[jax.ShapeDtypeStruct((MIG_CAP, span, width), pool.dtype)] * len(offsets),
        in_specs=[HBM] * 5,
        out_specs=[VMEM] * len(offsets),
        scratch_shapes=[
            pltpu.SMEM(cont_table.shape, jnp.int32),
            pltpu.SMEM(cont_len.shape, jnp.int32),
            pltpu.SMEM(migration.shape, jnp.int32),
            pltpu.SMEM((MIG_REACH * MIG_CAP,), jnp.int32),
            pltpu.VMEM(new_kv.shape, new_kv.dtype),
            pltpu.VMEM(new_kv.shape, jnp.float32),
            pltpu.SemaphoreType.DMA((len(offsets) * MIG_CAP, span // ROWS)),
            pltpu.SemaphoreType.DMA((4,)),
        ],
        compiler_params=pltpu.CompilerParams(vmem_limit_bytes=VMEM_BYTES),
        name="send_slots",
    )(*pinned(cont_table, cont_len, migration, new_kv, pool))


def column(values, count):
    rows = lax.broadcasted_iota(jnp.int32, (count, 1), 0)
    out = jnp.zeros((count, 1), jnp.int32)
    for r in range(count):
        out = jnp.where(rows == r, values[r], out)
    return out


def attention_kernel(low, prompt_table, prompt_len, req_group, cont_table, cont_len, lam, query, new_ref, *refs):
    prior = refs[:-6]
    weight, pool, out, held, weight_held, sems = refs[-6:]
    groups, prompt_pages = prompt_table.shape
    cont_pages, reqs = cont_table.shape
    page = pool.shape[1]
    span = prompt_pages * page
    own = cont_pages * page
    start = groups * span
    head_width = pool.shape[2] // lam.shape[0]
    value_width = head_width - 2 * KEY
    width = held.shape[1]
    heads = width // head_width
    columns = pl.ds(low * head_width, width)

    for g in range(groups):

        @pl.loop(0, prompt_pages)
        def _(j):
            at = pl.multiple_of(g * span + j * page, page)
            pltpu.make_async_copy(pool.at[prompt_table[g, j], :, columns], held.at[pl.ds(at, page)], sems.at[0]).start()

    @pl.loop(0, reqs)
    def _(r):
        for j in range(cont_pages):
            at = pl.multiple_of(start + r * own + j * page, page)
            pltpu.make_async_copy(pool.at[cont_table[j, r], :, columns], held.at[pl.ds(at, page)], sems.at[0]).start()

    rows = pl.ds(low * value_width, weight_held.shape[0])
    weight_copy = pltpu.make_async_copy(weight.at[rows], weight_held, sems.at[1])
    weight_copy.start()

    group_of = column(req_group, reqs)
    length_of = column(cont_len, reqs)
    biases = []
    pos = lax.broadcasted_iota(jnp.int32, (reqs, span), 1)
    for g in range(groups):
        live = (group_of == g) & (pos < prompt_len[g])
        biases.append(jnp.where(live, 0.0, -1e30))
    key = lax.broadcasted_iota(jnp.int32, (reqs, reqs * own), 1)
    pos = key - own * lax.broadcasted_iota(jnp.int32, (reqs, reqs * own), 0)
    biases.append(jnp.where((pos >= 0) & (pos < length_of), 0.0, -1e30))
    live = jnp.concatenate(biases, axis=1) == 0.0

    pltpu.make_async_copy(held, held, sems.at[0]).wait()

    scale = KEY**-0.5
    mixed = []
    for h in range(heads):
        first = h * head_width
        weights, new_weights = [], []
        for i in range(2):
            q = query[:, pl.ds((2 * (low + h) + i) * KEY, KEY)]
            cols = pl.ds(first + i * KEY, KEY)
            new_cols = pl.ds(low * head_width + first + i * KEY, KEY)
            score = lax.dot_general(
                q, held[:, cols], (((1,), (1,)), ((), ())), preferred_element_type=jnp.float32
            )
            score = jnp.where(live, score * scale, -1e30)
            new = jnp.sum(q.astype(jnp.float32) * new_ref[:, new_cols].astype(jnp.float32), axis=1, keepdims=True) * scale
            top = jnp.maximum(jnp.max(score, axis=1, keepdims=True), new)
            score = jnp.exp(score - top)
            new = jnp.exp(new - top)
            inverse = 1.0 / (jnp.sum(score, axis=1, keepdims=True) + new)
            weights.append((score * inverse).astype(jnp.bfloat16))
            new_weights.append((new * inverse).astype(jnp.bfloat16).astype(jnp.float32))
        cols = pl.ds(first + 2 * KEY, value_width)
        mixture = jnp.dot(jnp.concatenate(weights, axis=0), held[:, cols], preferred_element_type=jnp.float32)
        new_value = new_ref[:, pl.ds(low * head_width + first + 2 * KEY, value_width)].astype(jnp.float32)
        one = mixture[:reqs] + new_weights[0] * new_value
        two = mixture[reqs:] + new_weights[1] * new_value
        diff = one - lam[low + h] * two
        norm = lax.rsqrt(jnp.mean(diff * diff, axis=1, keepdims=True) + 1e-05)
        mixed.append((diff * norm * 0.8).astype(jnp.bfloat16))
    weight_copy.wait()
    mixed = jnp.concatenate(mixed, axis=1)
    product = jnp.dot(mixed, weight_held[...], preferred_element_type=jnp.float32)
    for part in prior:
        product = product + part[...]
    out[...] = product.astype(out.dtype)


def attention(query, new_kv, pool, prompt_table, prompt_len, req_group, cont_table, cont_len, lam, weight, low, high, prior):
    reqs = query.shape[0]
    page = pool.shape[1]
    heads = lam.shape[0]
    keys = (prompt_table.size + cont_table.size) * page
    width = pool.shape[2] // heads * (high - low)
    rows = weight.shape[0] // heads * (high - low)
    return pl.pallas_call(
        functools.partial(attention_kernel, low),
        out_shape=jax.ShapeDtypeStruct((reqs, weight.shape[1]), jnp.bfloat16 if high == heads else jnp.float32),
        in_specs=[SMEM] * 6 + [VMEM] * (2 + len(prior)) + [HBM, HBM],
        out_specs=VMEM,
        scratch_shapes=[
            pltpu.VMEM((keys, width), pool.dtype),
            pltpu.VMEM((rows, weight.shape[1]), weight.dtype),
            pltpu.SemaphoreType.DMA((2,)),
        ],
        compiler_params=pltpu.CompilerParams(vmem_limit_bytes=VMEM_BYTES),
        cost_estimate=pl.CostEstimate(
            flops=4 * reqs * keys * width + 2 * reqs * rows * weight.shape[1],
            bytes_accessed=2 * (keys * width + rows * weight.shape[1]),
            transcendentals=reqs * keys * 2 * (high - low),
        ),
        name="attention",
    )(prompt_table, prompt_len, req_group, cont_table, cont_len, lam, query, new_kv, *prior, *pinned(weight, pool))


def finish_kernel(count, hidden, gain, *refs):
    parts = refs[:count]
    hidden_out, normed_out = refs[count:]
    total = parts[0][...].astype(jnp.float32)
    for part in parts[1:]:
        total = total + part[...].astype(jnp.float32)
    summed = hidden[...].astype(jnp.float32) + total
    norm = lax.rsqrt(jnp.mean(summed * summed, axis=1, keepdims=True) + 1e-05)
    hidden_out[...] = summed.astype(hidden_out.dtype)
    normed_out[...] = (summed * norm * gain[...]).astype(normed_out.dtype)


def finish(hidden, gain, parts):
    shape = jax.ShapeDtypeStruct(hidden.shape, jnp.bfloat16)
    return pl.pallas_call(
        functools.partial(finish_kernel, len(parts)),
        out_shape=[shape, shape],
        in_specs=[VMEM] * (2 + len(parts)),
        out_specs=[VMEM, VMEM],
        compiler_params=pltpu.CompilerParams(vmem_limit_bytes=SMALL_VMEM_BYTES),
        name="finish",
    )(hidden, gain.reshape(1, -1), *parts)


def gather_kernel(choose, count, *refs):
    parts, out, sems = refs[:count], refs[-2], refs[-1]
    copies = []
    for place, part, taken in choose():
        slots, span = parts[part].shape[:2]
        for at in range(slots):
            for half in range(2):
                rows = pl.ds(half * span // 2, span // 2)
                source, target = parts[part].at[at, rows], out.at[place + at, rows]
                copies.append((pltpu.make_async_copy(source, target, sems.at[len(copies)]), taken))
    for copy, taken in copies:
        pl.when(taken)(copy.start)
    for copy, taken in copies:
        pl.when(taken)(copy.wait)


def arrive(parts, choose, rest=None):
    slots = MIG_REACH * MIG_CAP
    extra = [] if rest is None else pinned(rest)
    return pl.pallas_call(
        functools.partial(gather_kernel, choose, len(parts)),
        out_shape=jax.ShapeDtypeStruct((slots,) + parts[0].shape[1:], parts[0].dtype),
        in_specs=[VMEM] * len(parts) + [HBM] * len(extra),
        out_specs=HBM,
        scratch_shapes=[pltpu.SemaphoreType.DMA((4 * MIG_REACH * MIG_CAP,))],
        input_output_aliases={len(parts): 0} if extra else {},
        compiler_params=pltpu.CompilerParams(vmem_limit_bytes=SMALL_VMEM_BYTES),
        name="arrive",
    )(*parts, *extra)


def routed(value, targets):
    count, width = lax.axis_size("req"), lax.axis_size("tp")
    pairs = []
    for s in range(count):
        for t in range(width):
            target = targets(s, t % 2)
            if target is not None:
                target = target % count
                pairs.append((s * width + t, target * width + (t ^ 1 if target == s else t)))
    return lax.ppermute(value, ("req", "tp"), pairs)


def turn(s, steps):
    return s - s % MIG_REACH + (s + steps) % MIG_REACH


def route_early(s, odd):
    if s % 2 == 0:
        return s + 1
    return turn(s, 3) if odd else s + 3


def route_late(s, odd):
    return s + 3 if s % 2 == 0 else s + 1


def lift_two(s, odd):
    return s + MIG_REACH if s % MIG_REACH < 2 else s


def lift_early(s, odd):
    return s + MIG_REACH if odd and s % 2 == 0 else None


def choose_straight():
    return [(n * MIG_CAP, n, True) for n in range(MIG_REACH)]


def where_am_i():
    col = lax.rem(lax.axis_index("req"), MIG_REACH)
    odd = lax.rem(col, 2) == 1
    odd_core = lax.rem(lax.axis_index("tp"), 2) == 1
    return col, odd, jnp.logical_not(odd), odd_core


def choose_sooner():
    col, odd, even, odd_core = where_am_i()
    return [(0, 2, odd), (2, 0, col >= 2), (2, 1, col < 2), (4, 2, even & jnp.logical_not(odd_core)), (6, 3, True)]


def choose_later():
    col, odd, even, odd_core = where_am_i()
    return [(0, 1, even), (4, 1, odd), (4, 0, even & odd_core)]


def can_relay():
    count = lax.axis_size("req")
    return MIG_REACH == 4 and count % MIG_REACH == 0 and count > MIG_REACH and lax.axis_size("tp") % 2 == 0


def shards(
    hidden_in,
    query,
    new_kv,
    pool_cache,
    prompt_table,
    prompt_len,
    req_group,
    cont_table,
    cont_len,
    migration,
    diff_lambda,
    out_weight,
    norm_gain,
):
    cont_table, migration = cont_table.T, migration.T
    heads = diff_lambda.shape[0]
    half = heads // 2
    attend = functools.partial(
        attention, query, new_kv, pool_cache, prompt_table, prompt_len, req_group, cont_table, cont_len, diff_lambda, out_weight
    )
    send = (cont_table, cont_len, migration, new_kv, pool_cache)
    prior = [attend(0, half, [])] if half else []
    if can_relay():
        two, four, early = send_slots(((2, 2), (4, 4), (1, 3)), *send)
        two = routed(two, lambda s, odd: turn(s, 2))
        four = shifted(four, "req", 4)
        early = routed(early, route_early)
        prior, later_len = lax.optimization_barrier((prior, cont_len))
        (late,) = send_slots(((3, 1),), cont_table, later_len, *send[2:])
        prior, two, late = lax.optimization_barrier((prior, two, late))
        two_up = routed(two, lift_two)
        late = routed(late, route_late)
        early_up = routed(early, lift_early)
    else:
        outgoing = send_slots(tuple((o, o) for o in range(1, MIG_REACH + 1)), *send)
        arrived = arrive([shifted(part, "req", o + 1) for o, part in enumerate(outgoing)], choose_straight)
    partial = attend(half, heads, prior)
    if lax.axis_size("tp") == 2:
        parts = [partial, shifted(partial, "tp", 1)]
    else:
        parts = [lax.psum(partial, "tp")]
    hidden_out, normed_out = finish(hidden_in, norm_gain, parts)
    if can_relay():
        sooner = arrive((two, two_up, early, four), choose_sooner)
        arrived = arrive((early_up, late), choose_later, sooner)
    return (hidden_out, normed_out, arrived)


def solution(mesh):
    placed = (
        P("req", None),
        P("req", "tp"),
        P("req", "tp"),
        P("req", None, "tp"),
        P("req", None),
        P("req"),
        P("req"),
        P("req", None),
        P("req"),
        P("req", None),
        P("tp"),
        P("tp", None),
        P(),
    )
    return jax.shard_map(
        shards,
        mesh=mesh,
        in_specs=placed,
        out_specs=(P("req", None), P("req", None), P("req", None, "tp")),
        check_vma=False,
    )
```

```python
import functools

import jax
import jax.numpy as jnp
from jax import lax
from jax.experimental import pallas as pl
from jax.experimental.pallas import tpu as pltpu
from jax.sharding import PartitionSpec as P

MIG_REACH = 4
MIG_CAP = 2
KEY = 128
ROWS = 16

SMEM = pl.BlockSpec(memory_space=pltpu.SMEM)
VMEM = pl.BlockSpec(memory_space=pltpu.VMEM)
HBM = pl.BlockSpec(memory_space=pltpu.HBM)
VMEM_BYTES = 40 * 1024 * 1024
SMALL_VMEM_BYTES = 8 * 1024 * 1024


def pinned(*arrays):
    return [pltpu.with_memory_space_constraint(array, pltpu.HBM) for array in arrays]


def shifted(value, axis, steps):
    count = lax.axis_size(axis)
    pairs = [(source, (source + steps) % count) for source in range(count)]
    return lax.ppermute(value, axis, pairs)


def send_kernel(offsets, table_in, length_in, migration_in, new_in, pool, *refs):
    outs = refs[: len(offsets)]
    table, length, migration, holder, new_held, new_rows, sems, small_sems = refs[len(offsets) :]
    small = [
        pltpu.make_async_copy(source, target, small_sems.at[n])
        for n, (source, target) in enumerate(
            zip((table_in, length_in, migration_in, new_in), (table, length, migration, new_held))
        )
    ]
    for copy in small:
        copy.start()
    for copy in small[:3]:
        copy.wait()
    entries = migration.shape[1]
    pages, page = table.shape[0], pool.shape[1]
    for place in range(MIG_REACH * MIG_CAP):
        holder[place] = -1
    odd = lax.rem(lax.axis_index("req"), 2)
    where = []
    for n, (on_even, on_odd) in enumerate(offsets):
        offset = on_even + odd * (on_odd - on_even)
        for i in range(MIG_CAP):
            where.append((n * MIG_CAP + i, (offset - 1) * MIG_CAP + i, outs[n].at[i]))
    for e in range(entries):
        rank = jnp.int32(0)
        for before in range(e):
            rank += (migration[1, before] == migration[1, e]).astype(jnp.int32)
        holder[(migration[1, e] - 1) * MIG_CAP + rank] = migration[0, e]

    slots = [holder[place] for _, place, _ in where]
    lasts = [jnp.where(slot >= 0, length[jnp.maximum(slot, 0)], -1) for slot in slots]
    slots = [jnp.maximum(slot, 0) for slot in slots]
    blocks = [lax.div(last + ROWS, ROWS) for last in lasts]
    items = [(n, out, *rest) for (n, _, out), *rest in zip(where, slots, lasts, blocks)]

    def rows_of(block):
        return pl.ds(pl.multiple_of(block * ROWS, ROWS), ROWS)

    def block_copy(n, out, slot, block):
        per_page = page // ROWS
        source = pool.at[table[lax.div(block, per_page), slot], rows_of(lax.rem(block, per_page))]
        return pltpu.make_async_copy(source, out.at[rows_of(block)], sems.at[n, block])

    for n, out, slot, last, used in items:

        @pl.loop(0, used)
        def _(block):
            block_copy(n, out, slot, block).start()

    for n, out, slot, last, used in items:

        @pl.loop(used, pages * page // ROWS)
        def _(block):
            out[rows_of(block)] = jnp.zeros((ROWS, out.shape[1]), out.dtype)

    small[3].wait()
    new_rows[...] = new_held[...].astype(jnp.float32)
    for n, out, slot, last, used in items:

        @pl.loop(0, used)
        def _(block):
            block_copy(n, out, slot, block).wait()

        @pl.when(used > 0)
        def _():
            rows = rows_of(used - 1)
            held = out[rows].astype(jnp.float32)
            pos = (used - 1) * ROWS + lax.broadcasted_iota(jnp.int32, held.shape, 0)
            new = jnp.where(pos == last, new_rows[pl.ds(slot, 1)], 0.0)
            out[rows] = jnp.where(pos < last, held, new).astype(out.dtype)


def send_slots(offsets, cont_table, cont_len, migration, new_kv, pool):
    span = cont_table.shape[0] * pool.shape[1]
    width = pool.shape[2]
    return pl.pallas_call(
        functools.partial(send_kernel, offsets),
        out_shape=[jax.ShapeDtypeStruct((MIG_CAP, span, width), pool.dtype)] * len(offsets),
        in_specs=[HBM] * 5,
        out_specs=[VMEM] * len(offsets),
        scratch_shapes=[
            pltpu.SMEM(cont_table.shape, jnp.int32),
            pltpu.SMEM(cont_len.shape, jnp.int32),
            pltpu.SMEM(migration.shape, jnp.int32),
            pltpu.SMEM((MIG_REACH * MIG_CAP,), jnp.int32),
            pltpu.VMEM(new_kv.shape, new_kv.dtype),
            pltpu.VMEM(new_kv.shape, jnp.float32),
            pltpu.SemaphoreType.DMA((len(offsets) * MIG_CAP, span // ROWS)),
            pltpu.SemaphoreType.DMA((4,)),
        ],
        compiler_params=pltpu.CompilerParams(vmem_limit_bytes=VMEM_BYTES),
        name="send_slots",
    )(*pinned(cont_table, cont_len, migration, new_kv, pool))


def column(values, count):
    rows = lax.broadcasted_iota(jnp.int32, (count, 1), 0)
    out = jnp.zeros((count, 1), jnp.int32)
    for r in range(count):
        out = jnp.where(rows == r, values[r], out)
    return out


def attention_kernel(low, prompt_table, prompt_len, req_group, cont_table, cont_len, lam, query, new_ref, *refs):
    prior = refs[:-6]
    weight, pool, out, held, weight_held, sems = refs[-6:]
    groups, prompt_pages = prompt_table.shape
    cont_pages, reqs = cont_table.shape
    page = pool.shape[1]
    span = prompt_pages * page
    own = cont_pages * page
    start = groups * span
    head_width = pool.shape[2] // lam.shape[0]
    value_width = head_width - 2 * KEY
    width = held.shape[1]
    heads = width // head_width
    columns = pl.ds(low * head_width, width)

    for g in range(groups):

        @pl.loop(0, prompt_pages)
        def _(j):
            at = pl.multiple_of(g * span + j * page, page)
            pltpu.make_async_copy(pool.at[prompt_table[g, j], :, columns], held.at[pl.ds(at, page)], sems.at[0]).start()

    @pl.loop(0, reqs)
    def _(r):
        for j in range(cont_pages):
            at = pl.multiple_of(start + r * own + j * page, page)
            pltpu.make_async_copy(pool.at[cont_table[j, r], :, columns], held.at[pl.ds(at, page)], sems.at[0]).start()

    rows = pl.ds(low * value_width, weight_held.shape[0])
    weight_copy = pltpu.make_async_copy(weight.at[rows], weight_held, sems.at[1])
    weight_copy.start()

    group_of = column(req_group, reqs)
    length_of = column(cont_len, reqs)
    biases = []
    pos = lax.broadcasted_iota(jnp.int32, (reqs, span), 1)
    for g in range(groups):
        live = (group_of == g) & (pos < prompt_len[g])
        biases.append(jnp.where(live, 0.0, -1e30))
    key = lax.broadcasted_iota(jnp.int32, (reqs, reqs * own), 1)
    pos = key - own * lax.broadcasted_iota(jnp.int32, (reqs, reqs * own), 0)
    biases.append(jnp.where((pos >= 0) & (pos < length_of), 0.0, -1e30))
    live = jnp.concatenate(biases, axis=1) == 0.0

    pltpu.make_async_copy(held, held, sems.at[0]).wait()

    scale = KEY**-0.5
    mixed = []
    for h in range(heads):
        first = h * head_width
        weights, new_weights = [], []
        for i in range(2):
            q = query[:, pl.ds((2 * (low + h) + i) * KEY, KEY)]
            cols = pl.ds(first + i * KEY, KEY)
            new_cols = pl.ds(low * head_width + first + i * KEY, KEY)
            score = lax.dot_general(
                q, held[:, cols], (((1,), (1,)), ((), ())), preferred_element_type=jnp.float32
            )
            score = jnp.where(live, score * scale, -1e30)
            new = jnp.sum(q.astype(jnp.float32) * new_ref[:, new_cols].astype(jnp.float32), axis=1, keepdims=True) * scale
            top = jnp.maximum(jnp.max(score, axis=1, keepdims=True), new)
            score = jnp.exp(score - top)
            new = jnp.exp(new - top)
            inverse = 1.0 / (jnp.sum(score, axis=1, keepdims=True) + new)
            weights.append((score * inverse).astype(jnp.bfloat16))
            new_weights.append((new * inverse).astype(jnp.bfloat16).astype(jnp.float32))
        cols = pl.ds(first + 2 * KEY, value_width)
        mixture = jnp.dot(jnp.concatenate(weights, axis=0), held[:, cols], preferred_element_type=jnp.float32)
        new_value = new_ref[:, pl.ds(low * head_width + first + 2 * KEY, value_width)].astype(jnp.float32)
        one = mixture[:reqs] + new_weights[0] * new_value
        two = mixture[reqs:] + new_weights[1] * new_value
        diff = one - lam[low + h] * two
        norm = lax.rsqrt(jnp.mean(diff * diff, axis=1, keepdims=True) + 1e-05)
        mixed.append((diff * norm * 0.8).astype(jnp.bfloat16))
    weight_copy.wait()
    mixed = jnp.concatenate(mixed, axis=1)
    product = jnp.dot(mixed, weight_held[...], preferred_element_type=jnp.float32)
    for part in prior:
        product = product + part[...]
    out[...] = product.astype(out.dtype)


def attention(query, new_kv, pool, prompt_table, prompt_len, req_group, cont_table, cont_len, lam, weight, low, high, prior):
    reqs = query.shape[0]
    page = pool.shape[1]
    heads = lam.shape[0]
    keys = (prompt_table.size + cont_table.size) * page
    width = pool.shape[2] // heads * (high - low)
    rows = weight.shape[0] // heads * (high - low)
    return pl.pallas_call(
        functools.partial(attention_kernel, low),
        out_shape=jax.ShapeDtypeStruct((reqs, weight.shape[1]), jnp.bfloat16 if high == heads else jnp.float32),
        in_specs=[SMEM] * 6 + [VMEM] * (2 + len(prior)) + [HBM, HBM],
        out_specs=VMEM,
        scratch_shapes=[
            pltpu.VMEM((keys, width), pool.dtype),
            pltpu.VMEM((rows, weight.shape[1]), weight.dtype),
            pltpu.SemaphoreType.DMA((2,)),
        ],
        compiler_params=pltpu.CompilerParams(vmem_limit_bytes=VMEM_BYTES),
        cost_estimate=pl.CostEstimate(
            flops=4 * reqs * keys * width + 2 * reqs * rows * weight.shape[1],
            bytes_accessed=2 * (keys * width + rows * weight.shape[1]),
            transcendentals=reqs * keys * 2 * (high - low),
        ),
        name="attention",
    )(prompt_table, prompt_len, req_group, cont_table, cont_len, lam, query, new_kv, *prior, *pinned(weight, pool))


def finish_kernel(count, hidden, gain, *refs):
    parts = refs[:count]
    hidden_out, normed_out = refs[count:]
    total = parts[0][...].astype(jnp.float32)
    for part in parts[1:]:
        total = total + part[...].astype(jnp.float32)
    summed = hidden[...].astype(jnp.float32) + total
    norm = lax.rsqrt(jnp.mean(summed * summed, axis=1, keepdims=True) + 1e-05)
    hidden_out[...] = summed.astype(hidden_out.dtype)
    normed_out[...] = (summed * norm * gain[...]).astype(normed_out.dtype)


def finish(hidden, gain, parts):
    shape = jax.ShapeDtypeStruct(hidden.shape, jnp.bfloat16)
    return pl.pallas_call(
        functools.partial(finish_kernel, len(parts)),
        out_shape=[shape, shape],
        in_specs=[VMEM] * (2 + len(parts)),
        out_specs=[VMEM, VMEM],
        compiler_params=pltpu.CompilerParams(vmem_limit_bytes=SMALL_VMEM_BYTES),
        name="finish",
    )(hidden, gain.reshape(1, -1), *parts)


def gather_kernel(choose, count, *refs):
    parts, out, sems = refs[:count], refs[-2], refs[-1]
    copies = [
        (pltpu.make_async_copy(parts[part], out.at[pl.ds(place, MIG_CAP)], sems.at[n]), taken)
        for n, (place, part, taken) in enumerate(choose())
    ]
    for copy, taken in copies:
        pl.when(taken)(copy.start)
    for copy, taken in copies:
        pl.when(taken)(copy.wait)


def arrive(parts, choose, rest=None):
    slots = MIG_REACH * MIG_CAP
    extra = [] if rest is None else pinned(rest)
    return pl.pallas_call(
        functools.partial(gather_kernel, choose, len(parts)),
        out_shape=jax.ShapeDtypeStruct((slots,) + parts[0].shape[1:], parts[0].dtype),
        in_specs=[VMEM] * len(parts) + [HBM] * len(extra),
        out_specs=HBM,
        scratch_shapes=[pltpu.SemaphoreType.DMA((2 * MIG_REACH,))],
        input_output_aliases={len(parts): 0} if extra else {},
        compiler_params=pltpu.CompilerParams(vmem_limit_bytes=SMALL_VMEM_BYTES),
        name="arrive",
    )(*parts, *extra)


def routed(value, targets):
    count, width = lax.axis_size("req"), lax.axis_size("tp")
    pairs = []
    for s in range(count):
        for t in range(width):
            target = targets(s, t % 2)
            if target is not None:
                target = target % count
                pairs.append((s * width + t, target * width + (t ^ 1 if target == s else t)))
    return lax.ppermute(value, ("req", "tp"), pairs)


def turn(s, steps):
    return s - s % MIG_REACH + (s + steps) % MIG_REACH


def route_early(s, odd):
    if s % 2 == 0:
        return s + 1
    return turn(s, 3) if odd else s + 3


def route_late(s, odd):
    return s + 3 if s % 2 == 0 else s + 1


def lift_two(s, odd):
    return s + MIG_REACH if s % MIG_REACH < 2 else s


def lift_early(s, odd):
    return s + MIG_REACH if odd and s % 2 == 0 else None


def choose_straight():
    return [(n * MIG_CAP, n, True) for n in range(MIG_REACH)]


def where_am_i():
    col = lax.rem(lax.axis_index("req"), MIG_REACH)
    odd = lax.rem(col, 2) == 1
    odd_core = lax.rem(lax.axis_index("tp"), 2) == 1
    return col, odd, jnp.logical_not(odd), odd_core


def choose_sooner():
    col, odd, even, odd_core = where_am_i()
    return [(0, 2, odd), (2, 0, col >= 2), (2, 1, col < 2), (4, 2, even & jnp.logical_not(odd_core)), (6, 3, True)]


def choose_later():
    col, odd, even, odd_core = where_am_i()
    return [(0, 1, even), (4, 1, odd), (4, 0, even & odd_core)]


def can_relay():
    count = lax.axis_size("req")
    return MIG_REACH == 4 and count % MIG_REACH == 0 and count > MIG_REACH and lax.axis_size("tp") % 2 == 0


def shards(
    hidden_in,
    query,
    new_kv,
    pool_cache,
    prompt_table,
    prompt_len,
    req_group,
    cont_table,
    cont_len,
    migration,
    diff_lambda,
    out_weight,
    norm_gain,
):
    cont_table, migration = cont_table.T, migration.T
    heads = diff_lambda.shape[0]
    half = heads // 2
    attend = functools.partial(
        attention, query, new_kv, pool_cache, prompt_table, prompt_len, req_group, cont_table, cont_len, diff_lambda, out_weight
    )
    send = (cont_table, cont_len, migration, new_kv, pool_cache)
    prior = [attend(0, half, [])] if half else []
    if can_relay():
        two, four, early = send_slots(((2, 2), (4, 4), (1, 3)), *send)
        two = routed(two, lambda s, odd: turn(s, 2))
        four = shifted(four, "req", 4)
        early = routed(early, route_early)
        prior, later_len = lax.optimization_barrier((prior, cont_len))
        (late,) = send_slots(((3, 1),), cont_table, later_len, *send[2:])
        prior, two, late = lax.optimization_barrier((prior, two, late))
        two_up = routed(two, lift_two)
        late = routed(late, route_late)
        early_up = routed(early, lift_early)
    else:
        outgoing = send_slots(tuple((o, o) for o in range(1, MIG_REACH + 1)), *send)
        arrived = arrive([shifted(part, "req", o + 1) for o, part in enumerate(outgoing)], choose_straight)
    partial = attend(half, heads, prior)
    if lax.axis_size("tp") == 2:
        parts = [partial, shifted(partial, "tp", 1)]
    else:
        parts = [lax.psum(partial, "tp")]
    hidden_out, normed_out = finish(hidden_in, norm_gain, parts)
    if can_relay():
        sooner = arrive((two, two_up, early, four), choose_sooner)
        arrived = arrive((early_up, late), choose_later, sooner)
    return (hidden_out, normed_out, arrived)


def solution(mesh):
    placed = (
        P("req", None),
        P("req", "tp"),
        P("req", "tp"),
        P("req", None, "tp"),
        P("req", None),
        P("req"),
        P("req"),
        P("req", None),
        P("req"),
        P("req", None),
        P("tp"),
        P("tp", None),
        P(),
    )
    return jax.shard_map(
        shards,
        mesh=mesh,
        in_specs=placed,
        out_specs=(P("req", None), P("req", None), P("req", None, "tp")),
        check_vma=False,
    )
```

```python
import functools

import jax
import jax.numpy as jnp
from jax import lax
from jax.experimental import pallas as pl
from jax.experimental.pallas import tpu as pltpu
from jax.sharding import PartitionSpec as P

MIG_REACH = 4
MIG_CAP = 2
KEY = 128
ROWS = 16

SMEM = pl.BlockSpec(memory_space=pltpu.SMEM)
VMEM = pl.BlockSpec(memory_space=pltpu.VMEM)
HBM = pl.BlockSpec(memory_space=pltpu.HBM)
VMEM_BYTES = 40 * 1024 * 1024
SMALL_VMEM_BYTES = 8 * 1024 * 1024


def pinned(*arrays):
    return [pltpu.with_memory_space_constraint(array, pltpu.HBM) for array in arrays]


def shifted(value, axis, steps):
    count = lax.axis_size(axis)
    pairs = [(source, (source + steps) % count) for source in range(count)]
    return lax.ppermute(value, axis, pairs)


def send_kernel(offsets, table_in, length_in, migration_in, new_in, pool, *refs):
    outs = refs[: len(offsets)]
    table, length, migration, holder, new_held, new_rows, sems, small_sems = refs[len(offsets) :]
    small = [
        pltpu.make_async_copy(source, target, small_sems.at[n])
        for n, (source, target) in enumerate(
            zip((table_in, length_in, migration_in, new_in), (table, length, migration, new_held))
        )
    ]
    for copy in small:
        copy.start()
    for copy in small[:3]:
        copy.wait()
    entries = migration.shape[1]
    pages, page = table.shape[0], pool.shape[1]
    for place in range(MIG_REACH * MIG_CAP):
        holder[place] = -1
    odd = lax.rem(lax.axis_index("req"), 2)
    where = []
    for n, (on_even, on_odd) in enumerate(offsets):
        offset = on_even + odd * (on_odd - on_even)
        for i in range(MIG_CAP):
            where.append((n * MIG_CAP + i, (offset - 1) * MIG_CAP + i, outs[n].at[i]))
    for e in range(entries):
        rank = jnp.int32(0)
        for before in range(e):
            rank += (migration[1, before] == migration[1, e]).astype(jnp.int32)
        holder[(migration[1, e] - 1) * MIG_CAP + rank] = migration[0, e]

    def last_of(place):
        slot = holder[place]
        return jnp.where(slot >= 0, length[jnp.maximum(slot, 0)], -1)

    def block_copy(n, place, out, low):
        source = pool.at[table[low // page, jnp.maximum(holder[place], 0)], pl.ds(low % page, ROWS)]
        return pltpu.make_async_copy(source, out.at[pl.ds(low, ROWS)], sems.at[n, low // ROWS])

    lows = range(0, pages * page, ROWS)
    for n, place, out in where:
        for low in lows:

            @pl.when(last_of(place) >= low)
            def _():
                block_copy(n, place, out, low).start()

    for n, place, out in where:
        for low in lows:

            @pl.when(last_of(place) < low)
            def _():
                out[pl.ds(low, ROWS)] = jnp.zeros((ROWS, out.shape[1]), out.dtype)

    small[3].wait()
    new_rows[...] = new_held[...].astype(jnp.float32)
    for n, place, out in where:
        last = last_of(place)
        safe = jnp.maximum(holder[place], 0)
        for low in lows:

            @pl.when(last >= low)
            def _():
                block_copy(n, place, out, low).wait()

            @pl.when((last >= low) & (last < low + ROWS))
            def _():
                held = out[pl.ds(low, ROWS)].astype(jnp.float32)
                pos = low + lax.broadcasted_iota(jnp.int32, held.shape, 0)
                new = jnp.where(pos == last, new_rows[pl.ds(safe, 1)], 0.0)
                out[pl.ds(low, ROWS)] = jnp.where(pos < last, held, new).astype(out.dtype)


def send_slots(offsets, cont_table, cont_len, migration, new_kv, pool):
    span = cont_table.shape[0] * pool.shape[1]
    width = pool.shape[2]
    return pl.pallas_call(
        functools.partial(send_kernel, offsets),
        out_shape=[jax.ShapeDtypeStruct((MIG_CAP, span, width), pool.dtype)] * len(offsets),
        in_specs=[HBM] * 5,
        out_specs=[VMEM] * len(offsets),
        scratch_shapes=[
            pltpu.SMEM(cont_table.shape, jnp.int32),
            pltpu.SMEM(cont_len.shape, jnp.int32),
            pltpu.SMEM(migration.shape, jnp.int32),
            pltpu.SMEM((MIG_REACH * MIG_CAP,), jnp.int32),
            pltpu.VMEM(new_kv.shape, new_kv.dtype),
            pltpu.VMEM(new_kv.shape, jnp.float32),
            pltpu.SemaphoreType.DMA((len(offsets) * MIG_CAP, span // ROWS)),
            pltpu.SemaphoreType.DMA((4,)),
        ],
        compiler_params=pltpu.CompilerParams(vmem_limit_bytes=VMEM_BYTES),
        name="send_slots",
    )(*pinned(cont_table, cont_len, migration, new_kv, pool))


def column(values, count):
    rows = lax.broadcasted_iota(jnp.int32, (count, 1), 0)
    out = jnp.zeros((count, 1), jnp.int32)
    for r in range(count):
        out = jnp.where(rows == r, values[r], out)
    return out


def attention_kernel(low, prompt_table, prompt_len, req_group, cont_table, cont_len, lam, query, new_ref, *refs):
    prior = refs[:-6]
    weight, pool, out, held, weight_held, sems = refs[-6:]
    groups, prompt_pages = prompt_table.shape
    cont_pages, reqs = cont_table.shape
    page = pool.shape[1]
    span = prompt_pages * page
    own = cont_pages * page
    start = groups * span
    head_width = pool.shape[2] // lam.shape[0]
    value_width = head_width - 2 * KEY
    width = held.shape[1]
    heads = width // head_width
    columns = pl.ds(low * head_width, width)

    for g in range(groups):

        @pl.loop(0, prompt_pages)
        def _(j):
            at = pl.multiple_of(g * span + j * page, page)
            pltpu.make_async_copy(pool.at[prompt_table[g, j], :, columns], held.at[pl.ds(at, page)], sems.at[0]).start()

    @pl.loop(0, reqs)
    def _(r):
        for j in range(cont_pages):
            at = pl.multiple_of(start + r * own + j * page, page)
            pltpu.make_async_copy(pool.at[cont_table[j, r], :, columns], held.at[pl.ds(at, page)], sems.at[0]).start()

    rows = pl.ds(low * value_width, weight_held.shape[0])
    weight_copy = pltpu.make_async_copy(weight.at[rows], weight_held, sems.at[1])
    weight_copy.start()

    group_of = column(req_group, reqs)
    length_of = column(cont_len, reqs)
    biases = []
    pos = lax.broadcasted_iota(jnp.int32, (reqs, span), 1)
    for g in range(groups):
        live = (group_of == g) & (pos < prompt_len[g])
        biases.append(jnp.where(live, 0.0, -1e30))
    key = lax.broadcasted_iota(jnp.int32, (reqs, reqs * own), 1)
    pos = key - own * lax.broadcasted_iota(jnp.int32, (reqs, reqs * own), 0)
    biases.append(jnp.where((pos >= 0) & (pos < length_of), 0.0, -1e30))
    live = jnp.concatenate(biases, axis=1) == 0.0

    pltpu.make_async_copy(held, held, sems.at[0]).wait()

    scale = KEY**-0.5
    mixed = []
    for h in range(heads):
        first = h * head_width
        weights, new_weights = [], []
        for i in range(2):
            q = query[:, pl.ds((2 * (low + h) + i) * KEY, KEY)]
            cols = pl.ds(first + i * KEY, KEY)
            new_cols = pl.ds(low * head_width + first + i * KEY, KEY)
            score = lax.dot_general(
                q, held[:, cols], (((1,), (1,)), ((), ())), preferred_element_type=jnp.float32
            )
            score = jnp.where(live, score * scale, -1e30)
            new = jnp.sum(q.astype(jnp.float32) * new_ref[:, new_cols].astype(jnp.float32), axis=1, keepdims=True) * scale
            top = jnp.maximum(jnp.max(score, axis=1, keepdims=True), new)
            score = jnp.exp(score - top)
            new = jnp.exp(new - top)
            inverse = 1.0 / (jnp.sum(score, axis=1, keepdims=True) + new)
            weights.append((score * inverse).astype(jnp.bfloat16))
            new_weights.append((new * inverse).astype(jnp.bfloat16).astype(jnp.float32))
        cols = pl.ds(first + 2 * KEY, value_width)
        mixture = jnp.dot(jnp.concatenate(weights, axis=0), held[:, cols], preferred_element_type=jnp.float32)
        new_value = new_ref[:, pl.ds(low * head_width + first + 2 * KEY, value_width)].astype(jnp.float32)
        one = mixture[:reqs] + new_weights[0] * new_value
        two = mixture[reqs:] + new_weights[1] * new_value
        diff = one - lam[low + h] * two
        norm = lax.rsqrt(jnp.mean(diff * diff, axis=1, keepdims=True) + 1e-05)
        mixed.append((diff * norm * 0.8).astype(jnp.bfloat16))
    weight_copy.wait()
    mixed = jnp.concatenate(mixed, axis=1)
    product = jnp.dot(mixed, weight_held[...], preferred_element_type=jnp.float32)
    for part in prior:
        product = product + part[...]
    out[...] = product.astype(out.dtype)


def attention(query, new_kv, pool, prompt_table, prompt_len, req_group, cont_table, cont_len, lam, weight, low, high, prior):
    reqs = query.shape[0]
    page = pool.shape[1]
    heads = lam.shape[0]
    keys = (prompt_table.size + cont_table.size) * page
    width = pool.shape[2] // heads * (high - low)
    rows = weight.shape[0] // heads * (high - low)
    return pl.pallas_call(
        functools.partial(attention_kernel, low),
        out_shape=jax.ShapeDtypeStruct((reqs, weight.shape[1]), jnp.bfloat16 if high == heads else jnp.float32),
        in_specs=[SMEM] * 6 + [VMEM] * (2 + len(prior)) + [HBM, HBM],
        out_specs=VMEM,
        scratch_shapes=[
            pltpu.VMEM((keys, width), pool.dtype),
            pltpu.VMEM((rows, weight.shape[1]), weight.dtype),
            pltpu.SemaphoreType.DMA((2,)),
        ],
        compiler_params=pltpu.CompilerParams(vmem_limit_bytes=VMEM_BYTES),
        cost_estimate=pl.CostEstimate(
            flops=4 * reqs * keys * width + 2 * reqs * rows * weight.shape[1],
            bytes_accessed=2 * (keys * width + rows * weight.shape[1]),
            transcendentals=reqs * keys * 2 * (high - low),
        ),
        name="attention",
    )(prompt_table, prompt_len, req_group, cont_table, cont_len, lam, query, new_kv, *prior, *pinned(weight, pool))


def finish_kernel(count, hidden, gain, *refs):
    parts = refs[:count]
    hidden_out, normed_out = refs[count:]
    total = parts[0][...].astype(jnp.float32)
    for part in parts[1:]:
        total = total + part[...].astype(jnp.float32)
    summed = hidden[...].astype(jnp.float32) + total
    norm = lax.rsqrt(jnp.mean(summed * summed, axis=1, keepdims=True) + 1e-05)
    hidden_out[...] = summed.astype(hidden_out.dtype)
    normed_out[...] = (summed * norm * gain[...]).astype(normed_out.dtype)


def finish(hidden, gain, parts):
    shape = jax.ShapeDtypeStruct(hidden.shape, jnp.bfloat16)
    return pl.pallas_call(
        functools.partial(finish_kernel, len(parts)),
        out_shape=[shape, shape],
        in_specs=[VMEM] * (2 + len(parts)),
        out_specs=[VMEM, VMEM],
        compiler_params=pltpu.CompilerParams(vmem_limit_bytes=SMALL_VMEM_BYTES),
        name="finish",
    )(hidden, gain.reshape(1, -1), *parts)


def gather_kernel(choose, count, *refs):
    parts, out, sems = refs[:count], refs[-2], refs[-1]
    copies = [
        (pltpu.make_async_copy(parts[part], out.at[pl.ds(place, MIG_CAP)], sems.at[n]), taken)
        for n, (place, part, taken) in enumerate(choose())
    ]
    for copy, taken in copies:
        pl.when(taken)(copy.start)
    for copy, taken in copies:
        pl.when(taken)(copy.wait)


def arrive(parts, choose, rest=None):
    slots = MIG_REACH * MIG_CAP
    extra = [] if rest is None else pinned(rest)
    return pl.pallas_call(
        functools.partial(gather_kernel, choose, len(parts)),
        out_shape=jax.ShapeDtypeStruct((slots,) + parts[0].shape[1:], parts[0].dtype),
        in_specs=[VMEM] * len(parts) + [HBM] * len(extra),
        out_specs=HBM,
        scratch_shapes=[pltpu.SemaphoreType.DMA((2 * MIG_REACH,))],
        input_output_aliases={len(parts): 0} if extra else {},
        compiler_params=pltpu.CompilerParams(vmem_limit_bytes=SMALL_VMEM_BYTES),
        name="arrive",
    )(*parts, *extra)


def routed(value, targets):
    count, width = lax.axis_size("req"), lax.axis_size("tp")
    pairs = []
    for s in range(count):
        for t in range(width):
            target = targets(s, t % 2)
            if target is not None:
                target = target % count
                pairs.append((s * width + t, target * width + (t ^ 1 if target == s else t)))
    return lax.ppermute(value, ("req", "tp"), pairs)


def turn(s, steps):
    return s - s % MIG_REACH + (s + steps) % MIG_REACH


def route_early(s, odd):
    if s % 2 == 0:
        return s + 1
    return turn(s, 3) if odd == (s % MIG_REACH == 1) else s + 3


def route_late(s, odd):
    return s + 3 if s % 2 == 0 else s + 1


def lift_two(s, odd):
    return s + MIG_REACH if s % MIG_REACH < 2 else s


def lift_early(s, odd):
    return s + MIG_REACH if s % 2 == 0 and odd == (s % MIG_REACH == 0) else None


def choose_straight():
    return [(n * MIG_CAP, n, True) for n in range(MIG_REACH)]


def where_am_i():
    col = lax.rem(lax.axis_index("req"), MIG_REACH)
    odd = lax.rem(col, 2) == 1
    odd_core = lax.rem(lax.axis_index("tp"), 2) == 1
    return col, odd, jnp.logical_not(odd), odd_core


def choose_sooner():
    col, odd, even, odd_core = where_am_i()
    return [(0, 2, odd), (2, 0, col >= 2), (2, 1, col < 2), (4, 2, even & (odd_core != (col == 0))), (6, 3, True)]


def choose_later():
    col, odd, even, odd_core = where_am_i()
    return [(0, 1, even), (4, 1, odd), (4, 0, even & (odd_core == (col == 0)))]


def can_relay():
    count = lax.axis_size("req")
    return MIG_REACH == 4 and count % MIG_REACH == 0 and count > MIG_REACH and lax.axis_size("tp") % 2 == 0


def shards(
    hidden_in,
    query,
    new_kv,
    pool_cache,
    prompt_table,
    prompt_len,
    req_group,
    cont_table,
    cont_len,
    migration,
    diff_lambda,
    out_weight,
    norm_gain,
):
    cont_table, migration = cont_table.T, migration.T
    heads = diff_lambda.shape[0]
    half = heads // 2
    attend = functools.partial(
        attention, query, new_kv, pool_cache, prompt_table, prompt_len, req_group, cont_table, cont_len, diff_lambda, out_weight
    )
    send = (cont_table, cont_len, migration, new_kv, pool_cache)
    prior = [attend(0, half, [])] if half else []
    if can_relay():
        two, four, early = send_slots(((2, 2), (4, 4), (1, 3)), *send)
        two = routed(two, lambda s, odd: turn(s, 2))
        four = shifted(four, "req", 4)
        early = routed(early, route_early)
        prior, later_len = lax.optimization_barrier((prior, cont_len))
        (late,) = send_slots(((3, 1),), cont_table, later_len, *send[2:])
        prior, two, late = lax.optimization_barrier((prior, two, late))
        two_up = routed(two, lift_two)
        late = routed(late, route_late)
        early_up = routed(early, lift_early)
    else:
        outgoing = send_slots(tuple((o, o) for o in range(1, MIG_REACH + 1)), *send)
        arrived = arrive([shifted(part, "req", o + 1) for o, part in enumerate(outgoing)], choose_straight)
    partial = attend(half, heads, prior)
    if lax.axis_size("tp") == 2:
        parts = [partial, shifted(partial, "tp", 1)]
    else:
        parts = [lax.psum(partial, "tp")]
    hidden_out, normed_out = finish(hidden_in, norm_gain, parts)
    if can_relay():
        sooner = arrive((two, two_up, early, four), choose_sooner)
        arrived = arrive((early_up, late), choose_later, sooner)
    return (hidden_out, normed_out, arrived)


def solution(mesh):
    placed = (
        P("req", None),
        P("req", "tp"),
        P("req", "tp"),
        P("req", None, "tp"),
        P("req", None),
        P("req"),
        P("req"),
        P("req", None),
        P("req"),
        P("req", None),
        P("tp"),
        P("tp", None),
        P(),
    )
    return jax.shard_map(
        shards,
        mesh=mesh,
        in_specs=placed,
        out_specs=(P("req", None), P("req", None), P("req", None, "tp")),
        check_vma=False,
    )
```

```python
import functools

import jax
import jax.numpy as jnp
from jax import lax
from jax.experimental import pallas as pl
from jax.experimental.pallas import tpu as pltpu
from jax.sharding import PartitionSpec as P

MIG_REACH = 4
MIG_CAP = 2
KEY = 128
ROWS = 16

SMEM = pl.BlockSpec(memory_space=pltpu.SMEM)
VMEM = pl.BlockSpec(memory_space=pltpu.VMEM)
HBM = pl.BlockSpec(memory_space=pltpu.HBM)
VMEM_BYTES = 40 * 1024 * 1024
SMALL_VMEM_BYTES = 8 * 1024 * 1024


def pinned(*arrays):
    return [pltpu.with_memory_space_constraint(array, pltpu.HBM) for array in arrays]


def shifted(value, axis, steps):
    count = lax.axis_size(axis)
    pairs = [(source, (source + steps) % count) for source in range(count)]
    return lax.ppermute(value, axis, pairs)


def send_kernel(offsets, table_in, length_in, migration_in, new_in, pool, *refs):
    outs = refs[: len(offsets)]
    table, length, migration, holder, new_held, new_rows, sems, small_sems = refs[len(offsets) :]
    small = [
        pltpu.make_async_copy(source, target, small_sems.at[n])
        for n, (source, target) in enumerate(
            zip((table_in, length_in, migration_in, new_in), (table, length, migration, new_held))
        )
    ]
    for copy in small:
        copy.start()
    for copy in small[:3]:
        copy.wait()
    entries = migration.shape[1]
    pages, page = table.shape[0], pool.shape[1]
    for place in range(MIG_REACH * MIG_CAP):
        holder[place] = -1
    odd = lax.rem(lax.axis_index("req"), 2)
    where = []
    for n, (on_even, on_odd) in enumerate(offsets):
        offset = on_even + odd * (on_odd - on_even)
        for i in range(MIG_CAP):
            where.append((n * MIG_CAP + i, (offset - 1) * MIG_CAP + i, outs[n].at[i]))
    for e in range(entries):
        rank = jnp.int32(0)
        for before in range(e):
            rank += (migration[1, before] == migration[1, e]).astype(jnp.int32)
        holder[(migration[1, e] - 1) * MIG_CAP + rank] = migration[0, e]

    def last_of(place):
        slot = holder[place]
        return jnp.where(slot >= 0, length[jnp.maximum(slot, 0)], -1)

    def block_copy(n, place, out, low):
        source = pool.at[table[low // page, jnp.maximum(holder[place], 0)], pl.ds(low % page, ROWS)]
        return pltpu.make_async_copy(source, out.at[pl.ds(low, ROWS)], sems.at[n, low // ROWS])

    lows = range(0, pages * page, ROWS)
    for n, place, out in where:
        for low in lows:

            @pl.when(last_of(place) >= low)
            def _():
                block_copy(n, place, out, low).start()

    for n, place, out in where:
        for low in lows:

            @pl.when(last_of(place) < low)
            def _():
                out[pl.ds(low, ROWS)] = jnp.zeros((ROWS, out.shape[1]), out.dtype)

    small[3].wait()
    new_rows[...] = new_held[...].astype(jnp.float32)
    for n, place, out in where:
        last = last_of(place)
        safe = jnp.maximum(holder[place], 0)
        for low in lows:

            @pl.when(last >= low)
            def _():
                block_copy(n, place, out, low).wait()

            @pl.when((last >= low) & (last < low + ROWS))
            def _():
                held = out[pl.ds(low, ROWS)].astype(jnp.float32)
                pos = low + lax.broadcasted_iota(jnp.int32, held.shape, 0)
                new = jnp.where(pos == last, new_rows[pl.ds(safe, 1)], 0.0)
                out[pl.ds(low, ROWS)] = jnp.where(pos < last, held, new).astype(out.dtype)


def send_slots(offsets, cont_table, cont_len, migration, new_kv, pool):
    span = cont_table.shape[0] * pool.shape[1]
    width = pool.shape[2]
    return pl.pallas_call(
        functools.partial(send_kernel, offsets),
        out_shape=[jax.ShapeDtypeStruct((MIG_CAP, span, width), pool.dtype)] * len(offsets),
        in_specs=[HBM] * 5,
        out_specs=[VMEM] * len(offsets),
        scratch_shapes=[
            pltpu.SMEM(cont_table.shape, jnp.int32),
            pltpu.SMEM(cont_len.shape, jnp.int32),
            pltpu.SMEM(migration.shape, jnp.int32),
            pltpu.SMEM((MIG_REACH * MIG_CAP,), jnp.int32),
            pltpu.VMEM(new_kv.shape, new_kv.dtype),
            pltpu.VMEM(new_kv.shape, jnp.float32),
            pltpu.SemaphoreType.DMA((len(offsets) * MIG_CAP, span // ROWS)),
            pltpu.SemaphoreType.DMA((4,)),
        ],
        compiler_params=pltpu.CompilerParams(vmem_limit_bytes=VMEM_BYTES),
        name="send_slots",
    )(*pinned(cont_table, cont_len, migration, new_kv, pool))


def column(values, count):
    rows = lax.broadcasted_iota(jnp.int32, (count, 1), 0)
    out = jnp.zeros((count, 1), jnp.int32)
    for r in range(count):
        out = jnp.where(rows == r, values[r], out)
    return out


def attention_kernel(low, prompt_table, prompt_len, req_group, cont_table, cont_len, lam, query, new_ref, *refs):
    prior = refs[:-6]
    weight, pool, out, held, weight_held, sems = refs[-6:]
    groups, prompt_pages = prompt_table.shape
    cont_pages, reqs = cont_table.shape
    page = pool.shape[1]
    span = prompt_pages * page
    own = cont_pages * page
    start = groups * span
    head_width = pool.shape[2] // lam.shape[0]
    value_width = head_width - 2 * KEY
    width = held.shape[1]
    heads = width // head_width
    columns = pl.ds(low * head_width, width)

    for g in range(groups):

        @pl.loop(0, prompt_pages)
        def _(j):
            at = pl.multiple_of(g * span + j * page, page)
            pltpu.make_async_copy(pool.at[prompt_table[g, j], :, columns], held.at[pl.ds(at, page)], sems.at[0]).start()

    @pl.loop(0, reqs)
    def _(r):
        for j in range(cont_pages):
            at = pl.multiple_of(start + r * own + j * page, page)
            pltpu.make_async_copy(pool.at[cont_table[j, r], :, columns], held.at[pl.ds(at, page)], sems.at[0]).start()

    rows = pl.ds(low * value_width, weight_held.shape[0])
    weight_copy = pltpu.make_async_copy(weight.at[rows], weight_held, sems.at[1])
    weight_copy.start()

    group_of = column(req_group, reqs)
    length_of = column(cont_len, reqs)
    biases = []
    pos = lax.broadcasted_iota(jnp.int32, (reqs, span), 1)
    for g in range(groups):
        live = (group_of == g) & (pos < prompt_len[g])
        biases.append(jnp.where(live, 0.0, -1e30))
    key = lax.broadcasted_iota(jnp.int32, (reqs, reqs * own), 1)
    pos = key - own * lax.broadcasted_iota(jnp.int32, (reqs, reqs * own), 0)
    biases.append(jnp.where((pos >= 0) & (pos < length_of), 0.0, -1e30))
    live = jnp.concatenate(biases, axis=1) == 0.0

    pltpu.make_async_copy(held, held, sems.at[0]).wait()

    scale = KEY**-0.5
    mixed = []
    for h in range(heads):
        first = h * head_width
        weights, new_weights = [], []
        for i in range(2):
            q = query[:, pl.ds((2 * (low + h) + i) * KEY, KEY)]
            cols = pl.ds(first + i * KEY, KEY)
            new_cols = pl.ds(low * head_width + first + i * KEY, KEY)
            score = lax.dot_general(
                q, held[:, cols], (((1,), (1,)), ((), ())), preferred_element_type=jnp.float32
            )
            score = jnp.where(live, score * scale, -1e30)
            new = jnp.sum(q.astype(jnp.float32) * new_ref[:, new_cols].astype(jnp.float32), axis=1, keepdims=True) * scale
            top = jnp.maximum(jnp.max(score, axis=1, keepdims=True), new)
            score = jnp.exp(score - top)
            new = jnp.exp(new - top)
            inverse = 1.0 / (jnp.sum(score, axis=1, keepdims=True) + new)
            weights.append((score * inverse).astype(jnp.bfloat16))
            new_weights.append((new * inverse).astype(jnp.bfloat16).astype(jnp.float32))
        cols = pl.ds(first + 2 * KEY, value_width)
        mixture = jnp.dot(jnp.concatenate(weights, axis=0), held[:, cols], preferred_element_type=jnp.float32)
        new_value = new_ref[:, pl.ds(low * head_width + first + 2 * KEY, value_width)].astype(jnp.float32)
        one = mixture[:reqs] + new_weights[0] * new_value
        two = mixture[reqs:] + new_weights[1] * new_value
        diff = one - lam[low + h] * two
        norm = lax.rsqrt(jnp.mean(diff * diff, axis=1, keepdims=True) + 1e-05)
        mixed.append((diff * norm * 0.8).astype(jnp.bfloat16))
    weight_copy.wait()
    mixed = jnp.concatenate(mixed, axis=1)
    product = jnp.dot(mixed, weight_held[...], preferred_element_type=jnp.float32)
    for part in prior:
        product = product + part[...]
    out[...] = product.astype(out.dtype)


def attention(query, new_kv, pool, prompt_table, prompt_len, req_group, cont_table, cont_len, lam, weight, low, high, prior):
    reqs = query.shape[0]
    page = pool.shape[1]
    heads = lam.shape[0]
    keys = (prompt_table.size + cont_table.size) * page
    width = pool.shape[2] // heads * (high - low)
    rows = weight.shape[0] // heads * (high - low)
    return pl.pallas_call(
        functools.partial(attention_kernel, low),
        out_shape=jax.ShapeDtypeStruct((reqs, weight.shape[1]), jnp.bfloat16 if high == heads else jnp.float32),
        in_specs=[SMEM] * 6 + [VMEM] * (2 + len(prior)) + [HBM, HBM],
        out_specs=VMEM,
        scratch_shapes=[
            pltpu.VMEM((keys, width), pool.dtype),
            pltpu.VMEM((rows, weight.shape[1]), weight.dtype),
            pltpu.SemaphoreType.DMA((2,)),
        ],
        compiler_params=pltpu.CompilerParams(vmem_limit_bytes=VMEM_BYTES),
        cost_estimate=pl.CostEstimate(
            flops=4 * reqs * keys * width + 2 * reqs * rows * weight.shape[1],
            bytes_accessed=2 * (keys * width + rows * weight.shape[1]),
            transcendentals=reqs * keys * 2 * (high - low),
        ),
        name="attention",
    )(prompt_table, prompt_len, req_group, cont_table, cont_len, lam, query, new_kv, *prior, *pinned(weight, pool))


def finish_kernel(count, hidden, gain, *refs):
    parts = refs[:count]
    hidden_out, normed_out = refs[count:]
    total = parts[0][...].astype(jnp.float32)
    for part in parts[1:]:
        total = total + part[...].astype(jnp.float32)
    summed = hidden[...].astype(jnp.float32) + total
    norm = lax.rsqrt(jnp.mean(summed * summed, axis=1, keepdims=True) + 1e-05)
    hidden_out[...] = summed.astype(hidden_out.dtype)
    normed_out[...] = (summed * norm * gain[...]).astype(normed_out.dtype)


def finish(hidden, gain, parts):
    shape = jax.ShapeDtypeStruct(hidden.shape, jnp.bfloat16)
    return pl.pallas_call(
        functools.partial(finish_kernel, len(parts)),
        out_shape=[shape, shape],
        in_specs=[VMEM] * (2 + len(parts)),
        out_specs=[VMEM, VMEM],
        compiler_params=pltpu.CompilerParams(vmem_limit_bytes=SMALL_VMEM_BYTES),
        name="finish",
    )(hidden, gain.reshape(1, -1), *parts)


def gather_kernel(choose, count, *refs):
    parts, out, sems = refs[:count], refs[-2], refs[-1]
    copies = [
        (pltpu.make_async_copy(parts[part], out.at[pl.ds(place, MIG_CAP)], sems.at[n]), taken)
        for n, (place, part, taken) in enumerate(choose())
    ]
    for copy, taken in copies:
        pl.when(taken)(copy.start)
    for copy, taken in copies:
        pl.when(taken)(copy.wait)


def arrive(parts, choose, rest=None):
    slots = MIG_REACH * MIG_CAP
    extra = [] if rest is None else pinned(rest)
    return pl.pallas_call(
        functools.partial(gather_kernel, choose, len(parts)),
        out_shape=jax.ShapeDtypeStruct((slots,) + parts[0].shape[1:], parts[0].dtype),
        in_specs=[VMEM] * len(parts) + [HBM] * len(extra),
        out_specs=HBM,
        scratch_shapes=[pltpu.SemaphoreType.DMA((2 * MIG_REACH,))],
        input_output_aliases={len(parts): 0} if extra else {},
        compiler_params=pltpu.CompilerParams(vmem_limit_bytes=SMALL_VMEM_BYTES),
        name="arrive",
    )(*parts, *extra)


def routed(value, targets):
    count, width = lax.axis_size("req"), lax.axis_size("tp")
    pairs = []
    for s in range(count):
        for t in range(width):
            target = targets(s, t % 2)
            if target is not None:
                target = target % count
                pairs.append((s * width + t, target * width + (t ^ 1 if target == s else t)))
    return lax.ppermute(value, ("req", "tp"), pairs)


def turn(s, steps):
    return s - s % MIG_REACH + (s + steps) % MIG_REACH


def route_early(s, odd):
    if s % 2 == 0:
        return s + 1
    return turn(s, 3) if odd == (s % MIG_REACH == 1) else s + 3


def route_late(s, odd):
    return s + 3 if s % 2 == 0 else s + 1


def lift_two(s, odd):
    return s + MIG_REACH if s % MIG_REACH < 2 else s


def lift_early(s, odd):
    return s + MIG_REACH if s % 2 == 0 and odd == (s % MIG_REACH == 0) else None


def choose_straight():
    return [(n * MIG_CAP, n, True) for n in range(MIG_REACH)]


def where_am_i():
    col = lax.rem(lax.axis_index("req"), MIG_REACH)
    odd = lax.rem(col, 2) == 1
    odd_core = lax.rem(lax.axis_index("tp"), 2) == 1
    return col, odd, jnp.logical_not(odd), odd_core


def choose_sooner():
    col, odd, even, odd_core = where_am_i()
    return [(0, 2, odd), (2, 0, col >= 2), (2, 1, col < 2), (4, 2, even & (odd_core != (col == 0))), (6, 3, True)]


def choose_late():
    col, odd, even, odd_core = where_am_i()
    return [(0, 0, even), (4, 0, odd)]


def choose_last():
    col, odd, even, odd_core = where_am_i()
    return [(4, 0, even & (odd_core == (col == 0)))]


def can_relay():
    count = lax.axis_size("req")
    return MIG_REACH == 4 and count % MIG_REACH == 0 and count > MIG_REACH and lax.axis_size("tp") % 2 == 0


def shards(
    hidden_in,
    query,
    new_kv,
    pool_cache,
    prompt_table,
    prompt_len,
    req_group,
    cont_table,
    cont_len,
    migration,
    diff_lambda,
    out_weight,
    norm_gain,
):
    cont_table, migration = cont_table.T, migration.T
    heads = diff_lambda.shape[0]
    half = heads // 2
    attend = functools.partial(
        attention, query, new_kv, pool_cache, prompt_table, prompt_len, req_group, cont_table, cont_len, diff_lambda, out_weight
    )
    send = (cont_table, cont_len, migration, new_kv, pool_cache)
    prior = [attend(0, half, [])] if half else []
    if can_relay():
        two, four, early = send_slots(((2, 2), (4, 4), (1, 3)), *send)
        two = routed(two, lambda s, odd: turn(s, 2))
        four = shifted(four, "req", 4)
        early = routed(early, route_early)
        prior, later_len = lax.optimization_barrier((prior, cont_len))
        (late,) = send_slots(((3, 1),), cont_table, later_len, *send[2:])
        prior, two, late = lax.optimization_barrier((prior, two, late))
        two_up = routed(two, lift_two)
        late = routed(late, route_late)
        early_up = routed(early, lift_early)
    else:
        outgoing = send_slots(tuple((o, o) for o in range(1, MIG_REACH + 1)), *send)
        arrived = arrive([shifted(part, "req", o + 1) for o, part in enumerate(outgoing)], choose_straight)
    partial = attend(half, heads, prior)
    if lax.axis_size("tp") == 2:
        parts = [partial, shifted(partial, "tp", 1)]
    else:
        parts = [lax.psum(partial, "tp")]
    hidden_out, normed_out = finish(hidden_in, norm_gain, parts)
    if can_relay():
        sooner = arrive((two, two_up, early, four), choose_sooner)
        later = arrive((late,), choose_late, sooner)
        arrived = arrive((early_up,), choose_last, later)
    return (hidden_out, normed_out, arrived)


def solution(mesh):
    placed = (
        P("req", None),
        P("req", "tp"),
        P("req", "tp"),
        P("req", None, "tp"),
        P("req", None),
        P("req"),
        P("req"),
        P("req", None),
        P("req"),
        P("req", None),
        P("tp"),
        P("tp", None),
        P(),
    )
    return jax.shard_map(
        shards,
        mesh=mesh,
        in_specs=placed,
        out_specs=(P("req", None), P("req", None), P("req", None, "tp")),
        check_vma=False,
    )
```
